256 devices in a mesh: rec: 8 (over y, core), tm: 32 (over z, x).
Axes of the slice: x: 4, y: 4, z: 8, core: 2. Of those that a mesh axis runs over, the one named last changes fastest.
Arguments:
- wave: float32 [128, 1048576], P('rec', 'tm'), parts along dimension 0, may hold values from -6 to 6
- target_mod: float32 [12288, 1024], P(('rec', 'tm')), parts along dimension 0, may hold values from 0 to 0.5
- lengths: int32 [128], P('rec'), parts along dimension 0, may hold values from 1024 to 4096, as said below
Outputs:
- grad_wave: float32 [128, 1048576], P('rec', 'tm'), parts along dimension 0
- loss: float32 [128], P('rec'), parts along dimension 0
The draws below stay inside these ranges and needn't reach their ends.
There are 8 independent parts, one for each index of `rec`. The reference program is written for one: setup_inputs(seed, part) draws one part's arguments, and reference() takes and returns one part's arrays. A program takes and returns all parts, laid end to end along the dimension named above; each array names one. Nothing has to cross between parts.
Inputs may be any that keep to these rules, and one draw needn't show every extreme that they name: lengths[r] counts frames from the start of recording r; in every part some recording has all 4096 frames valid.
All inputs are finite; a program needn't handle non-finite values.
Results may differ from the reference program's by a relative error of at most 0.00027.
Values sent between devices are 32-bit elements; how exact they have to be, the bound alone decides.
A program may use at most 128 MiB of HBM per device.

```python
import math
import jax
import jax.numpy as jnp
from jax import lax

RECORDS = 16
FFT = 512
BANDS = 96
FRAMES = 4096
K = 1024
ROWS = 1536
SAMPLES = 1048576


def draw_lengths(key, part):
    first_key, second_key = jax.random.split(jax.random.fold_in(key, 17))
    values = jax.random.randint(first_key, (RECORDS,), FRAMES // 4, FRAMES + 1)
    chosen = jax.random.randint(second_key, (), 0, RECORDS)
    return jnp.where(jnp.arange(RECORDS) == chosen, FRAMES, values).astype(jnp.int32)


def level_of(rng, shape, cuts, low, largest):
    gain, own = 1.0, jax.random.fold_in(rng, 6)
    for position, shards_of in cuts:
        steps = jnp.exp(jax.random.uniform(jax.random.fold_in(own, position), (shards_of,), jnp.float32, low / len(cuts), largest / len(cuts)))
        gain = gain * jnp.repeat(steps, shape[position] // shards_of).reshape([-1 if axis == position else 1 for axis in range(len(shape))])
    return gain


def bell_draw(stream_key, extent, deviation, most, pieces=(), kind=jnp.bfloat16):
    drawn = jax.random.normal(stream_key, extent, jnp.float32) * deviation
    if len(pieces) > 0:
        drawn = level_of(stream_key, extent, pieces, -0.22, 0.18) * drawn
    return jnp.clip(drawn, min=-most, max=most).astype(kind)


def setup_inputs(seed: int = 0, part: int = 0) -> dict:
    key_of = jax.random.split(jax.random.key(seed), 4)
    part_splits = jax.random.split(jax.random.fold_in(key_of[3], part), 4)
    return {
        "wave": bell_draw(part_splits[0], (RECORDS, SAMPLES), 1.0, 6.0, ((1, 32),), jnp.float32),
        "target_mod": jnp.clip(0.5 * jax.random.uniform(part_splits[1], (ROWS, K), jnp.float32) ** level_of(part_splits[1], (ROWS, K), ((0, 32),), -0.2, 0.2), 0.0, 0.5),
        "lengths": draw_lengths(jax.random.fold_in(jax.random.fold_in(key_of[3], part), 71), part),
    }


HIGH = lax.Precision.HIGHEST
rate_hz = 16000.0

def a_weight(freq):
    square = freq * freq
    upper = 12194.0 ** 2 * square * square
    lower = (square + 20.6 ** 2) * jnp.sqrt((square + 107.7 ** 2) * (square + 737.9 ** 2)) * (square + 12194.0 ** 2)
    return upper / lower

def bark_scale(freq):
    return 13.0 * jnp.arctan(0.00076 * freq) + 3.5 * jnp.arctan((freq / 7500.0) ** 2)

def band_table(bins, bands):
    freq = jnp.arange(bins, dtype=jnp.float32) * (rate_hz / (2.0 * bins))
    height = bark_scale(freq)
    top_bark = bark_scale(jnp.asarray(rate_hz / 2.0, jnp.float32))
    centres = (jnp.arange(bands, dtype=jnp.float32) + 0.5) * (top_bark / bands)
    spread = jnp.maximum(0.5, 2.0 * top_bark / bands)
    shape = jnp.maximum(0.0, 1.0 - jnp.abs(height[:, None] - centres[None, :]) / spread)
    weight = 0.1 + a_weight(freq) / a_weight(jnp.asarray(1000.0, jnp.float32))
    return shape * weight[:, None] / jnp.maximum(lax.optimization_barrier(jnp.sum(shape, axis=0)), 1.0)[None, :]

def spectral_table(size):
    bins = size // 2
    index = jnp.arange(size, dtype=jnp.int32)[:, None] * jnp.arange(bins, dtype=jnp.int32)[None, :] % size
    angle = index.astype(jnp.float32) * (2.0 * math.pi / size)
    return jnp.concatenate([jnp.cos(angle), -jnp.sin(angle)], axis=1) * (1.0 / math.sqrt(size))

def hann_window(size):
    return 0.5 - 0.5 * jnp.cos(jnp.arange(size, dtype=jnp.float32) * (2.0 * math.pi / size))

def modulation_table(times, count, length):
    index = times[:, None] * jnp.arange(1, count + 1, dtype=jnp.int32)[None, :] % length
    angle = index.astype(jnp.float32) * (2.0 * math.pi / length)
    return jnp.concatenate([jnp.cos(angle), -jnp.sin(angle)], axis=1) * (1.0 / math.sqrt(length))

def reference(wave, target_mod, lengths):
    records = wave.shape[0]
    half = FFT // 2
    window = hann_window(FFT)
    spectral = spectral_table(FFT)
    filters = band_table(half, BANDS)
    padded = jnp.concatenate([wave, jnp.zeros((records, half), jnp.float32)], axis=1)
    blocks = padded.reshape(records, FRAMES + 1, half)
    frames = jnp.concatenate([blocks[:, :-1], blocks[:, 1:]], axis=2) * window
    spectrum = jnp.einsum('rfn,nk->rfk', frames, spectral, precision=HIGH)
    real_stft = spectrum[..., :half]
    imag_stft = spectrum[..., half:]
    power = real_stft * real_stft + imag_stft * imag_stft
    energy = jnp.einsum('rfk,kb->rbf', power, filters, precision=HIGH)
    envelope = (energy + 0.05) ** 0.3
    times = jnp.arange(FRAMES, dtype=jnp.int32)
    valid = (times[None, :] < lengths[:, None]).astype(jnp.float32)
    masked = envelope * valid[:, None, :]
    counts = lengths.astype(jnp.float32) * BANDS
    loudness = lax.optimization_barrier(jnp.sum(masked, axis=(1, 2))) / counts + 1e-05
    normed = masked / loudness[:, None, None]
    table = modulation_table(times, K, FRAMES)
    spectra = jnp.dot(normed.reshape(records * BANDS, FRAMES), table, precision=HIGH, preferred_element_type=jnp.float32)
    real_mod = spectra[:, :K]
    imag_mod = spectra[:, K:]
    mod_power = real_mod * real_mod + imag_mod * imag_mod
    mismatch = jnp.log1p(mod_power) - target_mod
    loss = 0.5 * lax.optimization_barrier(jnp.sum((mismatch * mismatch).reshape(records, -1), axis=1))
    factor = 2.0 * mismatch / (1.0 + mod_power)
    grad_real = factor * real_mod
    grad_imag = factor * imag_mod
    inner = lax.optimization_barrier(jnp.sum((grad_real * real_mod + grad_imag * imag_mod).reshape(records, -1), axis=1))
    grad_spectra = jnp.concatenate([grad_real, grad_imag], axis=1)
    grad_normed = lax.dot_general(grad_spectra, table, (((1,), (1,)), ((), ())), precision=HIGH, preferred_element_type=jnp.float32)
    grad_normed = grad_normed.reshape(records, BANDS, FRAMES)
    grad_env = (grad_normed - (inner / counts)[:, None, None]) / loudness[:, None, None] * valid[:, None, :]
    grad_energy = 0.3 * (energy + 0.05) ** (-0.7) * grad_env
    grad_power = jnp.einsum('rbf,kb->rfk', grad_energy, filters, precision=HIGH)
    grad_spectrum = jnp.concatenate([2.0 * real_stft * grad_power, 2.0 * imag_stft * grad_power], axis=2)
    grad_frames = jnp.einsum('rfk,nk->rfn', grad_spectrum, spectral, precision=HIGH) * window
    leading = grad_frames[..., :half]
    trailing = grad_frames[..., half:]
    spare = jnp.zeros((records, 1, half), jnp.float32)
    summed = jnp.concatenate([leading, spare], axis=1) + jnp.concatenate([spare, trailing], axis=1)
    grad_wave = summed[:, :FRAMES].reshape(records, FRAMES * half)
    return (grad_wave, loss)
```

```python
import functools
import math

import jax
import jax.numpy as jnp
import ml_dtypes
import numpy as np
from jax import lax
from jax.experimental import pallas as pl
from jax.experimental.pallas import tpu as pltpu
from jax.sharding import PartitionSpec as P

FFT = 512
HALF = FFT // 2
BANDS = 96
OWN = BANDS // 2
RECORDS = 16
DEVICES = 32
LOCAL = 128
FRAMES = LOCAL * DEVICES
SIDE = 32
SLOT = OWN + 1
RATE = 16000.0
F32 = jnp.float32
BF16 = jnp.bfloat16
MESH = pl.DeviceIdType.MESH


def a_weight(freq):
    square = freq * freq
    upper = 12194.0**2 * square * square
    lower = (
        (square + 20.6**2)
        * np.sqrt((square + 107.7**2) * (square + 737.9**2))
        * (square + 12194.0**2)
    )
    return upper / lower


def bark_scale(freq):
    return 13.0 * np.arctan(0.00076 * freq) + 3.5 * np.arctan((freq / 7500.0) ** 2)


def band_table():
    freq = np.arange(HALF) * (RATE / FFT)
    top = bark_scale(np.float64(RATE / 2.0))
    centres = (np.arange(BANDS) + 0.5) * (top / BANDS)
    spread = max(0.5, 2.0 * top / BANDS)
    shape = np.maximum(0.0, 1.0 - np.abs(bark_scale(freq)[:, None] - centres[None, :]) / spread)
    weight = 0.1 + a_weight(freq) / a_weight(np.float64(1000.0))
    return shape * weight[:, None] / np.maximum(shape.sum(axis=0), 1.0)[None, :]


def two(table):
    high = table.astype(np.float32).astype(ml_dtypes.bfloat16)
    low = (table - high.astype(np.float64)).astype(np.float32).astype(ml_dtypes.bfloat16)
    return high, low


def against(table, axis):
    high, low = two(table)
    return np.concatenate([high, high, low], axis=axis)


def cycle(index, length):
    angle = (index % length) * (2.0 * math.pi / length)
    return np.cos(angle), np.sin(angle)


@functools.cache
def tables():
    n, m = np.arange(HALF)[:, None], np.arange(HALF // 2)[None, :]
    halves = []
    for odd in (0, 1):
        cos, sin = cycle(n * (2 * m + odd), FFT)
        halves.append(np.concatenate([cos, -sin], axis=1) / math.sqrt(FFT))
    forward = np.concatenate([against(h, 0) for h in halves], axis=1)
    backward = np.concatenate([against(h.T, 0) for h in halves], axis=1)
    bands = band_table()
    bands = np.concatenate([bands[0::2], bands[1::2]], axis=0).T
    tau, a = np.arange(LOCAL)[:, None], np.arange(SIDE)[None, :]
    cos, sin = cycle(tau * a, LOCAL)
    cos, sin = cos / math.sqrt(FRAMES), sin / math.sqrt(FRAMES)
    re = np.concatenate([cos, sin], axis=0)
    im = np.concatenate([-sin, cos], axis=0)
    to_bins = np.concatenate([re, im, re, im, im, re, im, re], axis=1)
    high, low = two(np.concatenate([re.T, im.T], axis=0))
    to_time = np.concatenate([high, high, low, np.zeros_like(low)], axis=0)
    cos, sin = cycle((np.arange(SIDE)[:, None] + 1) * np.arange(LOCAL)[None, :], FRAMES)
    turn = np.concatenate([cos, sin], axis=0).astype(np.float32)
    window = 0.5 - 0.5 * np.cos(np.arange(HALF) * (2.0 * math.pi / FFT))
    window = np.broadcast_to(window.astype(np.float32), (8, HALF))
    return (
        forward,
        against(bands, 1),
        against(bands, 0),
        backward,
        against(to_bins, 0),
        to_time,
        turn,
        np.ascontiguousarray(window),
    )


def three(x, axis=-1):
    high = x.astype(BF16)
    low = (x - high.astype(F32)).astype(BF16)
    return jnp.concatenate([high, low, high], axis=axis)


def times(a, b, dims=(((1,), (0,)), ((), ()))):
    return lax.dot_general(a, b, dims, preferred_element_type=F32)


def turned(z, k, n):
    re, im = z
    k = k % n
    if im is None:
        im = jnp.zeros_like(re)
    if k == 0:
        return re, im
    if 4 * k == n:
        return im, -re
    if 2 * k == n:
        return -re, -im
    if 4 * k == 3 * n:
        return -im, re
    c, s = math.cos(2 * math.pi * k / n), math.sin(2 * math.pi * k / n)
    if 8 * k == n:
        return c * (re + im), c * (im - re)
    return c * re + s * im, c * im - s * re


def real_forward(x):
    n = len(x)
    if n == 1:
        return [(x[0], None)]
    if n == 2:
        return [(x[0] + x[1], None), (x[0] - x[1], None)]
    even, odd = real_forward(x[0::2]), real_forward(x[1::2])
    out = [None] * (n // 2 + 1)
    out[0] = (even[0][0] + odd[0][0], None)
    out[n // 2] = (even[0][0] - odd[0][0], None)
    quarter = n // 4
    out[quarter] = (even[quarter][0], -odd[quarter][0])
    for k in range(1, quarter):
        tr, ti = turned(odd[k], k, n)
        er, ei = even[k]
        out[k] = (er + tr, ei + ti)
        out[n // 2 - k] = (er - tr, ti - ei)
    return out


def real_backward(q, n):
    if n == 1:
        return [q[0][0]]
    if n == 2:
        return [q[0][0] + q[1][0], q[0][0] - q[1][0]]
    half, quarter = n // 2, n // 4
    a, b = [], []
    for j in range(quarter + 1):
        (xr, xi), (yr, yi) = q[j], q[half - j]
        if j == 0:
            a.append((xr + yr, None))
            b.append((xr - yr, None))
        elif j == quarter:
            a.append((xr + xr, None))
            b.append((-(xi + xi), None))
        else:
            a.append((xr + yr, xi - yi))
            dr, di = xr - yr, xi + yi
            b.append(turned((dr, di), n - j, n))
    even, odd = real_backward(a, half), real_backward(b, half)
    out = [None] * n
    out[0::2], out[1::2] = even, odd
    return out


def kernel(
    wave,
    target,
    lengths,
    h_forward,
    h_bands,
    h_bands_t,
    h_backward,
    h_bins,
    h_time,
    h_turn,
    h_window,
    out,
    sums,
    forward,
    bands,
    bands_t,
    backward,
    bins,
    to_time,
    turn,
    window,
    wbuf,
    tbuf,
    ttall,
    tperm,
    stft,
    slope,
    send1,
    recv1,
    mid,
    send2,
    recv2,
    obuf,
    edge,
    wave_sem,
    table_sem,
    target_sem,
    halo_sem,
    s1_sem,
    r1_sem,
    s2_sem,
    r2_sem,
    edge_sem,
    out_sem,
):
    me = lax.axis_index("tm")
    pair = me // 2
    side = me % 2
    partner = me + 1 - 2 * side

    barrier = pltpu.get_barrier_semaphore()

    @pl.loop(1, DEVICES)
    def _(j):
        pl.semaphore_signal(
            barrier,
            inc=1,
            device_id={"tm": (me + j) % DEVICES},
            device_id_type=MESH,
        )

    rows = LOCAL * 16
    loads = [
        pltpu.make_async_copy(wave.at[g], wbuf.at[g, pl.ds(0, rows)], wave_sem.at[g])
        for g in range(2)
    ]
    held = [
        pltpu.make_async_copy(src, dst, table_sem.at[i])
        for i, (src, dst) in enumerate(
            (
                (h_forward, forward),
                (h_bands, bands),
                (h_window, window),
                (h_turn, turn),
                (h_bins, bins),
                (h_time, to_time),
                (h_bands_t, bands_t),
                (h_backward, backward),
            )
        )
    ]
    load_target = pltpu.make_async_copy(target, tbuf, target_sem)
    for copy in held[:3] + loads + held[3:] + [load_target]:
        copy.start()

    pl.semaphore_wait(barrier, DEVICES - 1)
    halo = pltpu.make_async_remote_copy(
        src_ref=wave.at[:, pl.ds(0, 16)],
        dst_ref=wbuf.at[:, pl.ds(rows, 16)],
        send_sem=halo_sem.at[0],
        recv_sem=halo_sem.at[1],
        device_id={"tm": (me + DEVICES - 1) % DEVICES},
        device_id_type=MESH,
    )
    halo.start()
    for copy in held + loads + [load_target]:
        copy.wait()
    halo.wait()
    last = me == DEVICES - 1
    wbuf[:, pl.ds(rows, 16), :] = jnp.where(last, 0.0, wbuf[:, pl.ds(rows, 16), :])

    lane = lax.broadcasted_iota(jnp.int32, (1, LOCAL), 1)

    def hops(r, later):
        start = (r % 8) + later * 16
        return jnp.concatenate(
            [wbuf[r // 8, pl.ds(start + 8 * h, LOCAL, stride=16), :] for h in range(2)], axis=1
        )

    def message1(r, s, d):
        return pltpu.make_async_remote_copy(
            src_ref=send1.at[r, s],
            dst_ref=recv1.at[me],
            send_sem=s1_sem.at[d],
            recv_sem=r1_sem.at[me],
            device_id={"tm": d},
            device_id_type=MESH,
        )

    win = window[0:1, :]

    @pl.loop(0, RECORDS // 2)
    def _(i):
        both = [(pair + 1 + 2 * i + e) % RECORDS for e in range(2)]
        now = jnp.concatenate([hops(r, 0) for r in both], axis=0)
        later = jnp.concatenate([hops(r, 1) for r in both], axis=0)
        added = later + win * (now - later)
        taken = win * (now + later) - later
        even = times(three(added), forward[:, 0:HALF])
        odd = times(three(taken), forward[:, HALF:FFT])
        power = [z[:, 0:LOCAL] * z[:, 0:LOCAL] + z[:, LOCAL:] * z[:, LOCAL:] for z in (even, odd)]
        power = three(jnp.concatenate(power, axis=1))
        energy = times(bands[...], power, (((1,), (1,)), ((), ())))
        for e, r in enumerate(both):
            stft[r, :, 0:HALF] = even[e * LOCAL : (e + 1) * LOCAL]
            stft[r, :, HALF:FFT] = odd[e * LOCAL : (e + 1) * LOCAL]
            lifted = energy[:, e * LOCAL : (e + 1) * LOCAL] + 0.05
            valid = (me * LOCAL + lane < lengths[r]).astype(F32)
            masked = jnp.exp(0.3 * jnp.log(lifted)) * valid
            slope[r] = 0.3 * masked / lifted
            total = jnp.sum(masked, axis=0, keepdims=True)
            for s in range(2):
                send1[r, s, 0:OWN, :] = masked[s * OWN : (s + 1) * OWN]
                send1[r, s, OWN:SLOT, :] = total

        for s in range(2):
            message1(both[0], s, 2 * both[0] + s).start()

        @pl.when(i < RECORDS // 2 - 1)
        def _():
            for s in range(2):
                message1(both[1], s, 2 * both[1] + s).start()

    message1(pair, 1 - side, partner).start()
    pltpu.make_async_copy(send1.at[pair, side], recv1.at[me], r1_sem.at[me]).start()

    for i in range(8):
        ttall[pl.ds(i * 128, 128), 0:OWN] = tbuf[:, i * 128 : (i + 1) * 128].T

    @pl.loop(0, SIDE)
    def _(c):
        one = ttall[pl.ds(c, SIDE, stride=SIDE), :]
        tperm[c] = jnp.concatenate([one] * 4, axis=0).T[0:OWN]

    @pl.loop(0, DEVICES)
    def _(j):
        pltpu.make_async_copy(recv1.at[j], recv1.at[j], r1_sem.at[j]).wait()

    @pl.loop(0, OWN // 8)
    def _(i):
        at = pl.ds(pl.multiple_of(i * 8, 8), 8)
        spectrum = real_forward([recv1[p, at, :] for p in range(DEVICES)])
        for c in range(SIDE):
            j = (c + 1) % SIDE
            re, im = spectrum[min(j, SIDE - j)]
            cos, sin = turn[c : c + 1, :], turn[SIDE + c : SIDE + c + 1, :]
            if im is None:
                mid[c, at, 0:LOCAL] = re * cos
                mid[c, at, LOCAL:] = -re * sin
            else:
                if j > SIDE // 2:
                    im = -im
                mid[c, at, 0:LOCAL] = re * cos + im * sin
                mid[c, at, LOCAL:] = im * cos - re * sin

    count = lengths[pair].astype(F32) * BANDS
    total = jnp.sum(recv1[:, OWN:SLOT, :], axis=0)
    loud = jnp.sum(total, axis=1, keepdims=True) / count + 1e-5
    scale = 1.0 / loud
    chunk = 8
    wide = lax.broadcasted_iota(jnp.int32, (chunk * OWN, LOCAL), 1)
    loss = jnp.zeros((8, LOCAL), F32)
    inner = jnp.zeros((8, LOCAL), F32)
    for i in range(SIDE // chunk):
        part = mid[i * chunk : (i + 1) * chunk].reshape(chunk * OWN, HALF)
        z = times(three(part), bins[...]) * scale
        here, other = z[:, 0:LOCAL], z[:, LOCAL:]
        power = here * here + other * other
        above = 1.0 + power
        wanted = tperm[i * chunk : (i + 1) * chunk].reshape(chunk * OWN, LOCAL)
        mismatch = jnp.log(above) - wanted
        factor = 2.0 * mismatch / above
        loss += jnp.sum((mismatch * mismatch).reshape(-1, 8, LOCAL), axis=0)
        inner += jnp.sum((factor * power).reshape(-1, 8, LOCAL), axis=0)
        grad = here * (factor * scale)
        high = grad.astype(BF16)
        first = jnp.where(wide < 2 * SIDE, high.astype(F32), grad - high.astype(F32))
        back = times(jnp.concatenate([first.astype(BF16), high], axis=1), to_time[...])
        mid[i * chunk : (i + 1) * chunk] = back.reshape(chunk, OWN, HALF)
    loss = 0.125 * jnp.sum(jnp.sum(loss, axis=0, keepdims=True), axis=1, keepdims=True)
    inner = 0.25 * jnp.sum(jnp.sum(inner, axis=0, keepdims=True), axis=1, keepdims=True)
    inner = inner / count * scale
    extra = jnp.where(lane == 0, loss, inner)
    send2[:, OWN:SLOT, :] = jnp.broadcast_to(extra[None], (DEVICES, 1, LOCAL))

    @pl.loop(0, OWN // 8)
    def _(i):
        at = pl.ds(pl.multiple_of(i * 8, 8), 8)

        def bin_of(j):
            c = (j - 1) % SIDE
            re, im = mid[c, at, 0:LOCAL], mid[c, at, LOCAL:]
            cos, sin = turn[c : c + 1, :], turn[SIDE + c : SIDE + c + 1, :]
            return re * cos - im * sin, re * sin + im * cos

        paired = [(bin_of(0)[0], None)]
        for j in range(1, SIDE // 2):
            (xr, xi), (yr, yi) = bin_of(j), bin_of(SIDE - j)
            paired.append((0.5 * (xr + yr), 0.5 * (xi - yi)))
        paired.append((bin_of(SIDE // 2)[0], None))
        for p, g in enumerate(real_backward(paired, SIDE)):
            send2[p, at, :] = g

    def message2(d):
        return pltpu.make_async_remote_copy(
            src_ref=send2.at[d],
            dst_ref=recv2.at[me],
            send_sem=s2_sem.at[d],
            recv_sem=r2_sem.at[me],
            device_id={"tm": d},
            device_id_type=MESH,
        )

    @pl.loop(0, RECORDS - 1)
    def _(i):
        q = (pair + 1 + i) % RECORDS
        for s in range(2):
            message2(2 * q + s).start()

    message2(partner).start()
    pltpu.make_async_copy(send2.at[me], recv2.at[me], r2_sem.at[me]).start()

    row = lax.broadcasted_iota(jnp.int32, (LOCAL, HALF), 0)

    @pl.loop(0, RECORDS // 2)
    def _(i):
        both = [(pair + 2 * RECORDS - 1 - 2 * i - e) % RECORDS for e in range(2)]
        powers = []
        for r in both:
            for s in range(2):
                d = 2 * r + s
                pltpu.make_async_copy(recv2.at[d], recv2.at[d], r2_sem.at[d]).wait()
            extras = recv2[2 * r, OWN:SLOT, :] + recv2[2 * r + 1, OWN:SLOT, :]
            sums[pl.ds(r, 1), :] = extras
            mean = extras[:, 1:2]
            grad = jnp.concatenate(
                [recv2[2 * r, 0:OWN, :], recv2[2 * r + 1, 0:OWN, :]], axis=0
            )
            powers.append(three(slope[r] * (grad - mean), axis=0))
        grad = times(
            jnp.concatenate(powers, axis=1), bands_t[...], (((0,), (0,)), ((), ()))
        )
        grad = grad + grad
        pieces = []
        for h in range(2):
            z = jnp.concatenate([stft[r, :, h * HALF : (h + 1) * HALF] for r in both], axis=0)
            g = grad[:, h * LOCAL : (h + 1) * LOCAL]
            z = z * jnp.concatenate([g, g], axis=1)
            pieces.append(times(three(z), backward[:, h * HALF : (h + 1) * HALF]))
        leading = win * (pieces[0] + pieces[1])
        trailing = (1.0 - win) * (pieces[0] - pieces[1])
        for e, r in enumerate(both):
            lead = leading[e * LOCAL : (e + 1) * LOCAL]
            trail = trailing[e * LOCAL : (e + 1) * LOCAL]
            moved = jnp.where(row == 0, 0.0, pltpu.roll(trail, 1, 0))
            full = lead + moved
            for h in range(2):
                start = (r % 8) + 8 * h
                cut = slice(h * LOCAL, (h + 1) * LOCAL)
                obuf[r // 8, pl.ds(start, LOCAL, stride=16), :] = full[:, cut]
                obuf[r // 8, pl.ds(rows + start, 1), :] = trail[LOCAL - 1 : LOCAL, cut]

    over = pltpu.make_async_remote_copy(
        src_ref=obuf.at[:, pl.ds(rows, 16)],
        dst_ref=edge,
        send_sem=edge_sem.at[0],
        recv_sem=edge_sem.at[1],
        device_id={"tm": (me + 1) % DEVICES},
        device_id_type=MESH,
    )
    over.start()
    body = pltpu.make_async_copy(
        obuf.at[:, pl.ds(16, rows - 16)], out.at[:, pl.ds(16, rows - 16)], out_sem.at[0]
    )
    body.start()

    @pl.loop(1, DEVICES)
    def _(j):
        d = (me + j) % DEVICES
        pltpu.make_async_copy(send1.at[d // 2, d % 2], send1.at[d // 2, d % 2], s1_sem.at[d]).wait()
        pltpu.make_async_copy(send2.at[d], send2.at[d], s2_sem.at[d]).wait()

    over.wait()
    obuf[:, pl.ds(0, 16), :] = obuf[:, pl.ds(0, 16), :] + jnp.where(me == 0, 0.0, edge[...])
    head = pltpu.make_async_copy(
        obuf.at[:, pl.ds(0, 16)], out.at[:, pl.ds(0, 16)], out_sem.at[1]
    )
    head.start()
    body.wait()
    head.wait()


def body(wave, target_mod, lengths):
    rows = LOCAL * 16
    wave = wave.reshape(2, 8, LOCAL * 2, 128).transpose(0, 2, 1, 3).reshape(2, rows, 128)
    held = [jnp.asarray(t) for t in tables()]
    space = pl.BlockSpec(memory_space=pl.ANY)
    scratch = [pltpu.VMEM(t.shape, t.dtype) for t in held]
    scratch += [
        pltpu.VMEM((2, rows + 16, 128), F32),
        pltpu.VMEM((OWN, SIDE * SIDE), F32),
        pltpu.VMEM((SIDE * SIDE, 128), F32),
        pltpu.VMEM((SIDE, OWN, 128), F32),
        pltpu.VMEM((RECORDS, LOCAL, FFT), F32),
        pltpu.VMEM((RECORDS, BANDS, LOCAL), F32),
        pltpu.VMEM((RECORDS, 2, SLOT, LOCAL), F32),
        pltpu.VMEM((DEVICES, SLOT, LOCAL), F32),
        pltpu.VMEM((SIDE, OWN, HALF), F32),
        pltpu.VMEM((DEVICES, SLOT, LOCAL), F32),
        pltpu.VMEM((DEVICES, SLOT, LOCAL), F32),
        pltpu.VMEM((2, rows + 16, 128), F32),
        pltpu.VMEM((2, 16, 128), F32),
        pltpu.SemaphoreType.DMA((2,)),
        pltpu.SemaphoreType.DMA((len(held),)),
        pltpu.SemaphoreType.DMA,
        pltpu.SemaphoreType.DMA((2,)),
        pltpu.SemaphoreType.DMA((DEVICES,)),
        pltpu.SemaphoreType.DMA((DEVICES,)),
        pltpu.SemaphoreType.DMA((DEVICES,)),
        pltpu.SemaphoreType.DMA((DEVICES,)),
        pltpu.SemaphoreType.DMA((2,)),
        pltpu.SemaphoreType.DMA((2,)),
    ]
    grad, sums = pl.pallas_call(
        kernel,
        out_shape=(
            jax.ShapeDtypeStruct((2, rows, 128), F32),
            jax.ShapeDtypeStruct((RECORDS, 128), F32),
        ),
        in_specs=[space, space, pl.BlockSpec(memory_space=pltpu.SMEM)] + [space] * len(held),
        out_specs=(space, pl.BlockSpec(memory_space=pltpu.VMEM)),
        scratch_shapes=scratch,
        compiler_params=pltpu.CompilerParams(
            collective_id=0, has_side_effects=True, vmem_limit_bytes=48 * 1024 * 1024
        ),
    )(wave, target_mod, lengths, *held)
    grad = grad.reshape(2, LOCAL * 2, 8, 128).transpose(0, 2, 1, 3).reshape(RECORDS, LOCAL * HALF)
    return grad, sums[:, 0]


def solution(mesh):
    in_specs = (P("rec", "tm"), P(("rec", "tm"), None), P("rec"))
    out_specs = (P("rec", "tm"), P("rec"))
    return jax.shard_map(body, mesh=mesh, in_specs=in_specs, out_specs=out_specs, check_vma=False)
```

```python
import functools
import math

import jax
import jax.numpy as jnp
import ml_dtypes
import numpy as np
from jax import lax
from jax.experimental import pallas as pl
from jax.experimental.pallas import tpu as pltpu
from jax.sharding import PartitionSpec as P

FFT = 512
HALF = FFT // 2
BANDS = 96
OWN = BANDS // 2
RECORDS = 16
DEVICES = 32
LOCAL = 128
FRAMES = LOCAL * DEVICES
SIDE = 32
PART = OWN // 2
SLOT = PART + 1
RATE = 16000.0
F32 = jnp.float32
BF16 = jnp.bfloat16
MESH = pl.DeviceIdType.MESH


def a_weight(freq):
    square = freq * freq
    upper = 12194.0**2 * square * square
    lower = (
        (square + 20.6**2)
        * np.sqrt((square + 107.7**2) * (square + 737.9**2))
        * (square + 12194.0**2)
    )
    return upper / lower


def bark_scale(freq):
    return 13.0 * np.arctan(0.00076 * freq) + 3.5 * np.arctan((freq / 7500.0) ** 2)


def band_table():
    freq = np.arange(HALF) * (RATE / FFT)
    top = bark_scale(np.float64(RATE / 2.0))
    centres = (np.arange(BANDS) + 0.5) * (top / BANDS)
    spread = max(0.5, 2.0 * top / BANDS)
    shape = np.maximum(0.0, 1.0 - np.abs(bark_scale(freq)[:, None] - centres[None, :]) / spread)
    weight = 0.1 + a_weight(freq) / a_weight(np.float64(1000.0))
    return shape * weight[:, None] / np.maximum(shape.sum(axis=0), 1.0)[None, :]


def two(table):
    high = table.astype(np.float32).astype(ml_dtypes.bfloat16)
    low = (table - high.astype(np.float64)).astype(np.float32).astype(ml_dtypes.bfloat16)
    return high, low


def against(table, axis):
    high, low = two(table)
    return np.concatenate([high, high, low], axis=axis)


def cycle(index, length):
    angle = (index % length) * (2.0 * math.pi / length)
    return np.cos(angle), np.sin(angle)


@functools.cache
def tables():
    n, m = np.arange(HALF)[:, None], np.arange(HALF // 2)[None, :]
    halves = []
    for odd in (0, 1):
        cos, sin = cycle(n * (2 * m + odd), FFT)
        halves.append(np.concatenate([cos, -sin], axis=1) / math.sqrt(FFT))
    forward = np.concatenate([against(h, 0) for h in halves], axis=1)
    backward = np.concatenate([against(h.T, 0) for h in halves], axis=1)
    bands = band_table()
    bands = np.concatenate([bands[0::2], bands[1::2]], axis=0).T
    tau, a = np.arange(LOCAL)[:, None], np.arange(SIDE)[None, :]
    cos, sin = cycle(tau * a, LOCAL)
    cos, sin = cos / math.sqrt(FRAMES), sin / math.sqrt(FRAMES)
    re = np.concatenate([cos, sin], axis=0)
    im = np.concatenate([-sin, cos], axis=0)
    to_bins = np.concatenate([re, im, re, im, im, re, im, re], axis=1)
    high, low = two(np.concatenate([re.T, im.T], axis=0))
    to_time = np.concatenate([high, high, low, np.zeros_like(low)], axis=0)
    cos, sin = cycle((np.arange(SIDE)[:, None] + 1) * np.arange(LOCAL)[None, :], FRAMES)
    turn = np.concatenate([cos, sin], axis=0).astype(np.float32)
    window = 0.5 - 0.5 * np.cos(np.arange(HALF) * (2.0 * math.pi / FFT))
    window = np.broadcast_to(window.astype(np.float32), (8, HALF))
    return (
        forward,
        against(bands, 1),
        against(bands, 0),
        backward,
        against(to_bins, 0),
        to_time,
        turn,
        np.ascontiguousarray(window),
    )


def three(x, axis=-1):
    high = x.astype(BF16)
    low = (x - high.astype(F32)).astype(BF16)
    return jnp.concatenate([high, low, high], axis=axis)


def times(a, b, dims=(((1,), (0,)), ((), ()))):
    return lax.dot_general(a, b, dims, preferred_element_type=F32)


def turned(z, k, n):
    re, im = z
    k = k % n
    if im is None:
        im = jnp.zeros_like(re)
    if k == 0:
        return re, im
    if 4 * k == n:
        return im, -re
    if 2 * k == n:
        return -re, -im
    if 4 * k == 3 * n:
        return -im, re
    c, s = math.cos(2 * math.pi * k / n), math.sin(2 * math.pi * k / n)
    if 8 * k == n:
        return c * (re + im), c * (im - re)
    return c * re + s * im, c * im - s * re


def real_forward(x):
    n = len(x)
    if n == 1:
        return [(x[0], None)]
    if n == 2:
        return [(x[0] + x[1], None), (x[0] - x[1], None)]
    even, odd = real_forward(x[0::2]), real_forward(x[1::2])
    out = [None] * (n // 2 + 1)
    out[0] = (even[0][0] + odd[0][0], None)
    out[n // 2] = (even[0][0] - odd[0][0], None)
    quarter = n // 4
    out[quarter] = (even[quarter][0], -odd[quarter][0])
    for k in range(1, quarter):
        tr, ti = turned(odd[k], k, n)
        er, ei = even[k]
        out[k] = (er + tr, ei + ti)
        out[n // 2 - k] = (er - tr, ti - ei)
    return out


def real_backward(q, n):
    if n == 1:
        return [q[0][0]]
    if n == 2:
        return [q[0][0] + q[1][0], q[0][0] - q[1][0]]
    half, quarter = n // 2, n // 4
    a, b = [], []
    for j in range(quarter + 1):
        (xr, xi), (yr, yi) = q[j], q[half - j]
        if j == 0:
            a.append((xr + yr, None))
            b.append((xr - yr, None))
        elif j == quarter:
            a.append((xr + xr, None))
            b.append((-(xi + xi), None))
        else:
            a.append((xr + yr, xi - yi))
            dr, di = xr - yr, xi + yi
            b.append(turned((dr, di), n - j, n))
    even, odd = real_backward(a, half), real_backward(b, half)
    out = [None] * n
    out[0::2], out[1::2] = even, odd
    return out


def kernel(
    wave,
    target,
    lengths,
    h_forward,
    h_bands,
    h_bands_t,
    h_backward,
    h_bins,
    h_time,
    h_turn,
    h_window,
    out,
    losses,
    forward,
    bands,
    bands_t,
    backward,
    bins,
    to_time,
    turn,
    window,
    wbuf,
    tbuf,
    ttall,
    tperm,
    stft,
    slope,
    send1a,
    send1b,
    recv1a,
    recv1b,
    mid,
    send2a,
    send2b,
    recv2a,
    recv2b,
    obuf,
    edge,
    wave_sem,
    table_sem,
    target_sem,
    halo_sem,
    s1_sem,
    r1_sem,
    s2_sem,
    r2_sem,
    edge_sem,
    out_sem,
):
    me = lax.axis_index("tm")
    pair = me // 2
    side = me % 2

    barrier = pltpu.get_barrier_semaphore()

    @pl.loop(1, DEVICES)
    def _(j):
        pl.semaphore_signal(
            barrier,
            inc=1,
            device_id={"tm": (me + j) % DEVICES},
            device_id_type=MESH,
        )

    rows = LOCAL * 16
    loads = [
        pltpu.make_async_copy(wave.at[g], wbuf.at[g, pl.ds(0, rows)], wave_sem.at[g])
        for g in range(2)
    ]
    held = [
        pltpu.make_async_copy(src, dst, table_sem.at[i])
        for i, (src, dst) in enumerate(
            (
                (h_forward, forward),
                (h_bands, bands),
                (h_window, window),
                (h_turn, turn),
                (h_bins, bins),
                (h_time, to_time),
                (h_bands_t, bands_t),
                (h_backward, backward),
            )
        )
    ]
    load_target = pltpu.make_async_copy(target, tbuf, target_sem)
    for copy in held[:3] + loads + held[3:] + [load_target]:
        copy.start()

    pl.semaphore_wait(barrier, DEVICES - 1)
    halo = pltpu.make_async_remote_copy(
        src_ref=wave.at[:, pl.ds(0, 16)],
        dst_ref=wbuf.at[:, pl.ds(rows, 16)],
        send_sem=halo_sem.at[0],
        recv_sem=halo_sem.at[1],
        device_id={"tm": (me + DEVICES - 1) % DEVICES},
        device_id_type=MESH,
    )
    halo.start()
    for copy in held + loads + [load_target]:
        copy.wait()
    halo.wait()
    last = me == DEVICES - 1
    wbuf[:, pl.ds(rows, 16), :] = jnp.where(last, 0.0, wbuf[:, pl.ds(rows, 16), :])

    lane = lax.broadcasted_iota(jnp.int32, (1, LOCAL), 1)

    def hops(r, later):
        start = (r % 8) + later * 16
        return jnp.concatenate(
            [wbuf[r // 8, pl.ds(start + 8 * h, LOCAL, stride=16), :] for h in range(2)], axis=1
        )

    send1, recv1 = (send1a, send1b), (recv1a, recv1b)
    send2, recv2 = (send2a, send2b), (recv2a, recv2b)

    def message1(h, r, s):
        d = 2 * r + s
        return pltpu.make_async_remote_copy(
            src_ref=send1[h].at[r, s],
            dst_ref=recv1[h].at[me],
            send_sem=s1_sem.at[h, d],
            recv_sem=r1_sem.at[h, me],
            device_id={"tm": d},
            device_id_type=MESH,
        )

    def message2(h, d):
        return pltpu.make_async_remote_copy(
            src_ref=send2[h].at[d],
            dst_ref=recv2[h].at[me],
            send_sem=s2_sem.at[h, d],
            recv_sem=r2_sem.at[h, me],
            device_id={"tm": d},
            device_id_type=MESH,
        )

    def apart(i):
        return (pair + i + RECORDS // 2) % RECORDS, (pair + RECORDS // 2 - 1 - i) % RECORDS

    def all_apart(send):
        @pl.loop(0, RECORDS // 2)
        def _(i):
            both = apart(i)
            for s in range(2):
                send(both[0], s)

            @pl.when(i < RECORDS // 2 - 1)
            def _():
                for s in range(2):
                    send(both[1], s)

        send(pair, 1 - side)

    def await_all(ref, sem):
        @pl.loop(0, DEVICES)
        def _(j):
            pltpu.make_async_copy(ref.at[j], ref.at[j], sem.at[j]).wait()

    win = window[0:1, :]

    @pl.loop(0, RECORDS // 2)
    def _(i):
        both = apart(i)
        now = jnp.concatenate([hops(r, 0) for r in both], axis=0)
        later = jnp.concatenate([hops(r, 1) for r in both], axis=0)
        added = later + win * (now - later)
        taken = win * (now + later) - later
        even = times(three(added), forward[:, 0:HALF])
        odd = times(three(taken), forward[:, HALF:FFT])
        power = [z[:, 0:LOCAL] * z[:, 0:LOCAL] + z[:, LOCAL:] * z[:, LOCAL:] for z in (even, odd)]
        power = three(jnp.concatenate(power, axis=1))
        energy = times(bands[...], power, (((1,), (1,)), ((), ())))
        for e, r in enumerate(both):
            stft[r, :, 0:HALF] = even[e * LOCAL : (e + 1) * LOCAL]
            stft[r, :, HALF:FFT] = odd[e * LOCAL : (e + 1) * LOCAL]
            lifted = energy[:, e * LOCAL : (e + 1) * LOCAL] + 0.05
            valid = (me * LOCAL + lane < lengths[r]).astype(F32)
            masked = jnp.exp(0.3 * jnp.log(lifted)) * valid
            slope[r] = 0.3 * masked / lifted
            total = jnp.sum(masked, axis=0, keepdims=True)
            for s in range(2):
                send1a[r, s, 0:PART, :] = masked[s * OWN : s * OWN + PART]
                send1a[r, s, PART:SLOT, :] = total
                send1b[r, s] = masked[s * OWN + PART : (s + 1) * OWN]

        for s in range(2):
            message1(0, both[0], s).start()

        @pl.when(i < RECORDS // 2 - 1)
        def _():
            for s in range(2):
                message1(0, both[1], s).start()

    message1(0, pair, 1 - side).start()
    for h in range(2):
        pltpu.make_async_copy(send1[h].at[pair, side], recv1[h].at[me], r1_sem.at[h, me]).start()
    all_apart(lambda r, s: message1(1, r, s).start())

    for i in range(8):
        ttall[pl.ds(i * 128, 128), 0:OWN] = tbuf[:, i * 128 : (i + 1) * 128].T

    @pl.loop(0, SIDE)
    def _(c):
        one = ttall[pl.ds(c, SIDE, stride=SIDE), :]
        wanted = jnp.concatenate([one] * 4, axis=0).T
        for h in range(2):
            tperm[h, c] = wanted[h * PART : (h + 1) * PART]

    count = lengths[pair].astype(F32) * BANDS
    chunk = 16
    wide = lax.broadcasted_iota(jnp.int32, (chunk * PART, LOCAL), 1)

    def over_devices(h):
        @pl.loop(0, PART // 8)
        def _(i):
            at = pl.ds(pl.multiple_of(i * 8, 8), 8)
            spectrum = real_forward([recv1[h][p, at, :] for p in range(DEVICES)])
            for c in range(SIDE):
                j = (c + 1) % SIDE
                re, im = spectrum[min(j, SIDE - j)]
                cos, sin = turn[c : c + 1, :], turn[SIDE + c : SIDE + c + 1, :]
                if im is None:
                    mid[h, c, at, 0:LOCAL] = re * cos
                    mid[h, c, at, LOCAL:] = -re * sin
                else:
                    if j > SIDE // 2:
                        im = -im
                    mid[h, c, at, 0:LOCAL] = re * cos + im * sin
                    mid[h, c, at, LOCAL:] = im * cos - re * sin

    def in_device(h, scale):
        loss = jnp.zeros((8, LOCAL), F32)
        inner = jnp.zeros((8, LOCAL), F32)
        for i in range(SIDE // chunk):
            part = mid[h, i * chunk : (i + 1) * chunk].reshape(chunk * PART, HALF)
            z = times(three(part), bins[...]) * scale
            here, other = z[:, 0:LOCAL], z[:, LOCAL:]
            power = here * here + other * other
            above = 1.0 + power
            wanted = tperm[h, i * chunk : (i + 1) * chunk].reshape(chunk * PART, LOCAL)
            mismatch = jnp.log(above) - wanted
            factor = 2.0 * mismatch / above
            loss += jnp.sum((mismatch * mismatch).reshape(-1, 8, LOCAL), axis=0)
            inner += jnp.sum((factor * power).reshape(-1, 8, LOCAL), axis=0)
            grad = here * (factor * scale)
            high = grad.astype(BF16)
            first = jnp.where(wide < 2 * SIDE, high.astype(F32), grad - high.astype(F32))
            back = times(jnp.concatenate([first.astype(BF16), high], axis=1), to_time[...])
            mid[h, i * chunk : (i + 1) * chunk] = back.reshape(chunk, PART, HALF)
        return loss, inner

    def to_devices(h):
        @pl.loop(0, PART // 8)
        def _(i):
            at = pl.ds(pl.multiple_of(i * 8, 8), 8)

            def bin_of(j):
                c = (j - 1) % SIDE
                re, im = mid[h, c, at, 0:LOCAL], mid[h, c, at, LOCAL:]
                cos, sin = turn[c : c + 1, :], turn[SIDE + c : SIDE + c + 1, :]
                return re * cos - im * sin, re * sin + im * cos

            paired = [(bin_of(0)[0], None)]
            for j in range(1, SIDE // 2):
                (xr, xi), (yr, yi) = bin_of(j), bin_of(SIDE - j)
                paired.append((0.5 * (xr + yr), 0.5 * (xi - yi)))
            paired.append((bin_of(SIDE // 2)[0], None))
            for p, g in enumerate(real_backward(paired, SIDE)):
                send2[h][p, at, :] = g

    def back(h):
        all_apart(lambda r, s: message2(h, 2 * r + s).start())
        pltpu.make_async_copy(send2[h].at[me], recv2[h].at[me], r2_sem.at[h, me]).start()

    await_all(recv1a, r1_sem.at[0])
    over_devices(0)
    total = jnp.sum(recv1a[:, PART:SLOT, :], axis=0)
    loud = jnp.sum(total, axis=1, keepdims=True) / count + 1e-5
    scale = 1.0 / loud
    loss, inner = in_device(0, scale)
    to_devices(0)
    back(0)
    await_all(recv1b, r1_sem.at[1])
    over_devices(1)
    more_loss, more_inner = in_device(1, scale)
    loss, inner = loss + more_loss, inner + more_inner
    loss = 0.125 * jnp.sum(jnp.sum(loss, axis=0, keepdims=True), axis=1, keepdims=True)
    inner = 0.25 * jnp.sum(jnp.sum(inner, axis=0, keepdims=True), axis=1, keepdims=True)
    inner = inner / count * scale
    extra = jnp.where(lane == 0, loss, inner)
    send2b[:, PART:SLOT, :] = jnp.broadcast_to(extra[None], (DEVICES, 1, LOCAL))
    to_devices(1)
    back(1)

    row = lax.broadcasted_iota(jnp.int32, (LOCAL, HALF), 0)
    losses[...] = jnp.zeros((1, LOCAL), F32)

    @pl.loop(0, RECORDS // 2)
    def _(i):
        both = [(pair + RECORDS // 2 - i) % RECORDS, (pair + RECORDS // 2 + 1 + i) % RECORDS]
        powers = []
        for r in both:
            for d in (2 * r, 2 * r + 1):
                for h in range(2):
                    pltpu.make_async_copy(recv2[h].at[d], recv2[h].at[d], r2_sem.at[h, d]).wait()
            extras = recv2b[2 * r, PART:SLOT, :] + recv2b[2 * r + 1, PART:SLOT, :]
            losses[...] = jnp.where(lane == r, extras[:, 0:1], losses[...])
            mean = extras[:, 1:2]
            grad = jnp.concatenate(
                [ref[2 * r + s, 0:PART, :] for s in range(2) for ref in recv2], axis=0
            )
            powers.append(three(slope[r] * (grad - mean), axis=0))
        grad = times(
            jnp.concatenate(powers, axis=1), bands_t[...], (((0,), (0,)), ((), ()))
        )
        grad = grad + grad
        pieces = []
        for h in range(2):
            z = jnp.concatenate([stft[r, :, h * HALF : (h + 1) * HALF] for r in both], axis=0)
            g = grad[:, h * LOCAL : (h + 1) * LOCAL]
            z = z * jnp.concatenate([g, g], axis=1)
            pieces.append(times(three(z), backward[:, h * HALF : (h + 1) * HALF]))
        leading = win * (pieces[0] + pieces[1])
        trailing = (1.0 - win) * (pieces[0] - pieces[1])
        for e, r in enumerate(both):
            lead = leading[e * LOCAL : (e + 1) * LOCAL]
            trail = trailing[e * LOCAL : (e + 1) * LOCAL]
            moved = jnp.where(row == 0, 0.0, pltpu.roll(trail, 1, 0))
            full = lead + moved
            for h in range(2):
                start = (r % 8) + 8 * h
                cut = slice(h * LOCAL, (h + 1) * LOCAL)
                obuf[r // 8, pl.ds(start, LOCAL, stride=16), :] = full[:, cut]
                obuf[r // 8, pl.ds(rows + start, 1), :] = trail[LOCAL - 1 : LOCAL, cut]

    over = pltpu.make_async_remote_copy(
        src_ref=obuf.at[:, pl.ds(rows, 16)],
        dst_ref=edge,
        send_sem=edge_sem.at[0],
        recv_sem=edge_sem.at[1],
        device_id={"tm": (me + 1) % DEVICES},
        device_id_type=MESH,
    )
    over.start()
    body = pltpu.make_async_copy(
        obuf.at[:, pl.ds(16, rows - 16)], out.at[:, pl.ds(16, rows - 16)], out_sem.at[0]
    )
    body.start()

    @pl.loop(1, DEVICES)
    def _(j):
        d = (me + j) % DEVICES
        for h in range(2):
            one, two = send1[h].at[d // 2, d % 2], send2[h].at[d]
            pltpu.make_async_copy(one, one, s1_sem.at[h, d]).wait()
            pltpu.make_async_copy(two, two, s2_sem.at[h, d]).wait()

    over.wait()
    obuf[:, pl.ds(0, 16), :] = obuf[:, pl.ds(0, 16), :] + jnp.where(me == 0, 0.0, edge[...])
    head = pltpu.make_async_copy(
        obuf.at[:, pl.ds(0, 16)], out.at[:, pl.ds(0, 16)], out_sem.at[1]
    )
    head.start()
    body.wait()
    head.wait()


def hand_over(grad, losses, out, loss, sem):
    step = LOCAL * 16 // 4
    copies = []
    for i in range(8):
        at = (i // 4, pl.ds((i % 4) * step, step))
        copies.append(pltpu.make_async_copy(grad.at[at], out.at[at], sem.at[i]))
        copies[-1].start()
    for r in range(RECORDS):
        loss[r] = losses[0, r]
    for copy in copies:
        copy.wait()


def body(wave, target_mod, lengths):
    rows = LOCAL * 16
    wave = wave.reshape(2, 8, LOCAL * 2, 128).transpose(0, 2, 1, 3).reshape(2, rows, 128)
    held = [jnp.asarray(t) for t in tables()]
    space = pl.BlockSpec(memory_space=pl.ANY)
    scratch = [pltpu.VMEM(t.shape, t.dtype) for t in held]
    scratch += [
        pltpu.VMEM((2, rows + 16, 128), F32),
        pltpu.VMEM((OWN, SIDE * SIDE), F32),
        pltpu.VMEM((SIDE * SIDE, 128), F32),
        pltpu.VMEM((2, SIDE, PART, 128), F32),
        pltpu.VMEM((RECORDS, LOCAL, FFT), F32),
        pltpu.VMEM((RECORDS, BANDS, LOCAL), F32),
        pltpu.VMEM((RECORDS, 2, SLOT, LOCAL), F32),
        pltpu.VMEM((RECORDS, 2, PART, LOCAL), F32),
        pltpu.VMEM((DEVICES, SLOT, LOCAL), F32),
        pltpu.VMEM((DEVICES, PART, LOCAL), F32),
        pltpu.VMEM((2, SIDE, PART, HALF), F32),
        pltpu.VMEM((DEVICES, PART, LOCAL), F32),
        pltpu.VMEM((DEVICES, SLOT, LOCAL), F32),
        pltpu.VMEM((DEVICES, PART, LOCAL), F32),
        pltpu.VMEM((DEVICES, SLOT, LOCAL), F32),
        pltpu.VMEM((2, rows + 16, 128), F32),
        pltpu.VMEM((2, 16, 128), F32),
        pltpu.SemaphoreType.DMA((2,)),
        pltpu.SemaphoreType.DMA((len(held),)),
        pltpu.SemaphoreType.DMA,
        pltpu.SemaphoreType.DMA((2,)),
        pltpu.SemaphoreType.DMA((2, DEVICES)),
        pltpu.SemaphoreType.DMA((2, DEVICES)),
        pltpu.SemaphoreType.DMA((2, DEVICES)),
        pltpu.SemaphoreType.DMA((2, DEVICES)),
        pltpu.SemaphoreType.DMA((2,)),
        pltpu.SemaphoreType.DMA((2,)),
    ]
    grad, losses = pl.pallas_call(
        kernel,
        out_shape=(
            jax.ShapeDtypeStruct((2, rows, 128), F32),
            jax.ShapeDtypeStruct((1, LOCAL), F32),
        ),
        in_specs=[space, space, pl.BlockSpec(memory_space=pltpu.SMEM)] + [space] * len(held),
        out_specs=(space, pl.BlockSpec(memory_space=pltpu.VMEM)),
        scratch_shapes=scratch,
        compiler_params=pltpu.CompilerParams(
            collective_id=0, has_side_effects=True, vmem_limit_bytes=62 * 1024 * 1024
        ),
    )(wave, target_mod, lengths, *held)
    grad, loss = pl.pallas_call(
        hand_over,
        out_shape=(
            jax.ShapeDtypeStruct((2, rows, 128), F32),
            jax.ShapeDtypeStruct((RECORDS,), F32),
        ),
        in_specs=[space, pl.BlockSpec(memory_space=pltpu.SMEM)],
        out_specs=(space, pl.BlockSpec(memory_space=pltpu.SMEM)),
        scratch_shapes=[pltpu.SemaphoreType.DMA((8,))],
        compiler_params=pltpu.CompilerParams(vmem_limit_bytes=62 * 1024 * 1024),
    )(grad, losses)
    grad = grad.reshape(2, LOCAL * 2, 8, 128).transpose(0, 2, 1, 3).reshape(RECORDS, LOCAL * HALF)
    return grad, loss


def solution(mesh):
    in_specs = (P("rec", "tm"), P(("rec", "tm"), None), P("rec"))
    out_specs = (P("rec", "tm"), P("rec"))
    return jax.shard_map(body, mesh=mesh, in_specs=in_specs, out_specs=out_specs, check_vma=False)
```

```python
import functools
import math

import jax
import jax.numpy as jnp
import ml_dtypes
import numpy as np
from jax import lax
from jax.experimental import pallas as pl
from jax.experimental.pallas import tpu as pltpu
from jax.sharding import PartitionSpec as P

FFT = 512
HALF = FFT // 2
BANDS = 96
OWN = BANDS // 2
RECORDS = 16
DEVICES = 32
LOCAL = 128
FRAMES = LOCAL * DEVICES
SIDE = 32
PART = OWN // 2
SLOT = PART + 1
RATE = 16000.0
F32 = jnp.float32
BF16 = jnp.bfloat16
MESH = pl.DeviceIdType.MESH


def a_weight(freq):
    square = freq * freq
    upper = 12194.0**2 * square * square
    lower = (
        (square + 20.6**2)
        * np.sqrt((square + 107.7**2) * (square + 737.9**2))
        * (square + 12194.0**2)
    )
    return upper / lower


def bark_scale(freq):
    return 13.0 * np.arctan(0.00076 * freq) + 3.5 * np.arctan((freq / 7500.0) ** 2)


def band_table():
    freq = np.arange(HALF) * (RATE / FFT)
    top = bark_scale(np.float64(RATE / 2.0))
    centres = (np.arange(BANDS) + 0.5) * (top / BANDS)
    spread = max(0.5, 2.0 * top / BANDS)
    shape = np.maximum(0.0, 1.0 - np.abs(bark_scale(freq)[:, None] - centres[None, :]) / spread)
    weight = 0.1 + a_weight(freq) / a_weight(np.float64(1000.0))
    return shape * weight[:, None] / np.maximum(shape.sum(axis=0), 1.0)[None, :]


def two(table):
    high = table.astype(np.float32).astype(ml_dtypes.bfloat16)
    low = (table - high.astype(np.float64)).astype(np.float32).astype(ml_dtypes.bfloat16)
    return high, low


def against(table, axis):
    high, low = two(table)
    return np.concatenate([high, high, low], axis=axis)


def cycle(index, length):
    angle = (index % length) * (2.0 * math.pi / length)
    return np.cos(angle), np.sin(angle)


@functools.cache
def tables():
    n, m = np.arange(HALF)[:, None], np.arange(HALF // 2)[None, :]
    halves = []
    for odd in (0, 1):
        cos, sin = cycle(n * (2 * m + odd), FFT)
        halves.append(np.concatenate([cos, -sin], axis=1) / math.sqrt(FFT))
    forward = np.concatenate([against(h, 0) for h in halves], axis=1)
    backward = np.concatenate([against(h.T, 0) for h in halves], axis=1)
    bands = band_table()
    bands = np.concatenate([bands[0::2], bands[1::2]], axis=0).T
    tau, a = np.arange(LOCAL)[:, None], np.arange(SIDE)[None, :]
    cos, sin = cycle(tau * a, LOCAL)
    cos, sin = cos / math.sqrt(FRAMES), sin / math.sqrt(FRAMES)
    re = np.concatenate([cos, sin], axis=0)
    im = np.concatenate([-sin, cos], axis=0)
    to_bins = np.concatenate([re, im, re, im, im, re, im, re], axis=1)
    high, low = two(np.concatenate([re.T, im.T], axis=0))
    to_time = np.concatenate([high, high, low, np.zeros_like(low)], axis=0)
    cos, sin = cycle((np.arange(SIDE)[:, None] + 1) * np.arange(LOCAL)[None, :], FRAMES)
    turn = np.concatenate([cos, sin], axis=0).astype(np.float32)
    window = 0.5 - 0.5 * np.cos(np.arange(HALF) * (2.0 * math.pi / FFT))
    window = np.broadcast_to(window.astype(np.float32), (8, HALF))
    return (
        forward,
        against(bands, 1),
        against(bands, 0),
        backward,
        against(to_bins, 0),
        to_time,
        turn,
        np.ascontiguousarray(window),
    )


def three(x, axis=-1):
    high = x.astype(BF16)
    low = (x - high.astype(F32)).astype(BF16)
    return jnp.concatenate([high, low, high], axis=axis)


def times(a, b, dims=(((1,), (0,)), ((), ()))):
    return lax.dot_general(a, b, dims, preferred_element_type=F32)


def turned(z, k, n):
    re, im = z
    k = k % n
    if im is None:
        im = jnp.zeros_like(re)
    if k == 0:
        return re, im
    if 4 * k == n:
        return im, -re
    if 2 * k == n:
        return -re, -im
    if 4 * k == 3 * n:
        return -im, re
    c, s = math.cos(2 * math.pi * k / n), math.sin(2 * math.pi * k / n)
    if 8 * k == n:
        return c * (re + im), c * (im - re)
    return c * re + s * im, c * im - s * re


def real_forward(x):
    n = len(x)
    if n == 1:
        return [(x[0], None)]
    if n == 2:
        return [(x[0] + x[1], None), (x[0] - x[1], None)]
    even, odd = real_forward(x[0::2]), real_forward(x[1::2])
    out = [None] * (n // 2 + 1)
    out[0] = (even[0][0] + odd[0][0], None)
    out[n // 2] = (even[0][0] - odd[0][0], None)
    quarter = n // 4
    out[quarter] = (even[quarter][0], -odd[quarter][0])
    for k in range(1, quarter):
        tr, ti = turned(odd[k], k, n)
        er, ei = even[k]
        out[k] = (er + tr, ei + ti)
        out[n // 2 - k] = (er - tr, ti - ei)
    return out


def real_backward(q, n):
    if n == 1:
        return [q[0][0]]
    if n == 2:
        return [q[0][0] + q[1][0], q[0][0] - q[1][0]]
    half, quarter = n // 2, n // 4
    a, b = [], []
    for j in range(quarter + 1):
        (xr, xi), (yr, yi) = q[j], q[half - j]
        if j == 0:
            a.append((xr + yr, None))
            b.append((xr - yr, None))
        elif j == quarter:
            a.append((xr + xr, None))
            b.append((-(xi + xi), None))
        else:
            a.append((xr + yr, xi - yi))
            dr, di = xr - yr, xi + yi
            b.append(turned((dr, di), n - j, n))
    even, odd = real_backward(a, half), real_backward(b, half)
    out = [None] * n
    out[0::2], out[1::2] = even, odd
    return out


def kernel(
    wave,
    target,
    lengths,
    h_forward,
    h_bands,
    h_bands_t,
    h_backward,
    h_bins,
    h_time,
    h_turn,
    h_window,
    out,
    edge,
    losses,
    forward,
    bands,
    bands_t,
    backward,
    bins,
    to_time,
    turn,
    window,
    wbuf,
    tbuf,
    ttall,
    tperm,
    stft,
    slope,
    send1a,
    send1b,
    recv1a,
    recv1b,
    mid,
    send2a,
    send2b,
    recv2a,
    recv2b,
    obuf,
    wave_sem,
    table_sem,
    target_sem,
    halo_sem,
    s1_sem,
    r1_sem,
    s2_sem,
    r2_sem,
    edge_sem,
    out_sem,
):
    me = lax.axis_index("tm")
    pair = me // 2
    side = me % 2

    barrier = pltpu.get_barrier_semaphore()

    @pl.loop(1, DEVICES)
    def _(j):
        pl.semaphore_signal(
            barrier,
            inc=1,
            device_id={"tm": (me + j) % DEVICES},
            device_id_type=MESH,
        )

    rows = LOCAL * 16
    loads = [
        pltpu.make_async_copy(wave.at[g], wbuf.at[g, pl.ds(0, rows)], wave_sem.at[g])
        for g in range(2)
    ]
    held = [
        pltpu.make_async_copy(src, dst, table_sem.at[i])
        for i, (src, dst) in enumerate(
            (
                (h_forward, forward),
                (h_bands, bands),
                (h_window, window),
                (h_turn, turn),
                (h_bins, bins),
                (h_time, to_time),
                (h_bands_t, bands_t),
                (h_backward, backward),
            )
        )
    ]
    load_target = pltpu.make_async_copy(target, tbuf, target_sem)
    for copy in held[:3] + loads + held[3:] + [load_target]:
        copy.start()

    pl.semaphore_wait(barrier, DEVICES - 1)
    halo = pltpu.make_async_remote_copy(
        src_ref=wave.at[:, pl.ds(0, 16)],
        dst_ref=wbuf.at[:, pl.ds(rows, 16)],
        send_sem=halo_sem.at[0],
        recv_sem=halo_sem.at[1],
        device_id={"tm": (me + DEVICES - 1) % DEVICES},
        device_id_type=MESH,
    )
    halo.start()
    for copy in held + loads + [load_target]:
        copy.wait()
    halo.wait()
    last = me == DEVICES - 1
    wbuf[:, pl.ds(rows, 16), :] = jnp.where(last, 0.0, wbuf[:, pl.ds(rows, 16), :])

    lane = lax.broadcasted_iota(jnp.int32, (1, LOCAL), 1)

    def hops(r, later):
        start = (r % 8) + later * 16
        return jnp.concatenate(
            [wbuf[r // 8, pl.ds(start + 8 * h, LOCAL, stride=16), :] for h in range(2)], axis=1
        )

    send1, recv1 = (send1a, send1b), (recv1a, recv1b)
    send2, recv2 = (send2a, send2b), (recv2a, recv2b)

    def message1(h, r, s):
        d = 2 * r + s
        return pltpu.make_async_remote_copy(
            src_ref=send1[h].at[r, s],
            dst_ref=recv1[h].at[me],
            send_sem=s1_sem.at[h, d],
            recv_sem=r1_sem.at[h, me],
            device_id={"tm": d},
            device_id_type=MESH,
        )

    def message2(h, d):
        return pltpu.make_async_remote_copy(
            src_ref=send2[h].at[d],
            dst_ref=recv2[h].at[me],
            send_sem=s2_sem.at[h, d],
            recv_sem=r2_sem.at[h, me],
            device_id={"tm": d},
            device_id_type=MESH,
        )

    def apart(i):
        return (pair + i + RECORDS // 2) % RECORDS, (pair + RECORDS // 2 - 1 - i) % RECORDS

    def all_apart(send):
        @pl.loop(0, RECORDS // 2)
        def _(i):
            both = apart(i)
            for s in range(2):
                send(both[0], s)

            @pl.when(i < RECORDS // 2 - 1)
            def _():
                for s in range(2):
                    send(both[1], s)

        send(pair, 1 - side)

    def await_all(ref, sem):
        @pl.loop(0, DEVICES)
        def _(j):
            pltpu.make_async_copy(ref.at[j], ref.at[j], sem.at[j]).wait()

    win = window[0:1, :]

    @pl.loop(0, RECORDS // 2)
    def _(i):
        both = apart(i)
        now = jnp.concatenate([hops(r, 0) for r in both], axis=0)
        later = jnp.concatenate([hops(r, 1) for r in both], axis=0)
        added = later + win * (now - later)
        taken = win * (now + later) - later
        even = times(three(added), forward[:, 0:HALF])
        odd = times(three(taken), forward[:, HALF:FFT])
        power = [z[:, 0:LOCAL] * z[:, 0:LOCAL] + z[:, LOCAL:] * z[:, LOCAL:] for z in (even, odd)]
        power = three(jnp.concatenate(power, axis=1))
        energy = times(bands[...], power, (((1,), (1,)), ((), ())))
        for e, r in enumerate(both):
            stft[r, :, 0:HALF] = even[e * LOCAL : (e + 1) * LOCAL]
            stft[r, :, HALF:FFT] = odd[e * LOCAL : (e + 1) * LOCAL]
            lifted = energy[:, e * LOCAL : (e + 1) * LOCAL] + 0.05
            valid = (me * LOCAL + lane < lengths[r]).astype(F32)
            masked = jnp.exp(0.3 * jnp.log(lifted)) * valid
            slope[r] = 0.3 * masked / lifted
            total = jnp.sum(masked, axis=0, keepdims=True)
            for s in range(2):
                send1a[r, s, 0:PART, :] = masked[s * OWN : s * OWN + PART]
                send1a[r, s, PART:SLOT, :] = total
                send1b[r, s] = masked[s * OWN + PART : (s + 1) * OWN]

        for s in range(2):
            message1(0, both[0], s).start()

        @pl.when(i < RECORDS // 2 - 1)
        def _():
            for s in range(2):
                message1(0, both[1], s).start()

    message1(0, pair, 1 - side).start()
    for h in range(2):
        pltpu.make_async_copy(send1[h].at[pair, side], recv1[h].at[me], r1_sem.at[h, me]).start()
    all_apart(lambda r, s: message1(1, r, s).start())

    for i in range(8):
        ttall[pl.ds(i * 128, 128), 0:OWN] = tbuf[:, i * 128 : (i + 1) * 128].T

    @pl.loop(0, SIDE)
    def _(c):
        one = ttall[pl.ds(c, SIDE, stride=SIDE), :]
        wanted = jnp.concatenate([one] * 4, axis=0).T
        for h in range(2):
            tperm[h, c] = wanted[h * PART : (h + 1) * PART]

    count = lengths[pair].astype(F32) * BANDS
    chunk = 16
    wide = lax.broadcasted_iota(jnp.int32, (chunk * PART, LOCAL), 1)

    def over_devices(h):
        @pl.loop(0, PART // 8)
        def _(i):
            at = pl.ds(pl.multiple_of(i * 8, 8), 8)
            spectrum = real_forward([recv1[h][p, at, :] for p in range(DEVICES)])
            for c in range(SIDE):
                j = (c + 1) % SIDE
                re, im = spectrum[min(j, SIDE - j)]
                cos, sin = turn[c : c + 1, :], turn[SIDE + c : SIDE + c + 1, :]
                if im is None:
                    mid[h, c, at, 0:LOCAL] = re * cos
                    mid[h, c, at, LOCAL:] = -re * sin
                else:
                    if j > SIDE // 2:
                        im = -im
                    mid[h, c, at, 0:LOCAL] = re * cos + im * sin
                    mid[h, c, at, LOCAL:] = im * cos - re * sin

    def in_device(h, scale):
        loss = jnp.zeros((8, LOCAL), F32)
        inner = jnp.zeros((8, LOCAL), F32)
        for i in range(SIDE // chunk):
            part = mid[h, i * chunk : (i + 1) * chunk].reshape(chunk * PART, HALF)
            z = times(three(part), bins[...]) * scale
            here, other = z[:, 0:LOCAL], z[:, LOCAL:]
            power = here * here + other * other
            above = 1.0 + power
            wanted = tperm[h, i * chunk : (i + 1) * chunk].reshape(chunk * PART, LOCAL)
            mismatch = jnp.log(above) - wanted
            factor = 2.0 * mismatch / above
            loss += jnp.sum((mismatch * mismatch).reshape(-1, 8, LOCAL), axis=0)
            inner += jnp.sum((factor * power).reshape(-1, 8, LOCAL), axis=0)
            grad = here * (factor * scale)
            high = grad.astype(BF16)
            first = jnp.where(wide < 2 * SIDE, high.astype(F32), grad - high.astype(F32))
            back = times(jnp.concatenate([first.astype(BF16), high], axis=1), to_time[...])
            mid[h, i * chunk : (i + 1) * chunk] = back.reshape(chunk, PART, HALF)
        return loss, inner

    def to_devices(h):
        @pl.loop(0, PART // 8)
        def _(i):
            at = pl.ds(pl.multiple_of(i * 8, 8), 8)

            def bin_of(j):
                c = (j - 1) % SIDE
                re, im = mid[h, c, at, 0:LOCAL], mid[h, c, at, LOCAL:]
                cos, sin = turn[c : c + 1, :], turn[SIDE + c : SIDE + c + 1, :]
                return re * cos - im * sin, re * sin + im * cos

            paired = [(bin_of(0)[0], None)]
            for j in range(1, SIDE // 2):
                (xr, xi), (yr, yi) = bin_of(j), bin_of(SIDE - j)
                paired.append((0.5 * (xr + yr), 0.5 * (xi - yi)))
            paired.append((bin_of(SIDE // 2)[0], None))
            for p, g in enumerate(real_backward(paired, SIDE)):
                send2[h][p, at, :] = g

    def back(h):
        all_apart(lambda r, s: message2(h, 2 * r + s).start())
        pltpu.make_async_copy(send2[h].at[me], recv2[h].at[me], r2_sem.at[h, me]).start()

    await_all(recv1a, r1_sem.at[0])
    over_devices(0)
    total = jnp.sum(recv1a[:, PART:SLOT, :], axis=0)
    loud = jnp.sum(total, axis=1, keepdims=True) / count + 1e-5
    scale = 1.0 / loud
    loss, inner = in_device(0, scale)
    to_devices(0)
    back(0)
    await_all(recv1b, r1_sem.at[1])
    over_devices(1)
    more_loss, more_inner = in_device(1, scale)
    loss, inner = loss + more_loss, inner + more_inner
    loss = 0.125 * jnp.sum(jnp.sum(loss, axis=0, keepdims=True), axis=1, keepdims=True)
    inner = 0.25 * jnp.sum(jnp.sum(inner, axis=0, keepdims=True), axis=1, keepdims=True)
    inner = inner / count * scale
    extra = jnp.where(lane == 0, loss, inner)
    send2b[:, PART:SLOT, :] = jnp.broadcast_to(extra[None], (DEVICES, 1, LOCAL))
    to_devices(1)
    back(1)

    row = lax.broadcasted_iota(jnp.int32, (LOCAL, HALF), 0)
    losses[...] = jnp.zeros((1, LOCAL), F32)
    over = pltpu.make_async_remote_copy(
        src_ref=obuf.at[:, pl.ds(rows, 16)],
        dst_ref=edge,
        send_sem=edge_sem.at[0],
        recv_sem=edge_sem.at[1],
        device_id={"tm": (me + 1) % DEVICES},
        device_id_type=MESH,
    )

    @pl.loop(0, RECORDS // 2)
    def _(i):
        both = [(pair + RECORDS // 2 - i) % RECORDS, (pair + RECORDS // 2 + 1 + i) % RECORDS]
        powers = []
        for r in both:
            for d in (2 * r, 2 * r + 1):
                for h in range(2):
                    pltpu.make_async_copy(recv2[h].at[d], recv2[h].at[d], r2_sem.at[h, d]).wait()
            extras = recv2b[2 * r, PART:SLOT, :] + recv2b[2 * r + 1, PART:SLOT, :]
            losses[...] = jnp.where(lane == r, extras[:, 0:1], losses[...])
            mean = extras[:, 1:2]
            grad = jnp.concatenate(
                [ref[2 * r + s, 0:PART, :] for s in range(2) for ref in recv2], axis=0
            )
            powers.append(three(slope[r] * (grad - mean), axis=0))
        grad = times(
            jnp.concatenate(powers, axis=1), bands_t[...], (((0,), (0,)), ((), ()))
        )
        grad = grad + grad

        pieces = []
        for h in range(2):
            z = jnp.concatenate([stft[r, LOCAL - 8 :, h * HALF : (h + 1) * HALF] for r in both], axis=0)
            g = jnp.concatenate(
                [grad[(e + 1) * LOCAL - 8 : (e + 1) * LOCAL, h * LOCAL : (h + 1) * LOCAL] for e in range(2)],
                axis=0,
            )
            z = z * jnp.concatenate([g, g], axis=1)
            pieces.append(times(three(z), backward[:, h * HALF : (h + 1) * HALF]))
        trailing = jnp.where(last, 0.0, (1.0 - win) * (pieces[0] - pieces[1]))
        for e, r in enumerate(both):
            for h in range(2):
                at = pl.ds(rows + 8 * h + r % 8, 1)
                obuf[r // 8, at, :] = trailing[8 * e + 7 : 8 * e + 8, h * LOCAL : (h + 1) * LOCAL]

        @pl.when(i == RECORDS // 2 - 1)
        def _():
            over.start()

        pieces = []
        for h in range(2):
            z = jnp.concatenate([stft[r, :, h * HALF : (h + 1) * HALF] for r in both], axis=0)
            g = grad[:, h * LOCAL : (h + 1) * LOCAL]
            z = z * jnp.concatenate([g, g], axis=1)
            pieces.append(times(three(z), backward[:, h * HALF : (h + 1) * HALF]))
        leading = win * (pieces[0] + pieces[1])
        trailing = (1.0 - win) * (pieces[0] - pieces[1])
        for e, r in enumerate(both):
            lead = leading[e * LOCAL : (e + 1) * LOCAL]
            trail = trailing[e * LOCAL : (e + 1) * LOCAL]
            moved = jnp.where(row == 0, 0.0, pltpu.roll(trail, 1, 0))
            full = lead + moved
            for h in range(2):
                start = (r % 8) + 8 * h
                cut = slice(h * LOCAL, (h + 1) * LOCAL)
                obuf[r // 8, pl.ds(start, LOCAL, stride=16), :] = full[:, cut]

    body = pltpu.make_async_copy(
        obuf.at[:, pl.ds(0, rows)], out, out_sem
    )
    body.start()

    @pl.loop(1, DEVICES)
    def _(j):
        d = (me + j) % DEVICES
        for h in range(2):
            one, two = send1[h].at[d // 2, d % 2], send2[h].at[d]
            pltpu.make_async_copy(one, one, s1_sem.at[h, d]).wait()
            pltpu.make_async_copy(two, two, s2_sem.at[h, d]).wait()

    over.wait()
    body.wait()


def hand_over(grad, edge, losses, out, loss, held, came, sem):
    step = LOCAL * 16 // 4
    places = [(i // 4, pl.ds((i % 4) * step, step)) for i in range(8)]
    loads = [
        pltpu.make_async_copy(grad.at[at], held.at[at], sem.at[0, i])
        for i, at in enumerate(places)
    ]
    stores = [
        pltpu.make_async_copy(held.at[at], out.at[at], sem.at[1, i])
        for i, at in enumerate(places)
    ]
    arrive = pltpu.make_async_copy(edge, came, sem.at[2, 0])
    arrive.start()
    for copy in loads:
        copy.start()
    for r in range(RECORDS):
        loss[r] = losses[0, r]
    arrive.wait()
    for i, (load, store) in enumerate(zip(loads, stores)):
        load.wait()
        if i % 4 == 0:
            held[i // 4, 0:16, :] = held[i // 4, 0:16, :] + came[i // 4]
        store.start()
    for copy in stores:
        copy.wait()


def body(wave, target_mod, lengths):
    rows = LOCAL * 16
    wave = wave.reshape(2, 8, LOCAL * 2, 128).transpose(0, 2, 1, 3).reshape(2, rows, 128)
    held = [jnp.asarray(t) for t in tables()]
    space = pl.BlockSpec(memory_space=pl.ANY)
    scratch = [pltpu.VMEM(t.shape, t.dtype) for t in held]
    scratch += [
        pltpu.VMEM((2, rows + 16, 128), F32),
        pltpu.VMEM((OWN, SIDE * SIDE), F32),
        pltpu.VMEM((SIDE * SIDE, 128), F32),
        pltpu.VMEM((2, SIDE, PART, 128), F32),
        pltpu.VMEM((RECORDS, LOCAL, FFT), F32),
        pltpu.VMEM((RECORDS, BANDS, LOCAL), F32),
        pltpu.VMEM((RECORDS, 2, SLOT, LOCAL), F32),
        pltpu.VMEM((RECORDS, 2, PART, LOCAL), F32),
        pltpu.VMEM((DEVICES, SLOT, LOCAL), F32),
        pltpu.VMEM((DEVICES, PART, LOCAL), F32),
        pltpu.VMEM((2, SIDE, PART, HALF), F32),
        pltpu.VMEM((DEVICES, PART, LOCAL), F32),
        pltpu.VMEM((DEVICES, SLOT, LOCAL), F32),
        pltpu.VMEM((DEVICES, PART, LOCAL), F32),
        pltpu.VMEM((DEVICES, SLOT, LOCAL), F32),
        pltpu.VMEM((2, rows + 16, 128), F32),
        pltpu.SemaphoreType.DMA((2,)),
        pltpu.SemaphoreType.DMA((len(held),)),
        pltpu.SemaphoreType.DMA,
        pltpu.SemaphoreType.DMA((2,)),
        pltpu.SemaphoreType.DMA((2, DEVICES)),
        pltpu.SemaphoreType.DMA((2, DEVICES)),
        pltpu.SemaphoreType.DMA((2, DEVICES)),
        pltpu.SemaphoreType.DMA((2, DEVICES)),
        pltpu.SemaphoreType.DMA((2,)),
        pltpu.SemaphoreType.DMA,
    ]
    grad, edge, losses = pl.pallas_call(
        kernel,
        out_shape=(
            jax.ShapeDtypeStruct((2, rows, 128), F32),
            jax.ShapeDtypeStruct((2, 16, 128), F32),
            jax.ShapeDtypeStruct((1, LOCAL), F32),
        ),
        in_specs=[space, space, pl.BlockSpec(memory_space=pltpu.SMEM)] + [space] * len(held),
        out_specs=(space, space, pl.BlockSpec(memory_space=pltpu.VMEM)),
        scratch_shapes=scratch,
        compiler_params=pltpu.CompilerParams(
            collective_id=0, has_side_effects=True, vmem_limit_bytes=62 * 1024 * 1024
        ),
    )(wave, target_mod, lengths, *held)
    grad, loss = pl.pallas_call(
        hand_over,
        out_shape=(
            jax.ShapeDtypeStruct((2, rows, 128), F32),
            jax.ShapeDtypeStruct((RECORDS,), F32),
        ),
        in_specs=[space, space, pl.BlockSpec(memory_space=pltpu.SMEM)],
        out_specs=(space, pl.BlockSpec(memory_space=pltpu.SMEM)),
        scratch_shapes=[
            pltpu.VMEM((2, rows, 128), F32),
            pltpu.VMEM((2, 16, 128), F32),
            pltpu.SemaphoreType.DMA((3, 8)),
        ],
        compiler_params=pltpu.CompilerParams(vmem_limit_bytes=62 * 1024 * 1024),
    )(grad, edge, losses)
    grad = grad.reshape(2, LOCAL * 2, 8, 128).transpose(0, 2, 1, 3).reshape(RECORDS, LOCAL * HALF)
    return grad, loss


def solution(mesh):
    in_specs = (P("rec", "tm"), P(("rec", "tm"), None), P("rec"))
    out_specs = (P("rec", "tm"), P("rec"))
    return jax.shard_map(body, mesh=mesh, in_specs=in_specs, out_specs=out_specs, check_vma=False)
```

```python
import functools
import math

import jax
import jax.numpy as jnp
import ml_dtypes
import numpy as np
from jax import lax
from jax.experimental import pallas as pl
from jax.experimental.pallas import tpu as pltpu
from jax.sharding import PartitionSpec as P

FFT = 512
HALF = FFT // 2
BANDS = 96
OWN = BANDS // 2
RECORDS = 16
DEVICES = 32
LOCAL = 128
FRAMES = LOCAL * DEVICES
SIDE = 32
PART = OWN // 2
SLOT = PART + 1
RATE = 16000.0
F32 = jnp.float32
BF16 = jnp.bfloat16
MESH = pl.DeviceIdType.MESH


def a_weight(freq):
    square = freq * freq
    upper = 12194.0**2 * square * square
    lower = (
        (square + 20.6**2)
        * np.sqrt((square + 107.7**2) * (square + 737.9**2))
        * (square + 12194.0**2)
    )
    return upper / lower


def bark_scale(freq):
    return 13.0 * np.arctan(0.00076 * freq) + 3.5 * np.arctan((freq / 7500.0) ** 2)


def band_table():
    freq = np.arange(HALF) * (RATE / FFT)
    top = bark_scale(np.float64(RATE / 2.0))
    centres = (np.arange(BANDS) + 0.5) * (top / BANDS)
    spread = max(0.5, 2.0 * top / BANDS)
    shape = np.maximum(0.0, 1.0 - np.abs(bark_scale(freq)[:, None] - centres[None, :]) / spread)
    weight = 0.1 + a_weight(freq) / a_weight(np.float64(1000.0))
    return shape * weight[:, None] / np.maximum(shape.sum(axis=0), 1.0)[None, :]


def two(table):
    high = table.astype(np.float32).astype(ml_dtypes.bfloat16)
    low = (table - high.astype(np.float64)).astype(np.float32).astype(ml_dtypes.bfloat16)
    return high, low


def against(table, axis):
    high, low = two(table)
    return np.concatenate([high, high, low], axis=axis)


def cycle(index, length):
    angle = (index % length) * (2.0 * math.pi / length)
    return np.cos(angle), np.sin(angle)


@functools.cache
def tables():
    n, m = np.arange(HALF)[:, None], np.arange(HALF // 2)[None, :]
    halves = []
    for odd in (0, 1):
        cos, sin = cycle(n * (2 * m + odd), FFT)
        halves.append(np.concatenate([cos, -sin], axis=1) / math.sqrt(FFT))
    forward = np.concatenate([against(h, 0) for h in halves], axis=1)
    backward = np.concatenate([against(h.T, 0) for h in halves], axis=1)
    bands = band_table()
    bands = np.concatenate([bands[0::2], bands[1::2]], axis=0).T
    tau, a = np.arange(LOCAL)[:, None], np.arange(SIDE)[None, :]
    cos, sin = cycle(tau * a, LOCAL)
    cos, sin = cos / math.sqrt(FRAMES), sin / math.sqrt(FRAMES)
    re = np.concatenate([cos, sin], axis=0)
    im = np.concatenate([-sin, cos], axis=0)
    to_bins = np.concatenate([re, im, re, im, im, re, im, re], axis=1)
    high, low = two(np.concatenate([re.T, im.T], axis=0))
    to_time = np.concatenate([high, high, low, np.zeros_like(low)], axis=0)
    cos, sin = cycle((np.arange(SIDE)[:, None] + 1) * np.arange(LOCAL)[None, :], FRAMES)
    turn = np.concatenate([cos, sin], axis=0).astype(np.float32)
    window = 0.5 - 0.5 * np.cos(np.arange(HALF) * (2.0 * math.pi / FFT))
    window = np.broadcast_to(window.astype(np.float32), (8, HALF))
    return (
        forward,
        against(bands, 1),
        against(bands, 0),
        backward,
        against(to_bins, 0),
        to_time,
        turn,
        np.ascontiguousarray(window),
    )


def three(x, axis=-1):
    high = x.astype(BF16)
    low = (x - high.astype(F32)).astype(BF16)
    return jnp.concatenate([high, low, high], axis=axis)


def times(a, b, dims=(((1,), (0,)), ((), ()))):
    return lax.dot_general(a, b, dims, preferred_element_type=F32)


def turned(z, k, n):
    re, im = z
    k = k % n
    if im is None:
        im = jnp.zeros_like(re)
    if k == 0:
        return re, im
    if 4 * k == n:
        return im, -re
    if 2 * k == n:
        return -re, -im
    if 4 * k == 3 * n:
        return -im, re
    c, s = math.cos(2 * math.pi * k / n), math.sin(2 * math.pi * k / n)
    if 8 * k == n:
        return c * (re + im), c * (im - re)
    return c * re + s * im, c * im - s * re


def real_forward(x):
    n = len(x)
    if n == 1:
        return [(x[0], None)]
    if n == 2:
        return [(x[0] + x[1], None), (x[0] - x[1], None)]
    even, odd = real_forward(x[0::2]), real_forward(x[1::2])
    out = [None] * (n // 2 + 1)
    out[0] = (even[0][0] + odd[0][0], None)
    out[n // 2] = (even[0][0] - odd[0][0], None)
    quarter = n // 4
    out[quarter] = (even[quarter][0], -odd[quarter][0])
    for k in range(1, quarter):
        tr, ti = turned(odd[k], k, n)
        er, ei = even[k]
        out[k] = (er + tr, ei + ti)
        out[n // 2 - k] = (er - tr, ti - ei)
    return out


def real_backward(q, n):
    if n == 1:
        return [q[0][0]]
    if n == 2:
        return [q[0][0] + q[1][0], q[0][0] - q[1][0]]
    half, quarter = n // 2, n // 4
    a, b = [], []
    for j in range(quarter + 1):
        (xr, xi), (yr, yi) = q[j], q[half - j]
        if j == 0:
            a.append((xr + yr, None))
            b.append((xr - yr, None))
        elif j == quarter:
            a.append((xr + xr, None))
            b.append((-(xi + xi), None))
        else:
            a.append((xr + yr, xi - yi))
            dr, di = xr - yr, xi + yi
            b.append(turned((dr, di), n - j, n))
    even, odd = real_backward(a, half), real_backward(b, half)
    out = [None] * n
    out[0::2], out[1::2] = even, odd
    return out


def kernel(
    wave,
    target,
    lengths,
    h_forward,
    h_bands,
    h_bands_t,
    h_backward,
    h_bins,
    h_time,
    h_turn,
    h_window,
    out,
    edge,
    losses,
    forward,
    bands,
    bands_t,
    backward,
    bins,
    to_time,
    turn,
    window,
    wbuf,
    tbuf,
    ttall,
    tperm,
    stft,
    slope,
    send1a,
    send1b,
    recv1a,
    recv1b,
    mid,
    send2a,
    send2b,
    recv2a,
    recv2b,
    obuf,
    wave_sem,
    table_sem,
    target_sem,
    halo_sem,
    s1_sem,
    r1_sem,
    s2_sem,
    r2_sem,
    edge_sem,
    out_sem,
):
    me = lax.axis_index("tm")
    pair = me // 2
    side = me % 2

    barrier = pltpu.get_barrier_semaphore()

    @pl.loop(1, DEVICES)
    def _(j):
        pl.semaphore_signal(
            barrier,
            inc=1,
            device_id={"tm": (me + j) % DEVICES},
            device_id_type=MESH,
        )

    rows = LOCAL * 16
    loads = [
        pltpu.make_async_copy(wave.at[g], wbuf.at[g, pl.ds(0, rows)], wave_sem.at[g])
        for g in range(2)
    ]
    held = [
        pltpu.make_async_copy(src, dst, table_sem.at[i])
        for i, (src, dst) in enumerate(
            (
                (h_forward, forward),
                (h_bands, bands),
                (h_window, window),
                (h_turn, turn),
                (h_bins, bins),
                (h_time, to_time),
                (h_bands_t, bands_t),
                (h_backward, backward),
            )
        )
    ]
    load_target = pltpu.make_async_copy(target, tbuf, target_sem)
    for copy in held[:3] + loads + held[3:] + [load_target]:
        copy.start()

    pl.semaphore_wait(barrier, DEVICES - 1)
    halo = pltpu.make_async_remote_copy(
        src_ref=wave.at[:, pl.ds(0, 16)],
        dst_ref=wbuf.at[:, pl.ds(rows, 16)],
        send_sem=halo_sem.at[0],
        recv_sem=halo_sem.at[1],
        device_id={"tm": (me + DEVICES - 1) % DEVICES},
        device_id_type=MESH,
    )
    halo.start()
    for copy in held + loads + [load_target]:
        copy.wait()
    halo.wait()
    last = me == DEVICES - 1
    wbuf[:, pl.ds(rows, 16), :] = jnp.where(last, 0.0, wbuf[:, pl.ds(rows, 16), :])

    lane = lax.broadcasted_iota(jnp.int32, (1, LOCAL), 1)

    def hops(r, later):
        start = (r % 8) + later * 16
        return jnp.concatenate(
            [wbuf[r // 8, pl.ds(start + 8 * h, LOCAL, stride=16), :] for h in range(2)], axis=1
        )

    send1, recv1 = (send1a, send1b), (recv1a, recv1b)
    send2, recv2 = (send2a, send2b), (recv2a, recv2b)

    def message1(h, r, s):
        d = 2 * r + s
        return pltpu.make_async_remote_copy(
            src_ref=send1[h].at[r, s],
            dst_ref=recv1[h].at[me],
            send_sem=s1_sem.at[h, d],
            recv_sem=r1_sem.at[h, me],
            device_id={"tm": d},
            device_id_type=MESH,
        )

    def message2(h, d):
        return pltpu.make_async_remote_copy(
            src_ref=send2[h].at[d],
            dst_ref=recv2[h].at[me],
            send_sem=s2_sem.at[h, d],
            recv_sem=r2_sem.at[h, me],
            device_id={"tm": d},
            device_id_type=MESH,
        )

    def apart(i):
        return (pair + i + RECORDS // 2) % RECORDS, (pair + RECORDS // 2 - 1 - i) % RECORDS

    def all_apart(send):
        @pl.loop(0, RECORDS // 2)
        def _(i):
            both = apart(i)
            for s in range(2):
                send(both[0], s)

            @pl.when(i < RECORDS // 2 - 1)
            def _():
                for s in range(2):
                    send(both[1], s)

        send(pair, 1 - side)

    def await_all(ref, sem):
        @pl.loop(0, DEVICES)
        def _(j):
            pltpu.make_async_copy(ref.at[j], ref.at[j], sem.at[j]).wait()

    win = window[0:1, :]

    @pl.loop(0, RECORDS // 2)
    def _(i):
        both = apart(i)
        now = jnp.concatenate([hops(r, 0) for r in both], axis=0)
        later = jnp.concatenate([hops(r, 1) for r in both], axis=0)
        added = later + win * (now - later)
        taken = win * (now + later) - later
        even = times(three(added), forward[:, 0:HALF])
        odd = times(three(taken), forward[:, HALF:FFT])
        power = [z[:, 0:LOCAL] * z[:, 0:LOCAL] + z[:, LOCAL:] * z[:, LOCAL:] for z in (even, odd)]
        power = three(jnp.concatenate(power, axis=1))
        energy = times(bands[...], power, (((1,), (1,)), ((), ())))
        for e, r in enumerate(both):
            stft[r, :, 0:HALF] = even[e * LOCAL : (e + 1) * LOCAL]
            stft[r, :, HALF:FFT] = odd[e * LOCAL : (e + 1) * LOCAL]
            lifted = energy[:, e * LOCAL : (e + 1) * LOCAL] + 0.05
            valid = (me * LOCAL + lane < lengths[r]).astype(F32)
            masked = jnp.exp(0.3 * jnp.log(lifted)) * valid
            slope[r] = 0.3 * masked / lifted
            total = jnp.sum(masked, axis=0, keepdims=True)
            for s in range(2):
                send1a[r, s, 0:PART, :] = masked[s * OWN : s * OWN + PART]
                send1a[r, s, PART:SLOT, :] = total
                send1b[r, s] = masked[s * OWN + PART : (s + 1) * OWN]

        for s in range(2):
            message1(0, both[0], s).start()

        @pl.when(i < RECORDS // 2 - 1)
        def _():
            for s in range(2):
                message1(0, both[1], s).start()

    message1(0, pair, 1 - side).start()
    for h in range(2):
        pltpu.make_async_copy(send1[h].at[pair, side], recv1[h].at[me], r1_sem.at[h, me]).start()
    all_apart(lambda r, s: message1(1, r, s).start())

    for i in range(8):
        ttall[pl.ds(i * 128, 128), 0:OWN] = tbuf[:, i * 128 : (i + 1) * 128].T

    @pl.loop(0, SIDE)
    def _(c):
        one = ttall[pl.ds(c, SIDE, stride=SIDE), :]
        wanted = jnp.concatenate([one] * 4, axis=0).T
        for h in range(2):
            tperm[h, c] = wanted[h * PART : (h + 1) * PART]

    count = lengths[pair].astype(F32) * BANDS
    chunk = 16
    wide = lax.broadcasted_iota(jnp.int32, (chunk * PART, LOCAL), 1)

    def over_devices(h):
        @pl.loop(0, PART // 8)
        def _(i):
            at = pl.ds(pl.multiple_of(i * 8, 8), 8)
            spectrum = real_forward([recv1[h][p, at, :] for p in range(DEVICES)])
            for c in range(SIDE):
                j = (c + 1) % SIDE
                re, im = spectrum[min(j, SIDE - j)]
                cos, sin = turn[c : c + 1, :], turn[SIDE + c : SIDE + c + 1, :]
                if im is None:
                    mid[h, c, at, 0:LOCAL] = re * cos
                    mid[h, c, at, LOCAL:] = -re * sin
                else:
                    if j > SIDE // 2:
                        im = -im
                    mid[h, c, at, 0:LOCAL] = re * cos + im * sin
                    mid[h, c, at, LOCAL:] = im * cos - re * sin

    def in_device(h, scale):
        loss = jnp.zeros((8, LOCAL), F32)
        inner = jnp.zeros((8, LOCAL), F32)
        for i in range(SIDE // chunk):
            part = mid[h, i * chunk : (i + 1) * chunk].reshape(chunk * PART, HALF)
            z = times(three(part), bins[...]) * scale
            here, other = z[:, 0:LOCAL], z[:, LOCAL:]
            power = here * here + other * other
            above = 1.0 + power
            wanted = tperm[h, i * chunk : (i + 1) * chunk].reshape(chunk * PART, LOCAL)
            mismatch = jnp.log(above) - wanted
            factor = 2.0 * mismatch / above
            loss += jnp.sum((mismatch * mismatch).reshape(-1, 8, LOCAL), axis=0)
            inner += jnp.sum((factor * power).reshape(-1, 8, LOCAL), axis=0)
            grad = here * (factor * scale)
            high = grad.astype(BF16)
            first = jnp.where(wide < 2 * SIDE, high.astype(F32), grad - high.astype(F32))
            back = times(jnp.concatenate([first.astype(BF16), high], axis=1), to_time[...])
            mid[h, i * chunk : (i + 1) * chunk] = back.reshape(chunk, PART, HALF)
        return loss, inner

    def to_devices(h):
        @pl.loop(0, PART // 8)
        def _(i):
            at = pl.ds(pl.multiple_of(i * 8, 8), 8)

            def bin_of(j):
                c = (j - 1) % SIDE
                re, im = mid[h, c, at, 0:LOCAL], mid[h, c, at, LOCAL:]
                cos, sin = turn[c : c + 1, :], turn[SIDE + c : SIDE + c + 1, :]
                return re * cos - im * sin, re * sin + im * cos

            paired = [(bin_of(0)[0], None)]
            for j in range(1, SIDE // 2):
                (xr, xi), (yr, yi) = bin_of(j), bin_of(SIDE - j)
                paired.append((0.5 * (xr + yr), 0.5 * (xi - yi)))
            paired.append((bin_of(SIDE // 2)[0], None))
            for p, g in enumerate(real_backward(paired, SIDE)):
                send2[h][p, at, :] = g

    def back(h):
        all_apart(lambda r, s: message2(h, 2 * r + s).start())
        pltpu.make_async_copy(send2[h].at[me], recv2[h].at[me], r2_sem.at[h, me]).start()

    await_all(recv1a, r1_sem.at[0])
    over_devices(0)
    total = jnp.sum(recv1a[:, PART:SLOT, :], axis=0)
    loud = jnp.sum(total, axis=1, keepdims=True) / count + 1e-5
    scale = 1.0 / loud
    loss, inner = in_device(0, scale)
    to_devices(0)
    back(0)
    await_all(recv1b, r1_sem.at[1])
    over_devices(1)
    more_loss, more_inner = in_device(1, scale)
    loss, inner = loss + more_loss, inner + more_inner
    loss = 0.125 * jnp.sum(jnp.sum(loss, axis=0, keepdims=True), axis=1, keepdims=True)
    inner = 0.25 * jnp.sum(jnp.sum(inner, axis=0, keepdims=True), axis=1, keepdims=True)
    inner = inner / count * scale
    extra = jnp.where(lane == 0, loss, inner)
    send2b[:, PART:SLOT, :] = jnp.broadcast_to(extra[None], (DEVICES, 1, LOCAL))
    to_devices(1)
    back(1)

    row = lax.broadcasted_iota(jnp.int32, (LOCAL, HALF), 0)
    losses[...] = jnp.zeros((1, LOCAL), F32)
    over = pltpu.make_async_remote_copy(
        src_ref=obuf.at[:, pl.ds(rows, 16)],
        dst_ref=edge,
        send_sem=edge_sem.at[0],
        recv_sem=edge_sem.at[1],
        device_id={"tm": (me + 1) % DEVICES},
        device_id_type=MESH,
    )

    def await_back(both):
        for r in both:
            for d in (2 * r, 2 * r + 1):
                for h in range(2):
                    pltpu.make_async_copy(recv2[h].at[d], recv2[h].at[d], r2_sem.at[h, d]).wait()

    def grad_power(both):
        powers = []
        for r in both:
            extras = recv2b[2 * r, PART:SLOT, :] + recv2b[2 * r + 1, PART:SLOT, :]
            losses[...] = jnp.where(lane == r, extras[:, 0:1], losses[...])
            mean = extras[:, 1:2]
            grad = jnp.concatenate(
                [ref[2 * r + s, 0:PART, :] for s in range(2) for ref in recv2], axis=0
            )
            powers.append(three(slope[r] * (grad - mean), axis=0))
        grad = times(jnp.concatenate(powers, axis=1), bands_t[...], (((0,), (0,)), ((), ())))
        return grad + grad

    def to_frames(both, grad, first):
        pieces = []
        for h in range(2):
            z, g = [], []
            for e, r in enumerate(both):
                z.append(stft[r, first:, h * HALF : (h + 1) * HALF])
                g.append(grad[e * LOCAL + first : (e + 1) * LOCAL, h * LOCAL : (h + 1) * LOCAL])
            z, g = jnp.concatenate(z, axis=0), jnp.concatenate(g, axis=0)
            z = z * jnp.concatenate([g, g], axis=1)
            pieces.append(times(three(z), backward[:, h * HALF : (h + 1) * HALF]))
        return pieces

    def store_edge(r, trail):
        trail = jnp.where(last, 0.0, trail)
        for h in range(2):
            at = pl.ds(rows + 8 * h + r % 8, 1)
            obuf[r // 8, at, :] = trail[:, h * LOCAL : (h + 1) * LOCAL]

    def back_to_wave(both, grad, edges):
        plus, minus = to_frames(both, grad, 0)
        leading = win * (plus + minus)
        trailing = (1.0 - win) * (plus - minus)
        for e, r in enumerate(both):
            trail = trailing[e * LOCAL : (e + 1) * LOCAL]
            moved = jnp.where(row == 0, 0.0, pltpu.roll(trail, 1, 0))
            full = leading[e * LOCAL : (e + 1) * LOCAL] + moved
            for h in range(2):
                at = pl.ds((r % 8) + 8 * h, LOCAL, stride=16)
                obuf[r // 8, at, :] = full[:, h * LOCAL : (h + 1) * LOCAL]
            if edges:
                store_edge(r, trail[LOCAL - 1 :])

    def four(i):
        return [
            [(pair + RECORDS // 2 - n) % RECORDS, (pair + RECORDS // 2 + 1 + n) % RECORDS]
            for n in (2 * i, 2 * i + 1)
        ]

    @pl.loop(0, RECORDS // 4 - 1)
    def _(i):
        for both in four(i):
            await_back(both)
        for both in four(i):
            back_to_wave(both, grad_power(both), True)

    final = four(RECORDS // 4 - 1)
    for both in final:
        await_back(both)
    grads = [grad_power(both) for both in final]
    for both, grad in zip(final, grads):
        plus, minus = to_frames(both, grad, LOCAL - 8)
        trailing = (1.0 - win) * (plus - minus)
        for e, r in enumerate(both):
            store_edge(r, trailing[8 * e + 7 : 8 * e + 8])
    over.start()
    for both, grad in zip(final, grads):
        back_to_wave(both, grad, False)

    body = pltpu.make_async_copy(
        obuf.at[:, pl.ds(0, rows)], out, out_sem
    )
    body.start()

    @pl.loop(1, DEVICES)
    def _(j):
        d = (me + j) % DEVICES
        for h in range(2):
            one, two = send1[h].at[d // 2, d % 2], send2[h].at[d]
            pltpu.make_async_copy(one, one, s1_sem.at[h, d]).wait()
            pltpu.make_async_copy(two, two, s2_sem.at[h, d]).wait()

    over.wait()
    body.wait()


def hand_over(grad, edge, losses, out, loss, held, came, sem):
    step = LOCAL * 16 // 4
    places = [(i // 4, pl.ds((i % 4) * step, step)) for i in range(8)]
    loads = [
        pltpu.make_async_copy(grad.at[at], held.at[at], sem.at[0, i])
        for i, at in enumerate(places)
    ]
    stores = [
        pltpu.make_async_copy(held.at[at], out.at[at], sem.at[1, i])
        for i, at in enumerate(places)
    ]
    arrive = pltpu.make_async_copy(edge, came, sem.at[2, 0])
    arrive.start()
    for copy in loads:
        copy.start()
    for r in range(RECORDS):
        loss[r] = losses[0, r]
    arrive.wait()
    for i, (load, store) in enumerate(zip(loads, stores)):
        load.wait()
        if i % 4 == 0:
            held[i // 4, 0:16, :] = held[i // 4, 0:16, :] + came[i // 4]
        store.start()
    for copy in stores:
        copy.wait()


def body(wave, target_mod, lengths):
    rows = LOCAL * 16
    wave = wave.reshape(2, 8, LOCAL * 2, 128).transpose(0, 2, 1, 3).reshape(2, rows, 128)
    held = [jnp.asarray(t) for t in tables()]
    space = pl.BlockSpec(memory_space=pl.ANY)
    scratch = [pltpu.VMEM(t.shape, t.dtype) for t in held]
    scratch += [
        pltpu.VMEM((2, rows + 16, 128), F32),
        pltpu.VMEM((OWN, SIDE * SIDE), F32),
        pltpu.VMEM((SIDE * SIDE, 128), F32),
        pltpu.VMEM((2, SIDE, PART, 128), F32),
        pltpu.VMEM((RECORDS, LOCAL, FFT), F32),
        pltpu.VMEM((RECORDS, BANDS, LOCAL), F32),
        pltpu.VMEM((RECORDS, 2, SLOT, LOCAL), F32),
        pltpu.VMEM((RECORDS, 2, PART, LOCAL), F32),
        pltpu.VMEM((DEVICES, SLOT, LOCAL), F32),
        pltpu.VMEM((DEVICES, PART, LOCAL), F32),
        pltpu.VMEM((2, SIDE, PART, HALF), F32),
        pltpu.VMEM((DEVICES, PART, LOCAL), F32),
        pltpu.VMEM((DEVICES, SLOT, LOCAL), F32),
        pltpu.VMEM((DEVICES, PART, LOCAL), F32),
        pltpu.VMEM((DEVICES, SLOT, LOCAL), F32),
        pltpu.VMEM((2, rows + 16, 128), F32),
        pltpu.SemaphoreType.DMA((2,)),
        pltpu.SemaphoreType.DMA((len(held),)),
        pltpu.SemaphoreType.DMA,
        pltpu.SemaphoreType.DMA((2,)),
        pltpu.SemaphoreType.DMA((2, DEVICES)),
        pltpu.SemaphoreType.DMA((2, DEVICES)),
        pltpu.SemaphoreType.DMA((2, DEVICES)),
        pltpu.SemaphoreType.DMA((2, DEVICES)),
        pltpu.SemaphoreType.DMA((2,)),
        pltpu.SemaphoreType.DMA,
    ]
    grad, edge, losses = pl.pallas_call(
        kernel,
        out_shape=(
            jax.ShapeDtypeStruct((2, rows, 128), F32),
            jax.ShapeDtypeStruct((2, 16, 128), F32),
            jax.ShapeDtypeStruct((1, LOCAL), F32),
        ),
        in_specs=[space, space, pl.BlockSpec(memory_space=pltpu.SMEM)] + [space] * len(held),
        out_specs=(space, space, pl.BlockSpec(memory_space=pltpu.VMEM)),
        scratch_shapes=scratch,
        compiler_params=pltpu.CompilerParams(
            collective_id=0, has_side_effects=True, vmem_limit_bytes=62 * 1024 * 1024
        ),
    )(wave, target_mod, lengths, *held)
    grad, loss = pl.pallas_call(
        hand_over,
        out_shape=(
            jax.ShapeDtypeStruct((2, rows, 128), F32),
            jax.ShapeDtypeStruct((RECORDS,), F32),
        ),
        in_specs=[space, space, pl.BlockSpec(memory_space=pltpu.SMEM)],
        out_specs=(space, pl.BlockSpec(memory_space=pltpu.SMEM)),
        scratch_shapes=[
            pltpu.VMEM((2, rows, 128), F32),
            pltpu.VMEM((2, 16, 128), F32),
            pltpu.SemaphoreType.DMA((3, 8)),
        ],
        compiler_params=pltpu.CompilerParams(vmem_limit_bytes=62 * 1024 * 1024),
    )(grad, edge, losses)
    grad = grad.reshape(2, LOCAL * 2, 8, 128).transpose(0, 2, 1, 3).reshape(RECORDS, LOCAL * HALF)
    return grad, loss


def solution(mesh):
    in_specs = (P("rec", "tm"), P(("rec", "tm"), None), P("rec"))
    out_specs = (P("rec", "tm"), P("rec"))
    return jax.shard_map(body, mesh=mesh, in_specs=in_specs, out_specs=out_specs, check_vma=False)
```

```python
import functools
import math

import jax
import jax.numpy as jnp
import ml_dtypes
import numpy as np
from jax import lax
from jax.experimental import pallas as pl
from jax.experimental.pallas import tpu as pltpu
from jax.sharding import PartitionSpec as P

FFT = 512
HALF = FFT // 2
BANDS = 96
OWN = BANDS // 2
RECORDS = 16
DEVICES = 32
LOCAL = 128
FRAMES = LOCAL * DEVICES
SIDE = 32
PART = OWN // 2
SLOT = PART + 1
RATE = 16000.0
F32 = jnp.float32
BF16 = jnp.bfloat16
MESH = pl.DeviceIdType.MESH


def a_weight(freq):
    square = freq * freq
    upper = 12194.0**2 * square * square
    lower = (
        (square + 20.6**2)
        * np.sqrt((square + 107.7**2) * (square + 737.9**2))
        * (square + 12194.0**2)
    )
    return upper / lower


def bark_scale(freq):
    return 13.0 * np.arctan(0.00076 * freq) + 3.5 * np.arctan((freq / 7500.0) ** 2)


def band_table():
    freq = np.arange(HALF) * (RATE / FFT)
    top = bark_scale(np.float64(RATE / 2.0))
    centres = (np.arange(BANDS) + 0.5) * (top / BANDS)
    spread = max(0.5, 2.0 * top / BANDS)
    shape = np.maximum(0.0, 1.0 - np.abs(bark_scale(freq)[:, None] - centres[None, :]) / spread)
    weight = 0.1 + a_weight(freq) / a_weight(np.float64(1000.0))
    return shape * weight[:, None] / np.maximum(shape.sum(axis=0), 1.0)[None, :]


def two(table):
    high = table.astype(np.float32).astype(ml_dtypes.bfloat16)
    low = (table - high.astype(np.float64)).astype(np.float32).astype(ml_dtypes.bfloat16)
    return high, low


def against(table, axis):
    high, low = two(table)
    return np.concatenate([high, high, low], axis=axis)


def cycle(index, length):
    angle = (index % length) * (2.0 * math.pi / length)
    return np.cos(angle), np.sin(angle)


@functools.cache
def tables():
    n, m = np.arange(HALF)[:, None], np.arange(HALF // 2)[None, :]
    halves = []
    for odd in (0, 1):
        cos, sin = cycle(n * (2 * m + odd), FFT)
        halves.append(np.concatenate([cos, -sin], axis=1) / math.sqrt(FFT))
    forward = np.concatenate([against(h, 0) for h in halves], axis=1)
    backward = np.concatenate([against(h.T, 0) for h in halves], axis=1)
    bands = band_table()
    bands = np.concatenate([bands[0::2], bands[1::2]], axis=0).T
    tau, a = np.arange(LOCAL)[:, None], np.arange(SIDE)[None, :]
    cos, sin = cycle(tau * a, LOCAL)
    cos, sin = cos / math.sqrt(FRAMES), sin / math.sqrt(FRAMES)
    re = np.concatenate([cos, sin], axis=0)
    im = np.concatenate([-sin, cos], axis=0)
    to_bins = np.concatenate([re, im, re, im, im, re, im, re], axis=1)
    high, low = two(np.concatenate([re.T, im.T], axis=0))
    to_time = np.concatenate([high, high, low, np.zeros_like(low)], axis=0)
    cos, sin = cycle((np.arange(SIDE)[:, None] + 1) * np.arange(LOCAL)[None, :], FRAMES)
    turn = np.concatenate([cos, sin], axis=0).astype(np.float32)
    window = 0.5 - 0.5 * np.cos(np.arange(HALF) * (2.0 * math.pi / FFT))
    window = np.broadcast_to(window.astype(np.float32), (8, HALF))
    return (
        forward,
        against(bands, 1),
        against(bands, 0),
        backward,
        against(to_bins, 0),
        to_time,
        turn,
        np.ascontiguousarray(window),
    )


def three(x, axis=-1):
    high = x.astype(BF16)
    low = (x - high.astype(F32)).astype(BF16)
    return jnp.concatenate([high, low, high], axis=axis)


def times(a, b, dims=(((1,), (0,)), ((), ()))):
    return lax.dot_general(a, b, dims, preferred_element_type=F32)


def turned(z, k, n):
    re, im = z
    k = k % n
    if im is None:
        im = jnp.zeros_like(re)
    if k == 0:
        return re, im
    if 4 * k == n:
        return im, -re
    if 2 * k == n:
        return -re, -im
    if 4 * k == 3 * n:
        return -im, re
    c, s = math.cos(2 * math.pi * k / n), math.sin(2 * math.pi * k / n)
    if 8 * k == n:
        return c * (re + im), c * (im - re)
    return c * re + s * im, c * im - s * re


def real_forward(x):
    n = len(x)
    if n == 1:
        return [(x[0], None)]
    if n == 2:
        return [(x[0] + x[1], None), (x[0] - x[1], None)]
    even, odd = real_forward(x[0::2]), real_forward(x[1::2])
    out = [None] * (n // 2 + 1)
    out[0] = (even[0][0] + odd[0][0], None)
    out[n // 2] = (even[0][0] - odd[0][0], None)
    quarter = n // 4
    out[quarter] = (even[quarter][0], -odd[quarter][0])
    for k in range(1, quarter):
        tr, ti = turned(odd[k], k, n)
        er, ei = even[k]
        out[k] = (er + tr, ei + ti)
        out[n // 2 - k] = (er - tr, ti - ei)
    return out


def real_backward(q, n):
    if n == 1:
        return [q[0][0]]
    if n == 2:
        return [q[0][0] + q[1][0], q[0][0] - q[1][0]]
    half, quarter = n // 2, n // 4
    a, b = [], []
    for j in range(quarter + 1):
        (xr, xi), (yr, yi) = q[j], q[half - j]
        if j == 0:
            a.append((xr + yr, None))
            b.append((xr - yr, None))
        elif j == quarter:
            a.append((xr + xr, None))
            b.append((-(xi + xi), None))
        else:
            a.append((xr + yr, xi - yi))
            dr, di = xr - yr, xi + yi
            b.append(turned((dr, di), n - j, n))
    even, odd = real_backward(a, half), real_backward(b, half)
    out = [None] * n
    out[0::2], out[1::2] = even, odd
    return out


def kernel(
    wave,
    target,
    lengths,
    h_forward,
    h_bands,
    h_bands_t,
    h_backward,
    h_bins,
    h_time,
    h_turn,
    h_window,
    out,
    losses,
    forward,
    bands,
    bands_t,
    backward,
    bins,
    to_time,
    turn,
    window,
    wbuf,
    tbuf,
    ttall,
    tperm,
    stft,
    slope,
    send1a,
    send1b,
    recv1a,
    recv1b,
    mid,
    send2a,
    send2b,
    recv2a,
    recv2b,
    leave,
    edge,
    wave_sem,
    table_sem,
    target_sem,
    halo_sem,
    s1_sem,
    r1_sem,
    s2_sem,
    r2_sem,
    edge_sem,
):
    me = lax.axis_index("tm")
    pair = me // 2
    side = me % 2

    barrier = pltpu.get_barrier_semaphore()

    @pl.loop(1, DEVICES)
    def _(j):
        pl.semaphore_signal(
            barrier,
            inc=1,
            device_id={"tm": (me + j) % DEVICES},
            device_id_type=MESH,
        )

    rows = LOCAL * 16
    loads = [
        pltpu.make_async_copy(wave.at[g], wbuf.at[g, pl.ds(0, rows)], wave_sem.at[g])
        for g in range(2)
    ]
    held = [
        pltpu.make_async_copy(src, dst, table_sem.at[i])
        for i, (src, dst) in enumerate(
            (
                (h_forward, forward),
                (h_bands, bands),
                (h_window, window),
                (h_turn, turn),
                (h_bins, bins),
                (h_time, to_time),
                (h_bands_t, bands_t),
                (h_backward, backward),
            )
        )
    ]
    load_target = pltpu.make_async_copy(target, tbuf, target_sem)
    for copy in held[:3] + loads + held[3:] + [load_target]:
        copy.start()

    pl.semaphore_wait(barrier, DEVICES - 1)
    halo = pltpu.make_async_remote_copy(
        src_ref=wave.at[:, pl.ds(0, 16)],
        dst_ref=wbuf.at[:, pl.ds(rows, 16)],
        send_sem=halo_sem.at[0],
        recv_sem=halo_sem.at[1],
        device_id={"tm": (me + DEVICES - 1) % DEVICES},
        device_id_type=MESH,
    )
    halo.start()
    for copy in held + loads + [load_target]:
        copy.wait()
    halo.wait()
    last = me == DEVICES - 1
    wbuf[:, pl.ds(rows, 16), :] = jnp.where(last, 0.0, wbuf[:, pl.ds(rows, 16), :])

    lane = lax.broadcasted_iota(jnp.int32, (1, LOCAL), 1)

    def hops(r, later):
        start = (r % 8) + later * 16
        return jnp.concatenate(
            [wbuf[r // 8, pl.ds(start + 8 * h, LOCAL, stride=16), :] for h in range(2)], axis=1
        )

    send1, recv1 = (send1a, send1b), (recv1a, recv1b)
    send2, recv2 = (send2a, send2b), (recv2a, recv2b)

    def message1(h, r, s):
        d = 2 * r + s
        return pltpu.make_async_remote_copy(
            src_ref=send1[h].at[r, s],
            dst_ref=recv1[h].at[me],
            send_sem=s1_sem.at[h, d],
            recv_sem=r1_sem.at[h, me],
            device_id={"tm": d},
            device_id_type=MESH,
        )

    def message2(h, d):
        return pltpu.make_async_remote_copy(
            src_ref=send2[h].at[d],
            dst_ref=recv2[h].at[me],
            send_sem=s2_sem.at[h, d],
            recv_sem=r2_sem.at[h, me],
            device_id={"tm": d},
            device_id_type=MESH,
        )

    def apart(i):
        return (pair + i + RECORDS // 2) % RECORDS, (pair + RECORDS // 2 - 1 - i) % RECORDS

    def all_apart(send):
        @pl.loop(0, RECORDS // 2)
        def _(i):
            both = apart(i)
            for s in range(2):
                send(both[0], s)

            @pl.when(i < RECORDS // 2 - 1)
            def _():
                for s in range(2):
                    send(both[1], s)

        send(pair, 1 - side)

    def await_all(ref, sem):
        @pl.loop(0, DEVICES)
        def _(j):
            pltpu.make_async_copy(ref.at[j], ref.at[j], sem.at[j]).wait()

    win = window[0:1, :]

    @pl.loop(0, RECORDS // 2)
    def _(i):
        both = apart(i)
        now = jnp.concatenate([hops(r, 0) for r in both], axis=0)
        later = jnp.concatenate([hops(r, 1) for r in both], axis=0)
        added = later + win * (now - later)
        taken = win * (now + later) - later
        even = times(three(added), forward[:, 0:HALF])
        odd = times(three(taken), forward[:, HALF:FFT])
        power = [z[:, 0:LOCAL] * z[:, 0:LOCAL] + z[:, LOCAL:] * z[:, LOCAL:] for z in (even, odd)]
        power = three(jnp.concatenate(power, axis=1))
        energy = times(bands[...], power, (((1,), (1,)), ((), ())))
        for e, r in enumerate(both):
            stft[r, :, 0:HALF] = even[e * LOCAL : (e + 1) * LOCAL]
            stft[r, :, HALF:FFT] = odd[e * LOCAL : (e + 1) * LOCAL]
            lifted = energy[:, e * LOCAL : (e + 1) * LOCAL] + 0.05
            valid = (me * LOCAL + lane < lengths[r]).astype(F32)
            masked = jnp.exp(0.3 * jnp.log(lifted)) * valid
            slope[r] = 0.3 * masked / lifted
            total = jnp.sum(masked, axis=0, keepdims=True)
            for s in range(2):
                send1a[r, s, 0:PART, :] = masked[s * OWN : s * OWN + PART]
                send1a[r, s, PART:SLOT, :] = total
                send1b[r, s] = masked[s * OWN + PART : (s + 1) * OWN]

        for s in range(2):
            message1(0, both[0], s).start()

        @pl.when(i < RECORDS // 2 - 1)
        def _():
            for s in range(2):
                message1(0, both[1], s).start()

    message1(0, pair, 1 - side).start()
    for h in range(2):
        pltpu.make_async_copy(send1[h].at[pair, side], recv1[h].at[me], r1_sem.at[h, me]).start()
    all_apart(lambda r, s: message1(1, r, s).start())

    for i in range(8):
        ttall[pl.ds(i * 128, 128), 0:OWN] = tbuf[:, i * 128 : (i + 1) * 128].T

    @pl.loop(0, SIDE)
    def _(c):
        one = ttall[pl.ds(c, SIDE, stride=SIDE), :]
        wanted = jnp.concatenate([one] * 4, axis=0).T
        for h in range(2):
            tperm[h, c] = wanted[h * PART : (h + 1) * PART]

    count = lengths[pair].astype(F32) * BANDS
    chunk = 16
    wide = lax.broadcasted_iota(jnp.int32, (chunk * PART, LOCAL), 1)

    def over_devices(h):
        @pl.loop(0, PART // 8)
        def _(i):
            at = pl.ds(pl.multiple_of(i * 8, 8), 8)
            spectrum = real_forward([recv1[h][p, at, :] for p in range(DEVICES)])
            for c in range(SIDE):
                j = (c + 1) % SIDE
                re, im = spectrum[min(j, SIDE - j)]
                cos, sin = turn[c : c + 1, :], turn[SIDE + c : SIDE + c + 1, :]
                if im is None:
                    mid[h, c, at, 0:LOCAL] = re * cos
                    mid[h, c, at, LOCAL:] = -re * sin
                else:
                    if j > SIDE // 2:
                        im = -im
                    mid[h, c, at, 0:LOCAL] = re * cos + im * sin
                    mid[h, c, at, LOCAL:] = im * cos - re * sin

    def in_device(h, scale):
        loss = jnp.zeros((8, LOCAL), F32)
        inner = jnp.zeros((8, LOCAL), F32)
        for i in range(SIDE // chunk):
            part = mid[h, i * chunk : (i + 1) * chunk].reshape(chunk * PART, HALF)
            z = times(three(part), bins[...]) * scale
            here, other = z[:, 0:LOCAL], z[:, LOCAL:]
            power = here * here + other * other
            above = 1.0 + power
            wanted = tperm[h, i * chunk : (i + 1) * chunk].reshape(chunk * PART, LOCAL)
            mismatch = jnp.log(above) - wanted
            factor = 2.0 * mismatch / above
            loss += jnp.sum((mismatch * mismatch).reshape(-1, 8, LOCAL), axis=0)
            inner += jnp.sum((factor * power).reshape(-1, 8, LOCAL), axis=0)
            grad = here * (factor * scale)
            high = grad.astype(BF16)
            first = jnp.where(wide < 2 * SIDE, high.astype(F32), grad - high.astype(F32))
            back = times(jnp.concatenate([first.astype(BF16), high], axis=1), to_time[...])
            mid[h, i * chunk : (i + 1) * chunk] = back.reshape(chunk, PART, HALF)
        return loss, inner

    def to_devices(h):
        @pl.loop(0, PART // 8)
        def _(i):
            at = pl.ds(pl.multiple_of(i * 8, 8), 8)

            def bin_of(j):
                c = (j - 1) % SIDE
                re, im = mid[h, c, at, 0:LOCAL], mid[h, c, at, LOCAL:]
                cos, sin = turn[c : c + 1, :], turn[SIDE + c : SIDE + c + 1, :]
                return re * cos - im * sin, re * sin + im * cos

            paired = [(bin_of(0)[0], None)]
            for j in range(1, SIDE // 2):
                (xr, xi), (yr, yi) = bin_of(j), bin_of(SIDE - j)
                paired.append((0.5 * (xr + yr), 0.5 * (xi - yi)))
            paired.append((bin_of(SIDE // 2)[0], None))
            for p, g in enumerate(real_backward(paired, SIDE)):
                send2[h][p, at, :] = g

    def back(h):
        all_apart(lambda r, s: message2(h, 2 * r + s).start())
        pltpu.make_async_copy(send2[h].at[me], recv2[h].at[me], r2_sem.at[h, me]).start()

    await_all(recv1a, r1_sem.at[0])
    over_devices(0)
    total = jnp.sum(recv1a[:, PART:SLOT, :], axis=0)
    loud = jnp.sum(total, axis=1, keepdims=True) / count + 1e-5
    scale = 1.0 / loud
    loss, inner = in_device(0, scale)
    to_devices(0)
    back(0)
    await_all(recv1b, r1_sem.at[1])
    over_devices(1)
    more_loss, more_inner = in_device(1, scale)
    loss, inner = loss + more_loss, inner + more_inner
    loss = 0.125 * jnp.sum(jnp.sum(loss, axis=0, keepdims=True), axis=1, keepdims=True)
    inner = 0.25 * jnp.sum(jnp.sum(inner, axis=0, keepdims=True), axis=1, keepdims=True)
    inner = inner / count * scale
    extra = jnp.where(lane == 0, loss, inner)
    send2b[:, PART:SLOT, :] = jnp.broadcast_to(extra[None], (DEVICES, 1, LOCAL))
    to_devices(1)
    back(1)

    row = lax.broadcasted_iota(jnp.int32, (LOCAL, HALF), 0)
    losses[...] = jnp.zeros((1, LOCAL), F32)
    over = pltpu.make_async_remote_copy(
        src_ref=leave,
        dst_ref=edge,
        send_sem=edge_sem.at[0],
        recv_sem=edge_sem.at[1],
        device_id={"tm": (me + 1) % DEVICES},
        device_id_type=MESH,
    )

    def await_back(both):
        for r in both:
            for d in (2 * r, 2 * r + 1):
                for h in range(2):
                    pltpu.make_async_copy(recv2[h].at[d], recv2[h].at[d], r2_sem.at[h, d]).wait()

    def grad_power(both):
        powers = []
        for r in both:
            extras = recv2b[2 * r, PART:SLOT, :] + recv2b[2 * r + 1, PART:SLOT, :]
            losses[...] = jnp.where(lane == r, extras[:, 0:1], losses[...])
            mean = extras[:, 1:2]
            grad = jnp.concatenate(
                [ref[2 * r + s, 0:PART, :] for s in range(2) for ref in recv2], axis=0
            )
            powers.append(three(slope[r] * (grad - mean), axis=0))
        grad = times(jnp.concatenate(powers, axis=1), bands_t[...], (((0,), (0,)), ((), ())))
        return grad + grad

    def to_frames(both, grad, first):
        pieces = []
        for h in range(2):
            z, g = [], []
            for e, r in enumerate(both):
                z.append(stft[r, first:, h * HALF : (h + 1) * HALF])
                g.append(grad[e * LOCAL + first : (e + 1) * LOCAL, h * LOCAL : (h + 1) * LOCAL])
            z, g = jnp.concatenate(z, axis=0), jnp.concatenate(g, axis=0)
            z = z * jnp.concatenate([g, g], axis=1)
            pieces.append(times(three(z), backward[:, h * HALF : (h + 1) * HALF]))
        return pieces

    def store_edge(r, trail):
        trail = jnp.where(last, 0.0, trail)
        for h in range(2):
            leave[r // 8, pl.ds(8 * h + r % 8, 1), :] = trail[:, h * LOCAL : (h + 1) * LOCAL]

    def back_to_wave(both, grad, edges):
        plus, minus = to_frames(both, grad, 0)
        leading = win * (plus + minus)
        trailing = (1.0 - win) * (plus - minus)
        for e, r in enumerate(both):
            trail = trailing[e * LOCAL : (e + 1) * LOCAL]
            moved = jnp.where(row == 0, 0.0, pltpu.roll(trail, 1, 0))
            full = leading[e * LOCAL : (e + 1) * LOCAL] + moved
            for h in range(2):
                at = pl.ds((r % 8) + 8 * h, LOCAL, stride=16)
                out[r // 8, at, :] = full[:, h * LOCAL : (h + 1) * LOCAL]
            if edges:
                store_edge(r, trail[LOCAL - 1 :])

    def four(i):
        return [
            [(pair + RECORDS // 2 - n) % RECORDS, (pair + RECORDS // 2 + 1 + n) % RECORDS]
            for n in (2 * i, 2 * i + 1)
        ]

    @pl.loop(0, RECORDS // 4 - 1)
    def _(i):
        for both in four(i):
            await_back(both)
        for both in four(i):
            back_to_wave(both, grad_power(both), True)

    final = four(RECORDS // 4 - 1)
    for both in final:
        await_back(both)
    grads = [grad_power(both) for both in final]
    for both, grad in zip(final, grads):
        plus, minus = to_frames(both, grad, LOCAL - 8)
        trailing = (1.0 - win) * (plus - minus)
        for e, r in enumerate(both):
            store_edge(r, trailing[8 * e + 7 : 8 * e + 8])
    over.start()
    for both, grad in zip(final, grads):
        back_to_wave(both, grad, False)

    @pl.loop(1, DEVICES)
    def _(j):
        d = (me + j) % DEVICES
        for h in range(2):
            one, two = send1[h].at[d // 2, d % 2], send2[h].at[d]
            pltpu.make_async_copy(one, one, s1_sem.at[h, d]).wait()
            pltpu.make_async_copy(two, two, s2_sem.at[h, d]).wait()

    over.wait()
    out[:, 0:16, :] = out[:, 0:16, :] + edge[...]


def hand_over(grad, losses, out, loss, came, kept, sem):
    step = LOCAL * 16 // 4
    arrive = pltpu.make_async_copy(losses, came, sem.at[8])
    arrive.start()
    copies = []
    for i in range(8):
        at = (i // 4, pl.ds((i % 4) * step, step))
        copies.append(pltpu.make_async_copy(grad.at[at], out.at[at], sem.at[i]))
        copies[-1].start()
    arrive.wait()
    for r in range(RECORDS):
        kept[r] = came[0, r]
    copies.append(pltpu.make_async_copy(kept, loss, sem.at[9]))
    copies[-1].start()
    for copy in copies:
        copy.wait()


def body(wave, target_mod, lengths):
    rows = LOCAL * 16
    wave = wave.reshape(2, 8, LOCAL * 2, 128).transpose(0, 2, 1, 3).reshape(2, rows, 128)
    held = [jnp.asarray(t) for t in tables()]
    space = pl.BlockSpec(memory_space=pl.ANY)
    in_hbm = functools.partial(pltpu.with_memory_space_constraint, memory_space=pltpu.HBM)
    scratch = [pltpu.VMEM(t.shape, t.dtype) for t in held]
    scratch += [
        pltpu.VMEM((2, rows + 16, 128), F32),
        pltpu.VMEM((OWN, SIDE * SIDE), F32),
        pltpu.VMEM((SIDE * SIDE, 128), F32),
        pltpu.VMEM((2, SIDE, PART, 128), F32),
        pltpu.VMEM((RECORDS, LOCAL, FFT), F32),
        pltpu.VMEM((RECORDS, BANDS, LOCAL), F32),
        pltpu.VMEM((RECORDS, 2, SLOT, LOCAL), F32),
        pltpu.VMEM((RECORDS, 2, PART, LOCAL), F32),
        pltpu.VMEM((DEVICES, SLOT, LOCAL), F32),
        pltpu.VMEM((DEVICES, PART, LOCAL), F32),
        pltpu.VMEM((2, SIDE, PART, HALF), F32),
        pltpu.VMEM((DEVICES, PART, LOCAL), F32),
        pltpu.VMEM((DEVICES, SLOT, LOCAL), F32),
        pltpu.VMEM((DEVICES, PART, LOCAL), F32),
        pltpu.VMEM((DEVICES, SLOT, LOCAL), F32),
        pltpu.VMEM((2, 16, 128), F32),
        pltpu.VMEM((2, 16, 128), F32),
        pltpu.SemaphoreType.DMA((2,)),
        pltpu.SemaphoreType.DMA((len(held),)),
        pltpu.SemaphoreType.DMA,
        pltpu.SemaphoreType.DMA((2,)),
        pltpu.SemaphoreType.DMA((2, DEVICES)),
        pltpu.SemaphoreType.DMA((2, DEVICES)),
        pltpu.SemaphoreType.DMA((2, DEVICES)),
        pltpu.SemaphoreType.DMA((2, DEVICES)),
        pltpu.SemaphoreType.DMA((2,)),
    ]
    grad, losses = pl.pallas_call(
        kernel,
        out_shape=(
            pltpu.VMEM((2, rows, 128), F32),
            jax.ShapeDtypeStruct((1, LOCAL), F32),
        ),
        in_specs=[space, space, pl.BlockSpec(memory_space=pltpu.SMEM)] + [space] * len(held),
        out_specs=(pl.BlockSpec(memory_space=pltpu.VMEM),) * 2,
        scratch_shapes=scratch,
        compiler_params=pltpu.CompilerParams(
            collective_id=0, has_side_effects=True, vmem_limit_bytes=54000 * 1024
        ),
    )(in_hbm(wave), in_hbm(target_mod), lengths, *(in_hbm(t) for t in held))
    grad, loss = pl.pallas_call(
        hand_over,
        out_shape=(
            jax.ShapeDtypeStruct((2, rows, 128), F32),
            jax.ShapeDtypeStruct((RECORDS,), F32),
        ),
        in_specs=[pl.BlockSpec(memory_space=pltpu.VMEM), space],
        out_specs=(space, space),
        scratch_shapes=[
            pltpu.SMEM((1, LOCAL), F32),
            pltpu.SMEM((RECORDS,), F32),
            pltpu.SemaphoreType.DMA((10,)),
        ],
    )(pltpu.with_memory_space_constraint(grad, pltpu.VMEM), losses)
    grad = grad.reshape(2, LOCAL * 2, 8, 128).transpose(0, 2, 1, 3).reshape(RECORDS, LOCAL * HALF)
    return grad, loss


def solution(mesh):
    in_specs = (P("rec", "tm"), P(("rec", "tm"), None), P("rec"))
    out_specs = (P("rec", "tm"), P("rec"))
    return jax.shard_map(body, mesh=mesh, in_specs=in_specs, out_specs=out_specs, check_vma=False)
```

```python
import functools
import math

import jax
import jax.numpy as jnp
import ml_dtypes
import numpy as np
from jax import lax
from jax.experimental import pallas as pl
from jax.experimental.pallas import tpu as pltpu
from jax.sharding import PartitionSpec as P

FFT = 512
HALF = FFT // 2
BANDS = 96
OWN = BANDS // 2
RECORDS = 16
DEVICES = 32
LOCAL = 128
FRAMES = LOCAL * DEVICES
SIDE = 32
PART = OWN // 2
SLOT = PART + 1
RATE = 16000.0
F32 = jnp.float32
BF16 = jnp.bfloat16
MESH = pl.DeviceIdType.MESH


def a_weight(freq):
    square = freq * freq
    upper = 12194.0**2 * square * square
    lower = (
        (square + 20.6**2)
        * np.sqrt((square + 107.7**2) * (square + 737.9**2))
        * (square + 12194.0**2)
    )
    return upper / lower


def bark_scale(freq):
    return 13.0 * np.arctan(0.00076 * freq) + 3.5 * np.arctan((freq / 7500.0) ** 2)


def band_table():
    freq = np.arange(HALF) * (RATE / FFT)
    top = bark_scale(np.float64(RATE / 2.0))
    centres = (np.arange(BANDS) + 0.5) * (top / BANDS)
    spread = max(0.5, 2.0 * top / BANDS)
    shape = np.maximum(0.0, 1.0 - np.abs(bark_scale(freq)[:, None] - centres[None, :]) / spread)
    weight = 0.1 + a_weight(freq) / a_weight(np.float64(1000.0))
    return shape * weight[:, None] / np.maximum(shape.sum(axis=0), 1.0)[None, :]


def two(table):
    high = table.astype(np.float32).astype(ml_dtypes.bfloat16)
    low = (table - high.astype(np.float64)).astype(np.float32).astype(ml_dtypes.bfloat16)
    return high, low


def against(table, axis):
    high, low = two(table)
    return np.concatenate([high, high, low], axis=axis)


def cycle(index, length):
    angle = (index % length) * (2.0 * math.pi / length)
    return np.cos(angle), np.sin(angle)


@functools.cache
def tables():
    n, m = np.arange(HALF)[:, None], np.arange(HALF // 2)[None, :]
    halves = []
    for odd in (0, 1):
        cos, sin = cycle(n * (2 * m + odd), FFT)
        halves.append(np.concatenate([cos, -sin], axis=1) / math.sqrt(FFT))
    forward = np.concatenate([against(h, 0) for h in halves], axis=1)
    backward = np.concatenate([against(h.T, 0) for h in halves], axis=1)
    bands = band_table()
    bands = np.concatenate([bands[0::2], bands[1::2]], axis=0).T
    tau, a = np.arange(LOCAL)[:, None], np.arange(SIDE)[None, :]
    cos, sin = cycle(tau * a, LOCAL)
    cos, sin = cos / math.sqrt(FRAMES), sin / math.sqrt(FRAMES)
    re = np.concatenate([cos, sin], axis=0)
    im = np.concatenate([-sin, cos], axis=0)
    to_bins = np.concatenate([re, im, re, im, im, re, im, re], axis=1)
    high, low = two(np.concatenate([re.T, im.T], axis=0))
    to_time = np.concatenate([high, high, low, np.zeros_like(low)], axis=0)
    cos, sin = cycle((np.arange(SIDE)[:, None] + 1) * np.arange(LOCAL)[None, :], FRAMES)
    turn = np.concatenate([cos, sin], axis=0).astype(np.float32)
    window = 0.5 - 0.5 * np.cos(np.arange(HALF) * (2.0 * math.pi / FFT))
    window = np.broadcast_to(window.astype(np.float32), (8, HALF))
    return (
        forward,
        against(bands, 1),
        against(bands, 0),
        backward,
        against(to_bins, 0),
        to_time,
        turn,
        np.ascontiguousarray(window),
    )


def three(x, axis=-1):
    high = x.astype(BF16)
    low = (x - high.astype(F32)).astype(BF16)
    return jnp.concatenate([high, low, high], axis=axis)


def times(a, b, dims=(((1,), (0,)), ((), ()))):
    return lax.dot_general(a, b, dims, preferred_element_type=F32)


def turned(z, k, n):
    re, im = z
    k = k % n
    if im is None:
        im = jnp.zeros_like(re)
    if k == 0:
        return re, im
    if 4 * k == n:
        return im, -re
    if 2 * k == n:
        return -re, -im
    if 4 * k == 3 * n:
        return -im, re
    c, s = math.cos(2 * math.pi * k / n), math.sin(2 * math.pi * k / n)
    if 8 * k == n:
        return c * (re + im), c * (im - re)
    return c * re + s * im, c * im - s * re


def real_forward(x):
    n = len(x)
    if n == 1:
        return [(x[0], None)]
    if n == 2:
        return [(x[0] + x[1], None), (x[0] - x[1], None)]
    even, odd = real_forward(x[0::2]), real_forward(x[1::2])
    out = [None] * (n // 2 + 1)
    out[0] = (even[0][0] + odd[0][0], None)
    out[n // 2] = (even[0][0] - odd[0][0], None)
    quarter = n // 4
    out[quarter] = (even[quarter][0], -odd[quarter][0])
    for k in range(1, quarter):
        tr, ti = turned(odd[k], k, n)
        er, ei = even[k]
        out[k] = (er + tr, ei + ti)
        out[n // 2 - k] = (er - tr, ti - ei)
    return out


def real_backward(q, n):
    if n == 1:
        return [q[0][0]]
    if n == 2:
        return [q[0][0] + q[1][0], q[0][0] - q[1][0]]
    half, quarter = n // 2, n // 4
    a, b = [], []
    for j in range(quarter + 1):
        (xr, xi), (yr, yi) = q[j], q[half - j]
        if j == 0:
            a.append((xr + yr, None))
            b.append((xr - yr, None))
        elif j == quarter:
            a.append((xr + xr, None))
            b.append((-(xi + xi), None))
        else:
            a.append((xr + yr, xi - yi))
            dr, di = xr - yr, xi + yi
            b.append(turned((dr, di), n - j, n))
    even, odd = real_backward(a, half), real_backward(b, half)
    out = [None] * n
    out[0::2], out[1::2] = even, odd
    return out


def kernel(
    wave,
    target,
    lengths,
    h_forward,
    h_bands,
    h_bands_t,
    h_backward,
    h_bins,
    h_time,
    h_turn,
    h_window,
    out,
    losses,
    forward,
    bands,
    bands_t,
    backward,
    bins,
    to_time,
    turn,
    window,
    wbuf,
    tbuf,
    ttall,
    tperm,
    stft,
    slope,
    send1a,
    send1b,
    recv1a,
    recv1b,
    mid,
    send2a,
    send2b,
    recv2a,
    recv2b,
    leave,
    edge,
    wave_sem,
    table_sem,
    target_sem,
    halo_sem,
    s1_sem,
    r1_sem,
    s2_sem,
    r2_sem,
    edge_sem,
):
    me = lax.axis_index("tm")
    pair = me // 2
    side = me % 2

    barrier = pltpu.get_barrier_semaphore()

    for j in range(1, DEVICES):
        pl.semaphore_signal(
            barrier,
            inc=1,
            device_id={"tm": (me + j) % DEVICES},
            device_id_type=MESH,
        )

    rows = LOCAL * 16
    loads = [
        pltpu.make_async_copy(wave.at[g], wbuf.at[g, pl.ds(0, rows)], wave_sem.at[g])
        for g in range(2)
    ]
    held = [
        pltpu.make_async_copy(src, dst, table_sem.at[i])
        for i, (src, dst) in enumerate(
            (
                (h_forward, forward),
                (h_bands, bands),
                (h_window, window),
                (h_turn, turn),
                (h_bins, bins),
                (h_time, to_time),
                (h_bands_t, bands_t),
                (h_backward, backward),
            )
        )
    ]
    load_target = pltpu.make_async_copy(target, tbuf, target_sem)
    for copy in held[:3] + loads + held[3:] + [load_target]:
        copy.start()

    pl.semaphore_wait(barrier, DEVICES - 1)
    halo = pltpu.make_async_remote_copy(
        src_ref=wave.at[:, pl.ds(0, 16)],
        dst_ref=wbuf.at[:, pl.ds(rows, 16)],
        send_sem=halo_sem.at[0],
        recv_sem=halo_sem.at[1],
        device_id={"tm": (me + DEVICES - 1) % DEVICES},
        device_id_type=MESH,
    )
    halo.start()
    for copy in held + loads + [load_target]:
        copy.wait()
    halo.wait()
    last = me == DEVICES - 1
    wbuf[:, pl.ds(rows, 16), :] = jnp.where(last, 0.0, wbuf[:, pl.ds(rows, 16), :])

    lane = lax.broadcasted_iota(jnp.int32, (1, LOCAL), 1)

    def hops(r, later):
        start = (r % 8) + later * 16
        return jnp.concatenate(
            [wbuf[r // 8, pl.ds(start + 8 * h, LOCAL, stride=16), :] for h in range(2)], axis=1
        )

    send1, recv1 = (send1a, send1b), (recv1a, recv1b)
    send2, recv2 = (send2a, send2b), (recv2a, recv2b)

    def message1(h, r, s):
        d = 2 * r + s
        return pltpu.make_async_remote_copy(
            src_ref=send1[h].at[r, s],
            dst_ref=recv1[h].at[me],
            send_sem=s1_sem.at[h],
            recv_sem=r1_sem.at[h],
            device_id={"tm": d},
            device_id_type=MESH,
        )

    def message2(h, d):
        return pltpu.make_async_remote_copy(
            src_ref=send2[h].at[d],
            dst_ref=recv2[h].at[me],
            send_sem=s2_sem.at[h],
            recv_sem=r2_sem.at[h, me],
            device_id={"tm": d},
            device_id_type=MESH,
        )

    def apart(i):
        return (pair + i + RECORDS // 2) % RECORDS, (pair + RECORDS // 2 - 1 - i) % RECORDS

    def all_apart(send):
        @pl.loop(0, RECORDS // 2)
        def _(i):
            both = apart(i)
            for s in range(2):
                send(both[0], s)

            @pl.when(i < RECORDS // 2 - 1)
            def _():
                for s in range(2):
                    send(both[1], s)

        send(pair, 1 - side)

    def await_all(ref, sem):
        pltpu.make_async_copy(ref, ref, sem).wait()

    win = window[0:1, :]

    @pl.loop(0, RECORDS // 2)
    def _(i):
        both = apart(i)
        now = jnp.concatenate([hops(r, 0) for r in both], axis=0)
        later = jnp.concatenate([hops(r, 1) for r in both], axis=0)
        added = later + win * (now - later)
        taken = win * (now + later) - later
        even = times(three(added), forward[:, 0:HALF])
        odd = times(three(taken), forward[:, HALF:FFT])
        power = [z[:, 0:LOCAL] * z[:, 0:LOCAL] + z[:, LOCAL:] * z[:, LOCAL:] for z in (even, odd)]
        power = three(jnp.concatenate(power, axis=1))
        energy = times(bands[...], power, (((1,), (1,)), ((), ())))
        for e, r in enumerate(both):
            stft[r, :, 0:HALF] = even[e * LOCAL : (e + 1) * LOCAL]
            stft[r, :, HALF:FFT] = odd[e * LOCAL : (e + 1) * LOCAL]
            lifted = energy[:, e * LOCAL : (e + 1) * LOCAL] + 0.05
            valid = (me * LOCAL + lane < lengths[r]).astype(F32)
            masked = jnp.exp(0.3 * jnp.log(lifted)) * valid
            slope[r] = 0.3 * masked / lifted
            total = jnp.sum(masked, axis=0, keepdims=True)
            for s in range(2):
                send1a[r, s, 0:PART, :] = masked[s * OWN : s * OWN + PART]
                send1a[r, s, PART:SLOT, :] = total
                send1b[r, s] = masked[s * OWN + PART : (s + 1) * OWN]

        for s in range(2):
            message1(0, both[0], s).start()

        @pl.when(i < RECORDS // 2 - 1)
        def _():
            for s in range(2):
                message1(0, both[1], s).start()

    message1(0, pair, 1 - side).start()
    for h in range(2):
        pltpu.make_async_copy(send1[h].at[pair, side], recv1[h].at[me], r1_sem.at[h]).start()
    all_apart(lambda r, s: message1(1, r, s).start())

    for i in range(8):
        ttall[pl.ds(i * 128, 128), 0:OWN] = tbuf[:, i * 128 : (i + 1) * 128].T

    @pl.loop(0, SIDE)
    def _(c):
        one = ttall[pl.ds(c, SIDE, stride=SIDE), :]
        wanted = jnp.concatenate([one] * 4, axis=0).T
        for h in range(2):
            tperm[h, c] = wanted[h * PART : (h + 1) * PART]

    count = lengths[pair].astype(F32) * BANDS
    chunk = 16
    wide = lax.broadcasted_iota(jnp.int32, (chunk * PART, LOCAL), 1)

    def over_devices(h):
        @pl.loop(0, PART // 8)
        def _(i):
            at = pl.ds(pl.multiple_of(i * 8, 8), 8)
            spectrum = real_forward([recv1[h][p, at, :] for p in range(DEVICES)])
            for c in range(SIDE):
                j = (c + 1) % SIDE
                re, im = spectrum[min(j, SIDE - j)]
                cos, sin = turn[c : c + 1, :], turn[SIDE + c : SIDE + c + 1, :]
                if im is None:
                    mid[h, c, at, 0:LOCAL] = re * cos
                    mid[h, c, at, LOCAL:] = -re * sin
                else:
                    if j > SIDE // 2:
                        im = -im
                    mid[h, c, at, 0:LOCAL] = re * cos + im * sin
                    mid[h, c, at, LOCAL:] = im * cos - re * sin

    def in_device(h, scale):
        loss = jnp.zeros((8, LOCAL), F32)
        inner = jnp.zeros((8, LOCAL), F32)
        for i in range(SIDE // chunk):
            part = mid[h, i * chunk : (i + 1) * chunk].reshape(chunk * PART, HALF)
            z = times(three(part), bins[...]) * scale
            here, other = z[:, 0:LOCAL], z[:, LOCAL:]
            power = here * here + other * other
            above = 1.0 + power
            wanted = tperm[h, i * chunk : (i + 1) * chunk].reshape(chunk * PART, LOCAL)
            mismatch = jnp.log(above) - wanted
            factor = 2.0 * mismatch / above
            loss += jnp.sum((mismatch * mismatch).reshape(-1, 8, LOCAL), axis=0)
            inner += jnp.sum((factor * power).reshape(-1, 8, LOCAL), axis=0)
            grad = here * (factor * scale)
            high = grad.astype(BF16)
            first = jnp.where(wide < 2 * SIDE, high.astype(F32), grad - high.astype(F32))
            back = times(jnp.concatenate([first.astype(BF16), high], axis=1), to_time[...])
            mid[h, i * chunk : (i + 1) * chunk] = back.reshape(chunk, PART, HALF)
        return loss, inner

    def to_devices(h):
        @pl.loop(0, PART // 8)
        def _(i):
            at = pl.ds(pl.multiple_of(i * 8, 8), 8)

            def bin_of(j):
                c = (j - 1) % SIDE
                re, im = mid[h, c, at, 0:LOCAL], mid[h, c, at, LOCAL:]
                cos, sin = turn[c : c + 1, :], turn[SIDE + c : SIDE + c + 1, :]
                return re * cos - im * sin, re * sin + im * cos

            paired = [(bin_of(0)[0], None)]
            for j in range(1, SIDE // 2):
                (xr, xi), (yr, yi) = bin_of(j), bin_of(SIDE - j)
                paired.append((0.5 * (xr + yr), 0.5 * (xi - yi)))
            paired.append((bin_of(SIDE // 2)[0], None))
            for p, g in enumerate(real_backward(paired, SIDE)):
                send2[h][p, at, :] = g

    def back(h):
        all_apart(lambda r, s: message2(h, 2 * r + s).start())
        pltpu.make_async_copy(send2[h].at[me], recv2[h].at[me], r2_sem.at[h, me]).start()

    await_all(recv1a, r1_sem.at[0])
    over_devices(0)
    total = jnp.sum(recv1a[:, PART:SLOT, :], axis=0)
    loud = jnp.sum(total, axis=1, keepdims=True) / count + 1e-5
    scale = 1.0 / loud
    loss, inner = in_device(0, scale)
    to_devices(0)
    back(0)
    await_all(recv1b, r1_sem.at[1])
    over_devices(1)
    more_loss, more_inner = in_device(1, scale)
    loss, inner = loss + more_loss, inner + more_inner
    loss = 0.125 * jnp.sum(jnp.sum(loss, axis=0, keepdims=True), axis=1, keepdims=True)
    inner = 0.25 * jnp.sum(jnp.sum(inner, axis=0, keepdims=True), axis=1, keepdims=True)
    inner = inner / count * scale
    extra = jnp.where(lane == 0, loss, inner)
    send2b[:, PART:SLOT, :] = jnp.broadcast_to(extra[None], (DEVICES, 1, LOCAL))
    to_devices(1)
    back(1)

    row = lax.broadcasted_iota(jnp.int32, (LOCAL, HALF), 0)
    losses[...] = jnp.zeros((1, LOCAL), F32)
    over = pltpu.make_async_remote_copy(
        src_ref=leave,
        dst_ref=edge,
        send_sem=edge_sem.at[0],
        recv_sem=edge_sem.at[1],
        device_id={"tm": (me + 1) % DEVICES},
        device_id_type=MESH,
    )

    def await_back(both):
        for r in both:
            for d in (2 * r, 2 * r + 1):
                for h in range(2):
                    pltpu.make_async_copy(recv2[h].at[d], recv2[h].at[d], r2_sem.at[h, d]).wait()

    def grad_power(both):
        powers = []
        for r in both:
            extras = recv2b[2 * r, PART:SLOT, :] + recv2b[2 * r + 1, PART:SLOT, :]
            losses[...] = jnp.where(lane == r, extras[:, 0:1], losses[...])
            mean = extras[:, 1:2]
            grad = jnp.concatenate(
                [ref[2 * r + s, 0:PART, :] for s in range(2) for ref in recv2], axis=0
            )
            powers.append(three(slope[r] * (grad - mean), axis=0))
        grad = times(jnp.concatenate(powers, axis=1), bands_t[...], (((0,), (0,)), ((), ())))
        return grad + grad

    def to_frames(both, grad, first):
        pieces = []
        for h in range(2):
            z, g = [], []
            for e, r in enumerate(both):
                z.append(stft[r, first:, h * HALF : (h + 1) * HALF])
                g.append(grad[e * LOCAL + first : (e + 1) * LOCAL, h * LOCAL : (h + 1) * LOCAL])
            z, g = jnp.concatenate(z, axis=0), jnp.concatenate(g, axis=0)
            z = z * jnp.concatenate([g, g], axis=1)
            pieces.append(times(three(z), backward[:, h * HALF : (h + 1) * HALF]))
        return pieces

    def store_edge(r, trail):
        trail = jnp.where(last, 0.0, trail)
        for h in range(2):
            leave[r // 8, pl.ds(8 * h + r % 8, 1), :] = trail[:, h * LOCAL : (h + 1) * LOCAL]

    def back_to_wave(both, grad, edges):
        plus, minus = to_frames(both, grad, 0)
        leading = win * (plus + minus)
        trailing = (1.0 - win) * (plus - minus)
        for e, r in enumerate(both):
            trail = trailing[e * LOCAL : (e + 1) * LOCAL]
            moved = jnp.where(row == 0, 0.0, pltpu.roll(trail, 1, 0))
            full = leading[e * LOCAL : (e + 1) * LOCAL] + moved
            for h in range(2):
                at = pl.ds((r % 8) + 8 * h, LOCAL, stride=16)
                out[r // 8, at, :] = full[:, h * LOCAL : (h + 1) * LOCAL]
            if edges:
                store_edge(r, trail[LOCAL - 1 :])

    def four(i):
        return [
            [(pair + RECORDS // 2 - n) % RECORDS, (pair + RECORDS // 2 + 1 + n) % RECORDS]
            for n in (2 * i, 2 * i + 1)
        ]

    @pl.loop(0, RECORDS // 4 - 1)
    def _(i):
        for both in four(i):
            await_back(both)
        for both in four(i):
            back_to_wave(both, grad_power(both), True)

    final = four(RECORDS // 4 - 1)
    for both in final:
        await_back(both)
    grads = [grad_power(both) for both in final]
    for both, grad in zip(final, grads):
        plus, minus = to_frames(both, grad, LOCAL - 8)
        trailing = (1.0 - win) * (plus - minus)
        for e, r in enumerate(both):
            store_edge(r, trailing[8 * e + 7 : 8 * e + 8])
    over.start()
    for both, grad in zip(final, grads):
        back_to_wave(both, grad, False)

    others = pl.ds(0, DEVICES - 1)
    for h in range(2):
        await_all(recv1[h].at[others], s1_sem.at[h])
        await_all(recv2[h].at[others], s2_sem.at[h])
    over.wait()
    out[:, 0:16, :] = out[:, 0:16, :] + edge[...]


def hand_over(grad, losses, out, loss, came, kept, sem):
    step = LOCAL * 16 // 4
    arrive = pltpu.make_async_copy(losses, came, sem.at[8])
    arrive.start()
    copies = []
    for i in range(8):
        at = (i // 4, pl.ds((i % 4) * step, step))
        copies.append(pltpu.make_async_copy(grad.at[at], out.at[at], sem.at[i]))
        copies[-1].start()
    arrive.wait()
    for r in range(RECORDS):
        kept[r] = came[0, r]
    copies.append(pltpu.make_async_copy(kept, loss, sem.at[9]))
    copies[-1].start()
    for copy in copies:
        copy.wait()


def body(wave, target_mod, lengths):
    rows = LOCAL * 16
    wave = wave.reshape(2, 8, LOCAL * 2, 128).transpose(0, 2, 1, 3).reshape(2, rows, 128)
    held = [jnp.asarray(t) for t in tables()]
    space = pl.BlockSpec(memory_space=pl.ANY)
    in_hbm = functools.partial(pltpu.with_memory_space_constraint, memory_space=pltpu.HBM)
    scratch = [pltpu.VMEM(t.shape, t.dtype) for t in held]
    scratch += [
        pltpu.VMEM((2, rows + 16, 128), F32),
        pltpu.VMEM((OWN, SIDE * SIDE), F32),
        pltpu.VMEM((SIDE * SIDE, 128), F32),
        pltpu.VMEM((2, SIDE, PART, 128), F32),
        pltpu.VMEM((RECORDS, LOCAL, FFT), F32),
        pltpu.VMEM((RECORDS, BANDS, LOCAL), F32),
        pltpu.VMEM((RECORDS, 2, SLOT, LOCAL), F32),
        pltpu.VMEM((RECORDS, 2, PART, LOCAL), F32),
        pltpu.VMEM((DEVICES, SLOT, LOCAL), F32),
        pltpu.VMEM((DEVICES, PART, LOCAL), F32),
        pltpu.VMEM((2, SIDE, PART, HALF), F32),
        pltpu.VMEM((DEVICES, PART, LOCAL), F32),
        pltpu.VMEM((DEVICES, SLOT, LOCAL), F32),
        pltpu.VMEM((DEVICES, PART, LOCAL), F32),
        pltpu.VMEM((DEVICES, SLOT, LOCAL), F32),
        pltpu.VMEM((2, 16, 128), F32),
        pltpu.VMEM((2, 16, 128), F32),
        pltpu.SemaphoreType.DMA((2,)),
        pltpu.SemaphoreType.DMA((len(held),)),
        pltpu.SemaphoreType.DMA,
        pltpu.SemaphoreType.DMA((2,)),
        pltpu.SemaphoreType.DMA((2,)),
        pltpu.SemaphoreType.DMA((2,)),
        pltpu.SemaphoreType.DMA((2,)),
        pltpu.SemaphoreType.DMA((2, DEVICES)),
        pltpu.SemaphoreType.DMA((2,)),
    ]
    grad, losses = pl.pallas_call(
        kernel,
        out_shape=(
            pltpu.VMEM((2, rows, 128), F32),
            jax.ShapeDtypeStruct((1, LOCAL), F32),
        ),
        in_specs=[space, space, pl.BlockSpec(memory_space=pltpu.SMEM)] + [space] * len(held),
        out_specs=(pl.BlockSpec(memory_space=pltpu.VMEM),) * 2,
        scratch_shapes=scratch,
        compiler_params=pltpu.CompilerParams(
            collective_id=0, has_side_effects=True, vmem_limit_bytes=54000 * 1024
        ),
    )(in_hbm(wave), in_hbm(target_mod), lengths, *(in_hbm(t) for t in held))
    grad, loss = pl.pallas_call(
        hand_over,
        out_shape=(
            jax.ShapeDtypeStruct((2, rows, 128), F32),
            jax.ShapeDtypeStruct((RECORDS,), F32),
        ),
        in_specs=[pl.BlockSpec(memory_space=pltpu.VMEM), space],
        out_specs=(space, space),
        scratch_shapes=[
            pltpu.SMEM((1, LOCAL), F32),
            pltpu.SMEM((RECORDS,), F32),
            pltpu.SemaphoreType.DMA((10,)),
        ],
    )(pltpu.with_memory_space_constraint(grad, pltpu.VMEM), losses)
    grad = grad.reshape(2, LOCAL * 2, 8, 128).transpose(0, 2, 1, 3).reshape(RECORDS, LOCAL * HALF)
    return grad, loss


def solution(mesh):
    in_specs = (P("rec", "tm"), P(("rec", "tm"), None), P("rec"))
    out_specs = (P("rec", "tm"), P("rec"))
    return jax.shard_map(body, mesh=mesh, in_specs=in_specs, out_specs=out_specs, check_vma=False)
```

```python
import functools
import math

import jax
import jax.numpy as jnp
import ml_dtypes
import numpy as np
from jax import lax
from jax.experimental import pallas as pl
from jax.experimental.pallas import tpu as pltpu
from jax.sharding import PartitionSpec as P

FFT = 512
HALF = FFT // 2
BANDS = 96
OWN = BANDS // 2
RECORDS = 16
DEVICES = 32
LOCAL = 128
FRAMES = LOCAL * DEVICES
SIDE = 32
PART = OWN // 2
SLOT = PART + 1
RATE = 16000.0
F32 = jnp.float32
BF16 = jnp.bfloat16
MESH = pl.DeviceIdType.MESH


def a_weight(freq):
    square = freq * freq
    upper = 12194.0**2 * square * square
    lower = (
        (square + 20.6**2)
        * np.sqrt((square + 107.7**2) * (square + 737.9**2))
        * (square + 12194.0**2)
    )
    return upper / lower


def bark_scale(freq):
    return 13.0 * np.arctan(0.00076 * freq) + 3.5 * np.arctan((freq / 7500.0) ** 2)


def band_table():
    freq = np.arange(HALF) * (RATE / FFT)
    top = bark_scale(np.float64(RATE / 2.0))
    centres = (np.arange(BANDS) + 0.5) * (top / BANDS)
    spread = max(0.5, 2.0 * top / BANDS)
    shape = np.maximum(0.0, 1.0 - np.abs(bark_scale(freq)[:, None] - centres[None, :]) / spread)
    weight = 0.1 + a_weight(freq) / a_weight(np.float64(1000.0))
    return shape * weight[:, None] / np.maximum(shape.sum(axis=0), 1.0)[None, :]


def two(table):
    high = table.astype(np.float32).astype(ml_dtypes.bfloat16)
    low = (table - high.astype(np.float64)).astype(np.float32).astype(ml_dtypes.bfloat16)
    return high, low


def against(table, axis):
    high, low = two(table)
    return np.concatenate([high, high, low], axis=axis)


def cycle(index, length):
    angle = (index % length) * (2.0 * math.pi / length)
    return np.cos(angle), np.sin(angle)


@functools.cache
def tables():
    n, m = np.arange(HALF)[:, None], np.arange(HALF // 2)[None, :]
    halves = []
    for odd in (0, 1):
        cos, sin = cycle(n * (2 * m + odd), FFT)
        halves.append(np.concatenate([cos, -sin], axis=1) / math.sqrt(FFT))
    forward = np.concatenate([against(h, 0) for h in halves], axis=1)
    backward = np.concatenate([against(h.T, 0) for h in halves], axis=1)
    bands = band_table()
    bands = np.concatenate([bands[0::2], bands[1::2]], axis=0).T
    tau, a = np.arange(LOCAL)[:, None], np.arange(SIDE)[None, :]
    cos, sin = cycle(tau * a, LOCAL)
    cos, sin = cos / math.sqrt(FRAMES), sin / math.sqrt(FRAMES)
    re = np.concatenate([cos, sin], axis=0)
    im = np.concatenate([-sin, cos], axis=0)
    to_bins = np.concatenate([re, im, re, im, im, re, im, re], axis=1)
    high, low = two(np.concatenate([re.T, im.T], axis=0))
    to_time = np.concatenate([high, high, low, np.zeros_like(low)], axis=0)
    cos, sin = cycle((np.arange(SIDE)[:, None] + 1) * np.arange(LOCAL)[None, :], FRAMES)
    turn = np.concatenate([cos, sin], axis=0).astype(np.float32)
    window = 0.5 - 0.5 * np.cos(np.arange(HALF) * (2.0 * math.pi / FFT))
    window = np.broadcast_to(window.astype(np.float32), (8, HALF))
    return (
        forward,
        against(bands, 1),
        against(bands, 0),
        backward,
        against(to_bins, 0),
        to_time,
        turn,
        np.ascontiguousarray(window),
    )


def three(x, axis=-1):
    high = x.astype(BF16)
    low = (x - high.astype(F32)).astype(BF16)
    return jnp.concatenate([high, low, high], axis=axis)


def times(a, b, dims=(((1,), (0,)), ((), ()))):
    return lax.dot_general(a, b, dims, preferred_element_type=F32)


def turned(z, k, n):
    re, im = z
    k = k % n
    if im is None:
        im = jnp.zeros_like(re)
    if k == 0:
        return re, im
    if 4 * k == n:
        return im, -re
    if 2 * k == n:
        return -re, -im
    if 4 * k == 3 * n:
        return -im, re
    c, s = math.cos(2 * math.pi * k / n), math.sin(2 * math.pi * k / n)
    if 8 * k == n:
        return c * (re + im), c * (im - re)
    return c * re + s * im, c * im - s * re


def real_forward(x):
    n = len(x)
    if n == 1:
        return [(x[0], None)]
    if n == 2:
        return [(x[0] + x[1], None), (x[0] - x[1], None)]
    even, odd = real_forward(x[0::2]), real_forward(x[1::2])
    out = [None] * (n // 2 + 1)
    out[0] = (even[0][0] + odd[0][0], None)
    out[n // 2] = (even[0][0] - odd[0][0], None)
    quarter = n // 4
    out[quarter] = (even[quarter][0], -odd[quarter][0])
    for k in range(1, quarter):
        tr, ti = turned(odd[k], k, n)
        er, ei = even[k]
        out[k] = (er + tr, ei + ti)
        out[n // 2 - k] = (er - tr, ti - ei)
    return out


def real_backward(q, n):
    if n == 1:
        return [q[0][0]]
    if n == 2:
        return [q[0][0] + q[1][0], q[0][0] - q[1][0]]
    half, quarter = n // 2, n // 4
    a, b = [], []
    for j in range(quarter + 1):
        (xr, xi), (yr, yi) = q[j], q[half - j]
        if j == 0:
            a.append((xr + yr, None))
            b.append((xr - yr, None))
        elif j == quarter:
            a.append((xr + xr, None))
            b.append((-(xi + xi), None))
        else:
            a.append((xr + yr, xi - yi))
            dr, di = xr - yr, xi + yi
            b.append(turned((dr, di), n - j, n))
    even, odd = real_backward(a, half), real_backward(b, half)
    out = [None] * n
    out[0::2], out[1::2] = even, odd
    return out


def kernel(
    wave,
    target,
    lengths,
    h_forward,
    h_bands,
    h_bands_t,
    h_backward,
    h_bins,
    h_time,
    h_turn,
    h_window,
    out,
    losses,
    forward,
    bands,
    bands_t,
    backward,
    bins,
    to_time,
    turn,
    window,
    wbuf,
    tbuf,
    ttall,
    tperm,
    stft,
    slope,
    send1a,
    send1b,
    recv1a,
    recv1b,
    mid,
    send2a,
    send2b,
    recv2a,
    recv2b,
    leave,
    edge,
    wave_sem,
    table_sem,
    target_sem,
    halo_sem,
    s1_sem,
    r1_sem,
    s2_sem,
    r2_sem,
    edge_sem,
):
    me = lax.axis_index("tm")
    pair = me // 2
    side = me % 2

    barrier = pltpu.get_barrier_semaphore()

    for j in range(1, DEVICES):
        pl.semaphore_signal(
            barrier,
            inc=1,
            device_id={"tm": (me + j) % DEVICES},
            device_id_type=MESH,
        )

    rows = LOCAL * 16
    loads = [
        pltpu.make_async_copy(wave.at[g], wbuf.at[g, pl.ds(0, rows)], wave_sem.at[g])
        for g in range(2)
    ]
    held = [
        pltpu.make_async_copy(src, dst, table_sem.at[i])
        for i, (src, dst) in enumerate(
            (
                (h_forward, forward),
                (h_bands, bands),
                (h_window, window),
                (h_turn, turn),
                (h_bins, bins),
                (h_time, to_time),
                (h_bands_t, bands_t),
                (h_backward, backward),
            )
        )
    ]
    load_target = pltpu.make_async_copy(target, tbuf, target_sem)
    for copy in held[:3] + loads + held[3:] + [load_target]:
        copy.start()

    pl.semaphore_wait(barrier, DEVICES - 1)
    halo = pltpu.make_async_remote_copy(
        src_ref=wave.at[:, pl.ds(0, 16)],
        dst_ref=wbuf.at[:, pl.ds(rows, 16)],
        send_sem=halo_sem.at[0],
        recv_sem=halo_sem.at[1],
        device_id={"tm": (me + DEVICES - 1) % DEVICES},
        device_id_type=MESH,
    )

    @pl.when(me > 0)
    def _():
        halo.start()

    for copy in held + loads + [load_target]:
        copy.wait()

    @pl.when(me > 0)
    def _():
        halo.wait_send()

    @pl.when(me < DEVICES - 1)
    def _():
        halo.wait_recv()


    @pl.when(me == DEVICES - 1)
    def _():
        wbuf[:, pl.ds(rows, 16), :] = jnp.zeros((2, 16, 128), F32)


    lane = lax.broadcasted_iota(jnp.int32, (1, LOCAL), 1)

    def hops(r, later):
        start = (r % 8) + later * 16
        return jnp.concatenate(
            [wbuf[r // 8, pl.ds(start + 8 * h, LOCAL, stride=16), :] for h in range(2)], axis=1
        )

    send1, recv1 = (send1a, send1b), (recv1a, recv1b)
    send2, recv2 = (send2a, send2b), (recv2a, recv2b)

    def message1(h, r, s):
        d = 2 * r + s
        return pltpu.make_async_remote_copy(
            src_ref=send1[h].at[r, s],
            dst_ref=recv1[h].at[me],
            send_sem=s1_sem.at[h],
            recv_sem=r1_sem.at[h],
            device_id={"tm": d},
            device_id_type=MESH,
        )

    def message2(h, d):
        return pltpu.make_async_remote_copy(
            src_ref=send2[h].at[d],
            dst_ref=recv2[h].at[me],
            send_sem=s2_sem.at[h],
            recv_sem=r2_sem.at[h, me],
            device_id={"tm": d},
            device_id_type=MESH,
        )

    def apart(i):
        return (pair + i + RECORDS // 2) % RECORDS, (pair + RECORDS // 2 - 1 - i) % RECORDS

    def all_apart(send):
        @pl.loop(0, RECORDS // 2)
        def _(i):
            both = apart(i)
            for s in range(2):
                send(both[0], s)

            @pl.when(i < RECORDS // 2 - 1)
            def _():
                for s in range(2):
                    send(both[1], s)

        send(pair, 1 - side)

    def await_all(ref, sem):
        pltpu.make_async_copy(ref, ref, sem).wait()

    win = window[0:1, :]

    @pl.loop(0, RECORDS // 2)
    def _(i):
        both = apart(i)
        now = jnp.concatenate([hops(r, 0) for r in both], axis=0)
        later = jnp.concatenate([hops(r, 1) for r in both], axis=0)
        added = later + win * (now - later)
        taken = win * (now + later) - later
        even = times(three(added), forward[:, 0:HALF])
        odd = times(three(taken), forward[:, HALF:FFT])
        power = [z[:, 0:LOCAL] * z[:, 0:LOCAL] + z[:, LOCAL:] * z[:, LOCAL:] for z in (even, odd)]
        power = three(jnp.concatenate(power, axis=1))
        energy = times(bands[...], power, (((1,), (1,)), ((), ())))
        for e, r in enumerate(both):
            stft[r, :, 0:HALF] = even[e * LOCAL : (e + 1) * LOCAL]
            stft[r, :, HALF:FFT] = odd[e * LOCAL : (e + 1) * LOCAL]
            lifted = energy[:, e * LOCAL : (e + 1) * LOCAL] + 0.05
            valid = (me * LOCAL + lane < lengths[r]).astype(F32)
            masked = jnp.exp(0.3 * jnp.log(lifted)) * valid
            slope[r] = 0.3 * masked / lifted
            total = jnp.sum(masked, axis=0, keepdims=True)
            for s in range(2):
                send1a[r, s, 0:PART, :] = masked[s * OWN : s * OWN + PART]
                send1a[r, s, PART:SLOT, :] = total
                send1b[r, s] = masked[s * OWN + PART : (s + 1) * OWN]

        for s in range(2):
            message1(0, both[0], s).start()

        @pl.when(i < RECORDS // 2 - 1)
        def _():
            for s in range(2):
                message1(0, both[1], s).start()

    message1(0, pair, 1 - side).start()
    for h in range(2):
        pltpu.make_async_copy(send1[h].at[pair, side], recv1[h].at[me], r1_sem.at[h]).start()
    all_apart(lambda r, s: message1(1, r, s).start())

    for i in range(8):
        ttall[pl.ds(i * 128, 128), 0:OWN] = tbuf[:, i * 128 : (i + 1) * 128].T

    @pl.loop(0, SIDE)
    def _(c):
        one = ttall[pl.ds(c, SIDE, stride=SIDE), :]
        wanted = jnp.concatenate([one] * 4, axis=0).T
        for h in range(2):
            tperm[h, c] = wanted[h * PART : (h + 1) * PART]

    count = lengths[pair].astype(F32) * BANDS
    chunk = 16
    wide = lax.broadcasted_iota(jnp.int32, (chunk * PART, LOCAL), 1)

    def over_devices(h):
        @pl.loop(0, PART // 8)
        def _(i):
            at = pl.ds(pl.multiple_of(i * 8, 8), 8)
            spectrum = real_forward([recv1[h][p, at, :] for p in range(DEVICES)])
            for c in range(SIDE):
                j = (c + 1) % SIDE
                re, im = spectrum[min(j, SIDE - j)]
                cos, sin = turn[c : c + 1, :], turn[SIDE + c : SIDE + c + 1, :]
                if im is None:
                    mid[h, c, at, 0:LOCAL] = re * cos
                    mid[h, c, at, LOCAL:] = -re * sin
                else:
                    if j > SIDE // 2:
                        im = -im
                    mid[h, c, at, 0:LOCAL] = re * cos + im * sin
                    mid[h, c, at, LOCAL:] = im * cos - re * sin

    def in_device(h, scale):
        loss = jnp.zeros((8, LOCAL), F32)
        inner = jnp.zeros((8, LOCAL), F32)
        for i in range(SIDE // chunk):
            part = mid[h, i * chunk : (i + 1) * chunk].reshape(chunk * PART, HALF)
            z = times(three(part), bins[...]) * scale
            here, other = z[:, 0:LOCAL], z[:, LOCAL:]
            power = here * here + other * other
            above = 1.0 + power
            wanted = tperm[h, i * chunk : (i + 1) * chunk].reshape(chunk * PART, LOCAL)
            mismatch = jnp.log(above) - wanted
            factor = 2.0 * mismatch / above
            loss += jnp.sum((mismatch * mismatch).reshape(-1, 8, LOCAL), axis=0)
            inner += jnp.sum((factor * power).reshape(-1, 8, LOCAL), axis=0)
            grad = here * (factor * scale)
            high = grad.astype(BF16)
            first = jnp.where(wide < 2 * SIDE, high.astype(F32), grad - high.astype(F32))
            back = times(jnp.concatenate([first.astype(BF16), high], axis=1), to_time[...])
            mid[h, i * chunk : (i + 1) * chunk] = back.reshape(chunk, PART, HALF)
        return loss, inner

    def to_devices(h):
        @pl.loop(0, PART // 8)
        def _(i):
            at = pl.ds(pl.multiple_of(i * 8, 8), 8)

            def bin_of(j):
                c = (j - 1) % SIDE
                re, im = mid[h, c, at, 0:LOCAL], mid[h, c, at, LOCAL:]
                cos, sin = turn[c : c + 1, :], turn[SIDE + c : SIDE + c + 1, :]
                return re * cos - im * sin, re * sin + im * cos

            paired = [(bin_of(0)[0], None)]
            for j in range(1, SIDE // 2):
                (xr, xi), (yr, yi) = bin_of(j), bin_of(SIDE - j)
                paired.append((0.5 * (xr + yr), 0.5 * (xi - yi)))
            paired.append((bin_of(SIDE // 2)[0], None))
            for p, g in enumerate(real_backward(paired, SIDE)):
                send2[h][p, at, :] = g

    def back(h):
        all_apart(lambda r, s: message2(h, 2 * r + s).start())
        pltpu.make_async_copy(send2[h].at[me], recv2[h].at[me], r2_sem.at[h, me]).start()

    await_all(recv1a, r1_sem.at[0])
    over_devices(0)
    total = jnp.sum(recv1a[:, PART:SLOT, :], axis=0)
    loud = jnp.sum(total, axis=1, keepdims=True) / count + 1e-5
    scale = 1.0 / loud
    loss, inner = in_device(0, scale)
    to_devices(0)
    back(0)
    await_all(recv1b, r1_sem.at[1])
    over_devices(1)
    more_loss, more_inner = in_device(1, scale)
    loss, inner = loss + more_loss, inner + more_inner
    loss = 0.125 * jnp.sum(jnp.sum(loss, axis=0, keepdims=True), axis=1, keepdims=True)
    inner = 0.25 * jnp.sum(jnp.sum(inner, axis=0, keepdims=True), axis=1, keepdims=True)
    inner = inner / count * scale
    extra = jnp.where(lane == 0, loss, inner)
    send2b[:, PART:SLOT, :] = jnp.broadcast_to(extra[None], (DEVICES, 1, LOCAL))
    to_devices(1)
    back(1)

    row = lax.broadcasted_iota(jnp.int32, (LOCAL, HALF), 0)
    losses[...] = jnp.zeros((1, LOCAL), F32)
    over = pltpu.make_async_remote_copy(
        src_ref=leave,
        dst_ref=edge,
        send_sem=edge_sem.at[0],
        recv_sem=edge_sem.at[1],
        device_id={"tm": (me + 1) % DEVICES},
        device_id_type=MESH,
    )

    def await_back(both):
        for r in both:
            for d in (2 * r, 2 * r + 1):
                for h in range(2):
                    pltpu.make_async_copy(recv2[h].at[d], recv2[h].at[d], r2_sem.at[h, d]).wait()

    def grad_power(both):
        powers = []
        for r in both:
            extras = recv2b[2 * r, PART:SLOT, :] + recv2b[2 * r + 1, PART:SLOT, :]
            losses[...] = jnp.where(lane == r, extras[:, 0:1], losses[...])
            mean = extras[:, 1:2]
            grad = jnp.concatenate(
                [ref[2 * r + s, 0:PART, :] for s in range(2) for ref in recv2], axis=0
            )
            powers.append(three(slope[r] * (grad - mean), axis=0))
        grad = times(jnp.concatenate(powers, axis=1), bands_t[...], (((0,), (0,)), ((), ())))
        return grad + grad

    def to_frames(both, grad, first):
        pieces = []
        for h in range(2):
            z, g = [], []
            for e, r in enumerate(both):
                z.append(stft[r, first:, h * HALF : (h + 1) * HALF])
                g.append(grad[e * LOCAL + first : (e + 1) * LOCAL, h * LOCAL : (h + 1) * LOCAL])
            z, g = jnp.concatenate(z, axis=0), jnp.concatenate(g, axis=0)
            z = z * jnp.concatenate([g, g], axis=1)
            pieces.append(times(three(z), backward[:, h * HALF : (h + 1) * HALF]))
        return pieces

    def store_edge(r, trail):
        for h in range(2):
            leave[r // 8, pl.ds(8 * h + r % 8, 1), :] = trail[:, h * LOCAL : (h + 1) * LOCAL]

    def back_to_wave(both, grad, edges):
        plus, minus = to_frames(both, grad, 0)
        leading = win * (plus + minus)
        trailing = (1.0 - win) * (plus - minus)
        for e, r in enumerate(both):
            trail = trailing[e * LOCAL : (e + 1) * LOCAL]
            moved = jnp.where(row == 0, 0.0, pltpu.roll(trail, 1, 0))
            full = leading[e * LOCAL : (e + 1) * LOCAL] + moved
            for h in range(2):
                at = pl.ds((r % 8) + 8 * h, LOCAL, stride=16)
                out[r // 8, at, :] = full[:, h * LOCAL : (h + 1) * LOCAL]
            if edges:
                store_edge(r, trail[LOCAL - 1 :])

    def group(first, count):
        return [
            [(pair + RECORDS // 2 - n) % RECORDS, (pair + RECORDS // 2 + 1 + n) % RECORDS]
            for n in (first + m for m in range(count))
        ]

    @pl.loop(0, 2)
    def _(i):
        now = group(2 * i, 2)
        for both in now:
            await_back(both)
        for both in now:
            back_to_wave(both, grad_power(both), True)

    final = group(4, 4)
    for both in final:
        await_back(both)
    grads = [grad_power(both) for both in final]
    for both, grad in zip(final, grads):
        plus, minus = to_frames(both, grad, LOCAL - 8)
        trailing = (1.0 - win) * (plus - minus)
        for e, r in enumerate(both):
            store_edge(r, trailing[8 * e + 7 : 8 * e + 8])

    @pl.when(me < DEVICES - 1)
    def _():
        over.start()

    for both, grad in zip(final, grads):
        back_to_wave(both, grad, False)

    others = pl.ds(0, DEVICES - 1)
    for h in range(2):
        await_all(recv1[h].at[others], s1_sem.at[h])
        await_all(recv2[h].at[others], s2_sem.at[h])

    @pl.when(me < DEVICES - 1)
    def _():
        over.wait_send()

    @pl.when(me > 0)
    def _():
        over.wait_recv()
        out[:, 0:16, :] = out[:, 0:16, :] + edge[...]


def hand_over(grad, losses, out, loss, came, kept, sem):
    step = LOCAL * 16 // 4
    arrive = pltpu.make_async_copy(losses, came, sem.at[8])
    arrive.start()
    copies = []
    for i in range(8):
        at = (i // 4, pl.ds((i % 4) * step, step))
        copies.append(pltpu.make_async_copy(grad.at[at], out.at[at], sem.at[i]))
        copies[-1].start()
    arrive.wait()
    for r in range(RECORDS):
        kept[r] = came[0, r]
    copies.append(pltpu.make_async_copy(kept, loss, sem.at[9]))
    copies[-1].start()
    for copy in copies:
        copy.wait()


def body(wave, target_mod, lengths):
    rows = LOCAL * 16
    wave = wave.reshape(2, 8, LOCAL * 2, 128).transpose(0, 2, 1, 3).reshape(2, rows, 128)
    held = [jnp.asarray(t) for t in tables()]
    space = pl.BlockSpec(memory_space=pl.ANY)
    in_hbm = functools.partial(pltpu.with_memory_space_constraint, memory_space=pltpu.HBM)
    scratch = [pltpu.VMEM(t.shape, t.dtype) for t in held]
    scratch += [
        pltpu.VMEM((2, rows + 16, 128), F32),
        pltpu.VMEM((OWN, SIDE * SIDE), F32),
        pltpu.VMEM((SIDE * SIDE, 128), F32),
        pltpu.VMEM((2, SIDE, PART, 128), F32),
        pltpu.VMEM((RECORDS, LOCAL, FFT), F32),
        pltpu.VMEM((RECORDS, BANDS, LOCAL), F32),
        pltpu.VMEM((RECORDS, 2, SLOT, LOCAL), F32),
        pltpu.VMEM((RECORDS, 2, PART, LOCAL), F32),
        pltpu.VMEM((DEVICES, SLOT, LOCAL), F32),
        pltpu.VMEM((DEVICES, PART, LOCAL), F32),
        pltpu.VMEM((2, SIDE, PART, HALF), F32),
        pltpu.VMEM((DEVICES, PART, LOCAL), F32),
        pltpu.VMEM((DEVICES, SLOT, LOCAL), F32),
        pltpu.VMEM((DEVICES, PART, LOCAL), F32),
        pltpu.VMEM((DEVICES, SLOT, LOCAL), F32),
        pltpu.VMEM((2, 16, 128), F32),
        pltpu.VMEM((2, 16, 128), F32),
        pltpu.SemaphoreType.DMA((2,)),
        pltpu.SemaphoreType.DMA((len(held),)),
        pltpu.SemaphoreType.DMA,
        pltpu.SemaphoreType.DMA((2,)),
        pltpu.SemaphoreType.DMA((2,)),
        pltpu.SemaphoreType.DMA((2,)),
        pltpu.SemaphoreType.DMA((2,)),
        pltpu.SemaphoreType.DMA((2, DEVICES)),
        pltpu.SemaphoreType.DMA((2,)),
    ]
    grad, losses = pl.pallas_call(
        kernel,
        out_shape=(
            pltpu.VMEM((2, rows, 128), F32),
            jax.ShapeDtypeStruct((1, LOCAL), F32),
        ),
        in_specs=[space, space, pl.BlockSpec(memory_space=pltpu.SMEM)] + [space] * len(held),
        out_specs=(pl.BlockSpec(memory_space=pltpu.VMEM),) * 2,
        scratch_shapes=scratch,
        compiler_params=pltpu.CompilerParams(
            collective_id=0, has_side_effects=True, vmem_limit_bytes=54000 * 1024
        ),
    )(in_hbm(wave), in_hbm(target_mod), lengths, *(in_hbm(t) for t in held))
    grad, loss = pl.pallas_call(
        hand_over,
        out_shape=(
            jax.ShapeDtypeStruct((2, rows, 128), F32),
            jax.ShapeDtypeStruct((RECORDS,), F32),
        ),
        in_specs=[pl.BlockSpec(memory_space=pltpu.VMEM), space],
        out_specs=(space, space),
        scratch_shapes=[
            pltpu.SMEM((1, LOCAL), F32),
            pltpu.SMEM((RECORDS,), F32),
            pltpu.SemaphoreType.DMA((10,)),
        ],
    )(pltpu.with_memory_space_constraint(grad, pltpu.VMEM), losses)
    grad = grad.reshape(2, LOCAL * 2, 8, 128).transpose(0, 2, 1, 3).reshape(RECORDS, LOCAL * HALF)
    return grad, loss


def solution(mesh):
    in_specs = (P("rec", "tm"), P(("rec", "tm"), None), P("rec"))
    out_specs = (P("rec", "tm"), P("rec"))
    return jax.shard_map(body, mesh=mesh, in_specs=in_specs, out_specs=out_specs, check_vma=False)
```

```python
import functools
import math

import jax
import jax.numpy as jnp
import ml_dtypes
import numpy as np
from jax import lax
from jax.experimental import pallas as pl
from jax.experimental.pallas import tpu as pltpu
from jax.sharding import PartitionSpec as P

FFT = 512
HALF = FFT // 2
BANDS = 96
OWN = BANDS // 2
RECORDS = 16
DEVICES = 32
LOCAL = 128
FRAMES = LOCAL * DEVICES
SIDE = 32
PART = OWN // 2
SLOT = PART + 1
RATE = 16000.0
F32 = jnp.float32
BF16 = jnp.bfloat16
MESH = pl.DeviceIdType.MESH


def a_weight(freq):
    square = freq * freq
    upper = 12194.0**2 * square * square
    lower = (
        (square + 20.6**2)
        * np.sqrt((square + 107.7**2) * (square + 737.9**2))
        * (square + 12194.0**2)
    )
    return upper / lower


def bark_scale(freq):
    return 13.0 * np.arctan(0.00076 * freq) + 3.5 * np.arctan((freq / 7500.0) ** 2)


def band_table():
    freq = np.arange(HALF) * (RATE / FFT)
    top = bark_scale(np.float64(RATE / 2.0))
    centres = (np.arange(BANDS) + 0.5) * (top / BANDS)
    spread = max(0.5, 2.0 * top / BANDS)
    shape = np.maximum(0.0, 1.0 - np.abs(bark_scale(freq)[:, None] - centres[None, :]) / spread)
    weight = 0.1 + a_weight(freq) / a_weight(np.float64(1000.0))
    return shape * weight[:, None] / np.maximum(shape.sum(axis=0), 1.0)[None, :]


def two(table):
    high = table.astype(np.float32).astype(ml_dtypes.bfloat16)
    low = (table - high.astype(np.float64)).astype(np.float32).astype(ml_dtypes.bfloat16)
    return high, low


def against(table, axis):
    high, low = two(table)
    return np.concatenate([high, high, low], axis=axis)


def cycle(index, length):
    angle = (index % length) * (2.0 * math.pi / length)
    return np.cos(angle), np.sin(angle)


@functools.cache
def tables():
    n, m = np.arange(HALF)[:, None], np.arange(HALF // 2)[None, :]
    halves = []
    for odd in (0, 1):
        cos, sin = cycle(n * (2 * m + odd), FFT)
        halves.append(np.concatenate([cos, -sin], axis=1) / math.sqrt(FFT))
    forward = np.concatenate([against(h, 0) for h in halves], axis=1)
    backward = np.concatenate([against(h.T, 0) for h in halves], axis=1)
    bands = band_table()
    bands = np.concatenate([bands[0::2], bands[1::2]], axis=0).T
    tau, a = np.arange(LOCAL)[:, None], np.arange(SIDE)[None, :]
    cos, sin = cycle(tau * a, LOCAL)
    cos, sin = cos / math.sqrt(FRAMES), sin / math.sqrt(FRAMES)
    re = np.concatenate([cos, sin], axis=0)
    im = np.concatenate([-sin, cos], axis=0)
    to_bins = np.concatenate([re, im, re, im, im, re, im, re], axis=1)
    high, low = two(np.concatenate([re.T, im.T], axis=0))
    to_time = np.concatenate([high, high, low, np.zeros_like(low)], axis=0)
    cos, sin = cycle((np.arange(SIDE)[:, None] + 1) * np.arange(LOCAL)[None, :], FRAMES)
    turn = np.concatenate([cos, sin], axis=0).astype(np.float32)
    window = 0.5 - 0.5 * np.cos(np.arange(HALF) * (2.0 * math.pi / FFT))
    window = np.broadcast_to(window.astype(np.float32), (8, HALF))
    return (
        forward,
        against(bands, 1),
        against(bands, 0),
        backward,
        against(to_bins, 0),
        to_time,
        turn,
        np.ascontiguousarray(window),
    )


def three(x, axis=-1):
    high = x.astype(BF16)
    low = (x - high.astype(F32)).astype(BF16)
    return jnp.concatenate([high, low, high], axis=axis)


def times(a, b, dims=(((1,), (0,)), ((), ()))):
    return lax.dot_general(a, b, dims, preferred_element_type=F32)


def turned(z, k, n):
    re, im = z
    k = k % n
    if im is None:
        im = jnp.zeros_like(re)
    if k == 0:
        return re, im
    if 4 * k == n:
        return im, -re
    if 2 * k == n:
        return -re, -im
    if 4 * k == 3 * n:
        return -im, re
    c, s = math.cos(2 * math.pi * k / n), math.sin(2 * math.pi * k / n)
    if 8 * k == n:
        return c * (re + im), c * (im - re)
    return c * re + s * im, c * im - s * re


def real_forward(x):
    n = len(x)
    if n == 1:
        return [(x[0], None)]
    if n == 2:
        return [(x[0] + x[1], None), (x[0] - x[1], None)]
    even, odd = real_forward(x[0::2]), real_forward(x[1::2])
    out = [None] * (n // 2 + 1)
    out[0] = (even[0][0] + odd[0][0], None)
    out[n // 2] = (even[0][0] - odd[0][0], None)
    quarter = n // 4
    out[quarter] = (even[quarter][0], -odd[quarter][0])
    for k in range(1, quarter):
        tr, ti = turned(odd[k], k, n)
        er, ei = even[k]
        out[k] = (er + tr, ei + ti)
        out[n // 2 - k] = (er - tr, ti - ei)
    return out


def real_backward(q, n):
    if n == 1:
        return [q[0][0]]
    if n == 2:
        return [q[0][0] + q[1][0], q[0][0] - q[1][0]]
    half, quarter = n // 2, n // 4
    a, b = [], []
    for j in range(quarter + 1):
        (xr, xi), (yr, yi) = q[j], q[half - j]
        if j == 0:
            a.append((xr + yr, None))
            b.append((xr - yr, None))
        elif j == quarter:
            a.append((xr + xr, None))
            b.append((-(xi + xi), None))
        else:
            a.append((xr + yr, xi - yi))
            dr, di = xr - yr, xi + yi
            b.append(turned((dr, di), n - j, n))
    even, odd = real_backward(a, half), real_backward(b, half)
    out = [None] * n
    out[0::2], out[1::2] = even, odd
    return out


def kernel(
    wave,
    target,
    lengths,
    h_forward,
    h_bands,
    h_bands_t,
    h_backward,
    h_bins,
    h_time,
    h_turn,
    h_window,
    out,
    losses,
    forward,
    bands,
    bands_t,
    backward,
    bins,
    to_time,
    turn,
    window,
    wbuf,
    tbuf,
    ttall,
    tperm,
    stft,
    slope,
    send1a,
    send1b,
    recv1a,
    recv1b,
    mid,
    send2a,
    send2b,
    recv2a,
    recv2b,
    leave,
    edge,
    wave_sem,
    table_sem,
    target_sem,
    halo_sem,
    s1_sem,
    r1_sem,
    s2_sem,
    r2_sem,
    edge_sem,
):
    me = lax.axis_index("tm")
    pair = me // 2
    side = me % 2

    barrier = pltpu.get_barrier_semaphore()

    for j in range(1, DEVICES):
        pl.semaphore_signal(
            barrier,
            inc=1,
            device_id={"tm": (me + j) % DEVICES},
            device_id_type=MESH,
        )

    rows = LOCAL * 16
    loads = [
        pltpu.make_async_copy(wave.at[g], wbuf.at[g, pl.ds(0, rows)], wave_sem.at[g])
        for g in range(2)
    ]
    held = [
        pltpu.make_async_copy(src, dst, table_sem.at[i])
        for i, (src, dst) in enumerate(
            (
                (h_forward, forward),
                (h_bands, bands),
                (h_window, window),
                (h_turn, turn),
                (h_bins, bins),
                (h_time, to_time),
                (h_bands_t, bands_t),
                (h_backward, backward),
            )
        )
    ]
    load_target = pltpu.make_async_copy(target, tbuf, target_sem)
    for copy in held[:3] + loads:
        copy.start()

    pl.semaphore_wait(barrier, DEVICES - 1)
    halo = pltpu.make_async_remote_copy(
        src_ref=wave.at[:, pl.ds(0, 16)],
        dst_ref=wbuf.at[:, pl.ds(rows, 16)],
        send_sem=halo_sem.at[0],
        recv_sem=halo_sem.at[1],
        device_id={"tm": (me + DEVICES - 1) % DEVICES},
        device_id_type=MESH,
    )

    @pl.when(me > 0)
    def _():
        halo.start()

    for copy in held[3:] + [load_target]:
        copy.start()
    for copy in held[:3] + loads:
        copy.wait()

    @pl.when(me > 0)
    def _():
        halo.wait_send()

    @pl.when(me < DEVICES - 1)
    def _():
        halo.wait_recv()


    @pl.when(me == DEVICES - 1)
    def _():
        wbuf[:, pl.ds(rows, 16), :] = jnp.zeros((2, 16, 128), F32)


    lane = lax.broadcasted_iota(jnp.int32, (1, LOCAL), 1)

    def hops(r, later):
        start = (r % 8) + later * 16
        return jnp.concatenate(
            [wbuf[r // 8, pl.ds(start + 8 * h, LOCAL, stride=16), :] for h in range(2)], axis=1
        )

    send1, recv1 = (send1a, send1b), (recv1a, recv1b)
    send2, recv2 = (send2a, send2b), (recv2a, recv2b)

    def message1(h, r, s):
        d = 2 * r + s
        return pltpu.make_async_remote_copy(
            src_ref=send1[h].at[r, s],
            dst_ref=recv1[h].at[me],
            send_sem=s1_sem.at[h],
            recv_sem=r1_sem.at[h],
            device_id={"tm": d},
            device_id_type=MESH,
        )

    def message2(h, i, d):
        return pltpu.make_async_remote_copy(
            src_ref=send2[h].at[d],
            dst_ref=recv2[h].at[me],
            send_sem=s2_sem.at[h],
            recv_sem=r2_sem.at[h, i // 2],
            device_id={"tm": d},
            device_id_type=MESH,
        )

    def apart(i):
        return (pair + i + RECORDS // 2) % RECORDS, (pair + RECORDS // 2 - 1 - i) % RECORDS

    def all_apart(send):
        @pl.loop(0, RECORDS // 2)
        def _(i):
            both = apart(i)
            for s in range(2):
                send(i, both[0], s)

            @pl.when(i < RECORDS // 2 - 1)
            def _():
                for s in range(2):
                    send(i, both[1], s)

        send(RECORDS // 2 - 1, pair, 1 - side)

    def await_all(ref, sem):
        pltpu.make_async_copy(ref, ref, sem).wait()

    win = window[0:1, :]

    @pl.loop(0, RECORDS // 2)
    def _(i):
        both = apart(i)
        now = jnp.concatenate([hops(r, 0) for r in both], axis=0)
        later = jnp.concatenate([hops(r, 1) for r in both], axis=0)
        added = later + win * (now - later)
        taken = win * (now + later) - later
        even = times(three(added), forward[:, 0:HALF])
        odd = times(three(taken), forward[:, HALF:FFT])
        power = [z[:, 0:LOCAL] * z[:, 0:LOCAL] + z[:, LOCAL:] * z[:, LOCAL:] for z in (even, odd)]
        power = three(jnp.concatenate(power, axis=1))
        energy = times(bands[...], power, (((1,), (1,)), ((), ())))
        for e, r in enumerate(both):
            stft[r, :, 0:HALF] = even[e * LOCAL : (e + 1) * LOCAL]
            stft[r, :, HALF:FFT] = odd[e * LOCAL : (e + 1) * LOCAL]
            lifted = energy[:, e * LOCAL : (e + 1) * LOCAL] + 0.05
            valid = (me * LOCAL + lane < lengths[r]).astype(F32)
            masked = jnp.exp(0.3 * jnp.log(lifted)) * valid
            slope[r] = 0.3 * masked / lifted
            total = jnp.sum(masked, axis=0, keepdims=True)
            for s in range(2):
                send1a[r, s, 0:PART, :] = masked[s * OWN : s * OWN + PART]
                send1a[r, s, PART:SLOT, :] = total
                send1b[r, s] = masked[s * OWN + PART : (s + 1) * OWN]

        for s in range(2):
            message1(0, both[0], s).start()

        @pl.when(i < RECORDS // 2 - 1)
        def _():
            for s in range(2):
                message1(0, both[1], s).start()

    message1(0, pair, 1 - side).start()
    for h in range(2):
        pltpu.make_async_copy(send1[h].at[pair, side], recv1[h].at[me], r1_sem.at[h]).start()
    all_apart(lambda i, r, s: message1(1, r, s).start())

    for copy in held[3:] + [load_target]:
        copy.wait()

    for i in range(8):
        ttall[pl.ds(i * 128, 128), 0:OWN] = tbuf[:, i * 128 : (i + 1) * 128].T

    @pl.loop(0, SIDE)
    def _(c):
        one = ttall[pl.ds(c, SIDE, stride=SIDE), :]
        wanted = jnp.concatenate([one] * 4, axis=0).T
        for h in range(2):
            tperm[h, c] = wanted[h * PART : (h + 1) * PART]

    count = lengths[pair].astype(F32) * BANDS
    chunk = 16
    wide = lax.broadcasted_iota(jnp.int32, (chunk * PART, LOCAL), 1)

    def over_devices(h):
        @pl.loop(0, PART // 8)
        def _(i):
            at = pl.ds(pl.multiple_of(i * 8, 8), 8)
            spectrum = real_forward([recv1[h][p, at, :] for p in range(DEVICES)])
            for c in range(SIDE):
                j = (c + 1) % SIDE
                re, im = spectrum[min(j, SIDE - j)]
                cos, sin = turn[c : c + 1, :], turn[SIDE + c : SIDE + c + 1, :]
                if im is None:
                    mid[h, c, at, 0:LOCAL] = re * cos
                    mid[h, c, at, LOCAL:] = -re * sin
                else:
                    if j > SIDE // 2:
                        im = -im
                    mid[h, c, at, 0:LOCAL] = re * cos + im * sin
                    mid[h, c, at, LOCAL:] = im * cos - re * sin

    def in_device(h, scale):
        loss = jnp.zeros((8, LOCAL), F32)
        inner = jnp.zeros((8, LOCAL), F32)
        for i in range(SIDE // chunk):
            part = mid[h, i * chunk : (i + 1) * chunk].reshape(chunk * PART, HALF)
            z = times(three(part), bins[...]) * scale
            here, other = z[:, 0:LOCAL], z[:, LOCAL:]
            power = here * here + other * other
            above = 1.0 + power
            wanted = tperm[h, i * chunk : (i + 1) * chunk].reshape(chunk * PART, LOCAL)
            mismatch = jnp.log(above) - wanted
            factor = 2.0 * mismatch / above
            loss += jnp.sum((mismatch * mismatch).reshape(-1, 8, LOCAL), axis=0)
            inner += jnp.sum((factor * power).reshape(-1, 8, LOCAL), axis=0)
            grad = here * (factor * scale)
            high = grad.astype(BF16)
            first = jnp.where(wide < 2 * SIDE, high.astype(F32), grad - high.astype(F32))
            back = times(jnp.concatenate([first.astype(BF16), high], axis=1), to_time[...])
            mid[h, i * chunk : (i + 1) * chunk] = back.reshape(chunk, PART, HALF)
        return loss, inner

    def to_devices(h):
        @pl.loop(0, PART // 8)
        def _(i):
            at = pl.ds(pl.multiple_of(i * 8, 8), 8)

            def bin_of(j):
                c = (j - 1) % SIDE
                re, im = mid[h, c, at, 0:LOCAL], mid[h, c, at, LOCAL:]
                cos, sin = turn[c : c + 1, :], turn[SIDE + c : SIDE + c + 1, :]
                return re * cos - im * sin, re * sin + im * cos

            paired = [(bin_of(0)[0], None)]
            for j in range(1, SIDE // 2):
                (xr, xi), (yr, yi) = bin_of(j), bin_of(SIDE - j)
                paired.append((0.5 * (xr + yr), 0.5 * (xi - yi)))
            paired.append((bin_of(SIDE // 2)[0], None))
            for p, g in enumerate(real_backward(paired, SIDE)):
                send2[h][p, at, :] = g

    def back(h):
        all_apart(lambda i, r, s: message2(h, i, 2 * r + s).start())
        pltpu.make_async_copy(send2[h].at[me], recv2[h].at[me], r2_sem.at[h, 3]).start()

    await_all(recv1a, r1_sem.at[0])
    over_devices(0)
    total = jnp.sum(recv1a[:, PART:SLOT, :], axis=0)
    loud = jnp.sum(total, axis=1, keepdims=True) / count + 1e-5
    scale = 1.0 / loud
    loss, inner = in_device(0, scale)
    to_devices(0)
    back(0)
    await_all(recv1b, r1_sem.at[1])
    over_devices(1)
    more_loss, more_inner = in_device(1, scale)
    loss, inner = loss + more_loss, inner + more_inner
    loss = 0.125 * jnp.sum(jnp.sum(loss, axis=0, keepdims=True), axis=1, keepdims=True)
    inner = 0.25 * jnp.sum(jnp.sum(inner, axis=0, keepdims=True), axis=1, keepdims=True)
    inner = inner / count * scale
    extra = jnp.where(lane == 0, loss, inner)
    send2b[:, PART:SLOT, :] = jnp.broadcast_to(extra[None], (DEVICES, 1, LOCAL))
    to_devices(1)
    back(1)

    row = lax.broadcasted_iota(jnp.int32, (LOCAL, HALF), 0)
    losses[...] = jnp.zeros((1, LOCAL), F32)
    over = pltpu.make_async_remote_copy(
        src_ref=leave,
        dst_ref=edge,
        send_sem=edge_sem.at[0],
        recv_sem=edge_sem.at[1],
        device_id={"tm": (me + 1) % DEVICES},
        device_id_type=MESH,
    )

    def await_back(quarter):
        for h in range(2):
            await_all(recv2[h].at[pl.ds(0, DEVICES // 4)], r2_sem.at[h, quarter])

    def grad_power(both):
        powers = []
        for r in both:
            extras = recv2b[2 * r, PART:SLOT, :] + recv2b[2 * r + 1, PART:SLOT, :]
            losses[...] = jnp.where(lane == r, extras[:, 0:1], losses[...])
            mean = extras[:, 1:2]
            grad = jnp.concatenate(
                [ref[2 * r + s, 0:PART, :] for s in range(2) for ref in recv2], axis=0
            )
            powers.append(three(slope[r] * (grad - mean), axis=0))
        grad = times(jnp.concatenate(powers, axis=1), bands_t[...], (((0,), (0,)), ((), ())))
        return grad + grad

    def to_frames(both, grad, first):
        pieces = []
        for h in range(2):
            z, g = [], []
            for e, r in enumerate(both):
                z.append(stft[r, first:, h * HALF : (h + 1) * HALF])
                g.append(grad[e * LOCAL + first : (e + 1) * LOCAL, h * LOCAL : (h + 1) * LOCAL])
            z, g = jnp.concatenate(z, axis=0), jnp.concatenate(g, axis=0)
            z = z * jnp.concatenate([g, g], axis=1)
            pieces.append(times(three(z), backward[:, h * HALF : (h + 1) * HALF]))
        return pieces

    def store_edge(r, trail):
        for h in range(2):
            leave[r // 8, pl.ds(8 * h + r % 8, 1), :] = trail[:, h * LOCAL : (h + 1) * LOCAL]

    def back_to_wave(both, grad, edges):
        plus, minus = to_frames(both, grad, 0)
        leading = win * (plus + minus)
        trailing = (1.0 - win) * (plus - minus)
        for e, r in enumerate(both):
            trail = trailing[e * LOCAL : (e + 1) * LOCAL]
            moved = jnp.where(row == 0, 0.0, pltpu.roll(trail, 1, 0))
            full = leading[e * LOCAL : (e + 1) * LOCAL] + moved
            for h in range(2):
                at = pl.ds((r % 8) + 8 * h, LOCAL, stride=16)
                out[r // 8, at, :] = full[:, h * LOCAL : (h + 1) * LOCAL]
            if edges:
                store_edge(r, trail[LOCAL - 1 :])

    def group(first, count):
        return [
            [(pair + RECORDS // 2 - n) % RECORDS, (pair + RECORDS // 2 + 1 + n) % RECORDS]
            for n in (first + m for m in range(count))
        ]

    @pl.loop(0, 2)
    def _(i):
        now = group(2 * i, 2)
        await_back(i)
        for both in now:
            back_to_wave(both, grad_power(both), True)

    final = group(4, 4)
    for quarter in (2, 3):
        await_back(quarter)
    grads = [grad_power(both) for both in final]
    for both, grad in zip(final, grads):
        plus, minus = to_frames(both, grad, LOCAL - 8)
        trailing = (1.0 - win) * (plus - minus)
        for e, r in enumerate(both):
            store_edge(r, trailing[8 * e + 7 : 8 * e + 8])

    @pl.when(me < DEVICES - 1)
    def _():
        over.start()

    for both, grad in zip(final, grads):
        back_to_wave(both, grad, False)

    others = pl.ds(0, DEVICES - 1)
    for h in range(2):
        await_all(recv1[h].at[others], s1_sem.at[h])
        await_all(recv2[h].at[others], s2_sem.at[h])

    @pl.when(me < DEVICES - 1)
    def _():
        over.wait_send()

    @pl.when(me > 0)
    def _():
        over.wait_recv()
        out[:, 0:16, :] = out[:, 0:16, :] + edge[...]


def hand_over(grad, losses, out, loss, came, kept, sem):
    step = LOCAL * 16 // 4
    arrive = pltpu.make_async_copy(losses, came, sem.at[8])
    arrive.start()
    copies = []
    for i in range(8):
        at = (i // 4, pl.ds((i % 4) * step, step))
        copies.append(pltpu.make_async_copy(grad.at[at], out.at[at], sem.at[i]))
        copies[-1].start()
    arrive.wait()
    for r in range(RECORDS):
        kept[r] = came[0, r]
    copies.append(pltpu.make_async_copy(kept, loss, sem.at[9]))
    copies[-1].start()
    for copy in copies:
        copy.wait()


def body(wave, target_mod, lengths):
    rows = LOCAL * 16
    wave = wave.reshape(2, 8, LOCAL * 2, 128).transpose(0, 2, 1, 3).reshape(2, rows, 128)
    held = [jnp.asarray(t) for t in tables()]
    space = pl.BlockSpec(memory_space=pl.ANY)
    in_hbm = functools.partial(pltpu.with_memory_space_constraint, memory_space=pltpu.HBM)
    scratch = [pltpu.VMEM(t.shape, t.dtype) for t in held]
    scratch += [
        pltpu.VMEM((2, rows + 16, 128), F32),
        pltpu.VMEM((OWN, SIDE * SIDE), F32),
        pltpu.VMEM((SIDE * SIDE, 128), F32),
        pltpu.VMEM((2, SIDE, PART, 128), F32),
        pltpu.VMEM((RECORDS, LOCAL, FFT), F32),
        pltpu.VMEM((RECORDS, BANDS, LOCAL), F32),
        pltpu.VMEM((RECORDS, 2, SLOT, LOCAL), F32),
        pltpu.VMEM((RECORDS, 2, PART, LOCAL), F32),
        pltpu.VMEM((DEVICES, SLOT, LOCAL), F32),
        pltpu.VMEM((DEVICES, PART, LOCAL), F32),
        pltpu.VMEM((2, SIDE, PART, HALF), F32),
        pltpu.VMEM((DEVICES, PART, LOCAL), F32),
        pltpu.VMEM((DEVICES, SLOT, LOCAL), F32),
        pltpu.VMEM((DEVICES, PART, LOCAL), F32),
        pltpu.VMEM((DEVICES, SLOT, LOCAL), F32),
        pltpu.VMEM((2, 16, 128), F32),
        pltpu.VMEM((2, 16, 128), F32),
        pltpu.SemaphoreType.DMA((2,)),
        pltpu.SemaphoreType.DMA((len(held),)),
        pltpu.SemaphoreType.DMA,
        pltpu.SemaphoreType.DMA((2,)),
        pltpu.SemaphoreType.DMA((2,)),
        pltpu.SemaphoreType.DMA((2,)),
        pltpu.SemaphoreType.DMA((2,)),
        pltpu.SemaphoreType.DMA((2, 4)),
        pltpu.SemaphoreType.DMA((2,)),
    ]
    grad, losses = pl.pallas_call(
        kernel,
        out_shape=(
            pltpu.VMEM((2, rows, 128), F32),
            jax.ShapeDtypeStruct((1, LOCAL), F32),
        ),
        in_specs=[space, space, pl.BlockSpec(memory_space=pltpu.SMEM)] + [space] * len(held),
        out_specs=(pl.BlockSpec(memory_space=pltpu.VMEM),) * 2,
        scratch_shapes=scratch,
        compiler_params=pltpu.CompilerParams(
            collective_id=0, has_side_effects=True, vmem_limit_bytes=54000 * 1024
        ),
    )(in_hbm(wave), in_hbm(target_mod), lengths, *(in_hbm(t) for t in held))
    grad, loss = pl.pallas_call(
        hand_over,
        out_shape=(
            jax.ShapeDtypeStruct((2, rows, 128), F32),
            jax.ShapeDtypeStruct((RECORDS,), F32),
        ),
        in_specs=[pl.BlockSpec(memory_space=pltpu.VMEM), space],
        out_specs=(space, space),
        scratch_shapes=[
            pltpu.SMEM((1, LOCAL), F32),
            pltpu.SMEM((RECORDS,), F32),
            pltpu.SemaphoreType.DMA((10,)),
        ],
    )(pltpu.with_memory_space_constraint(grad, pltpu.VMEM), losses)
    grad = grad.reshape(2, LOCAL * 2, 8, 128).transpose(0, 2, 1, 3).reshape(RECORDS, LOCAL * HALF)
    return grad, loss


def solution(mesh):
    in_specs = (P("rec", "tm"), P(("rec", "tm"), None), P("rec"))
    out_specs = (P("rec", "tm"), P("rec"))
    return jax.shard_map(body, mesh=mesh, in_specs=in_specs, out_specs=out_specs, check_vma=False)
```

```python
import functools
import math

import jax
import jax.numpy as jnp
import ml_dtypes
import numpy as np
from jax import lax
from jax.experimental import pallas as pl
from jax.experimental.pallas import tpu as pltpu
from jax.sharding import PartitionSpec as P

FFT = 512
HALF = FFT // 2
BANDS = 96
OWN = BANDS // 2
RECORDS = 16
DEVICES = 32
LOCAL = 128
FRAMES = LOCAL * DEVICES
SIDE = 32
PART = OWN // 2
SLOT = PART + 1
RATE = 16000.0
F32 = jnp.float32
BF16 = jnp.bfloat16
MESH = pl.DeviceIdType.MESH


def a_weight(freq):
    square = freq * freq
    upper = 12194.0**2 * square * square
    lower = (
        (square + 20.6**2)
        * np.sqrt((square + 107.7**2) * (square + 737.9**2))
        * (square + 12194.0**2)
    )
    return upper / lower


def bark_scale(freq):
    return 13.0 * np.arctan(0.00076 * freq) + 3.5 * np.arctan((freq / 7500.0) ** 2)


def band_table():
    freq = np.arange(HALF) * (RATE / FFT)
    top = bark_scale(np.float64(RATE / 2.0))
    centres = (np.arange(BANDS) + 0.5) * (top / BANDS)
    spread = max(0.5, 2.0 * top / BANDS)
    shape = np.maximum(0.0, 1.0 - np.abs(bark_scale(freq)[:, None] - centres[None, :]) / spread)
    weight = 0.1 + a_weight(freq) / a_weight(np.float64(1000.0))
    return shape * weight[:, None] / np.maximum(shape.sum(axis=0), 1.0)[None, :]


def two(table):
    high = table.astype(np.float32).astype(ml_dtypes.bfloat16)
    low = (table - high.astype(np.float64)).astype(np.float32).astype(ml_dtypes.bfloat16)
    return high, low


def against(table, axis):
    high, low = two(table)
    return np.concatenate([high, high, low], axis=axis)


def cycle(index, length):
    angle = (index % length) * (2.0 * math.pi / length)
    return np.cos(angle), np.sin(angle)


@functools.cache
def tables():
    n, m = np.arange(HALF)[:, None], np.arange(HALF // 2)[None, :]
    halves = []
    for odd in (0, 1):
        cos, sin = cycle(n * (2 * m + odd), FFT)
        halves.append(np.concatenate([cos, -sin], axis=1) / math.sqrt(FFT))
    forward = np.concatenate([against(h, 0) for h in halves], axis=1)
    backward = np.concatenate([against(h.T, 0) for h in halves], axis=1)
    bands = band_table()
    bands = np.concatenate([bands[0::2], bands[1::2]], axis=0).T
    tau, a = np.arange(LOCAL)[:, None], np.arange(SIDE)[None, :]
    cos, sin = cycle(tau * a, LOCAL)
    cos, sin = cos / math.sqrt(FRAMES), sin / math.sqrt(FRAMES)
    re = np.concatenate([cos, sin], axis=0)
    im = np.concatenate([-sin, cos], axis=0)
    to_bins = np.concatenate([re, im, re, im, im, re, im, re], axis=1)
    high, low = two(np.concatenate([re.T, im.T], axis=0))
    to_time = np.concatenate([high, high, low, np.zeros_like(low)], axis=0)
    cos, sin = cycle((np.arange(SIDE)[:, None] + 1) * np.arange(LOCAL)[None, :], FRAMES)
    turn = np.concatenate([cos, sin], axis=0).astype(np.float32)
    window = 0.5 - 0.5 * np.cos(np.arange(HALF) * (2.0 * math.pi / FFT))
    window = np.broadcast_to(window.astype(np.float32), (8, HALF))
    return (
        forward,
        against(bands, 1),
        against(bands, 0),
        backward,
        against(to_bins, 0),
        to_time,
        turn,
        np.ascontiguousarray(window),
    )


def three(x, axis=-1):
    high = x.astype(BF16)
    low = (x - high.astype(F32)).astype(BF16)
    return jnp.concatenate([high, low, high], axis=axis)


def times(a, b, dims=(((1,), (0,)), ((), ()))):
    return lax.dot_general(a, b, dims, preferred_element_type=F32)


def turned(z, k, n):
    re, im = z
    k = k % n
    if im is None:
        im = jnp.zeros_like(re)
    if k == 0:
        return re, im
    if 4 * k == n:
        return im, -re
    if 2 * k == n:
        return -re, -im
    if 4 * k == 3 * n:
        return -im, re
    c, s = math.cos(2 * math.pi * k / n), math.sin(2 * math.pi * k / n)
    if 8 * k == n:
        return c * (re + im), c * (im - re)
    return c * re + s * im, c * im - s * re


def real_forward(x):
    n = len(x)
    if n == 1:
        return [(x[0], None)]
    if n == 2:
        return [(x[0] + x[1], None), (x[0] - x[1], None)]
    even, odd = real_forward(x[0::2]), real_forward(x[1::2])
    out = [None] * (n // 2 + 1)
    out[0] = (even[0][0] + odd[0][0], None)
    out[n // 2] = (even[0][0] - odd[0][0], None)
    quarter = n // 4
    out[quarter] = (even[quarter][0], -odd[quarter][0])
    for k in range(1, quarter):
        tr, ti = turned(odd[k], k, n)
        er, ei = even[k]
        out[k] = (er + tr, ei + ti)
        out[n // 2 - k] = (er - tr, ti - ei)
    return out


def real_backward(q, n):
    if n == 1:
        return [q[0][0]]
    if n == 2:
        return [q[0][0] + q[1][0], q[0][0] - q[1][0]]
    half, quarter = n // 2, n // 4
    a, b = [], []
    for j in range(quarter + 1):
        (xr, xi), (yr, yi) = q[j], q[half - j]
        if j == 0:
            a.append((xr + yr, None))
            b.append((xr - yr, None))
        elif j == quarter:
            a.append((xr + xr, None))
            b.append((-(xi + xi), None))
        else:
            a.append((xr + yr, xi - yi))
            dr, di = xr - yr, xi + yi
            b.append(turned((dr, di), n - j, n))
    even, odd = real_backward(a, half), real_backward(b, half)
    out = [None] * n
    out[0::2], out[1::2] = even, odd
    return out


def kernel(
    wave,
    target,
    lengths,
    h_forward,
    h_bands,
    h_bands_t,
    h_backward,
    h_bins,
    h_time,
    h_turn,
    h_window,
    out,
    losses,
    forward,
    bands,
    bands_t,
    backward,
    bins,
    to_time,
    turn,
    window,
    wbuf,
    tbuf,
    ttall,
    tperm,
    stft,
    slope,
    send1a,
    send1b,
    recv1a,
    recv1b,
    mid,
    send2a,
    send2b,
    recv2a,
    recv2b,
    leave,
    edge,
    wave_sem,
    table_sem,
    target_sem,
    halo_sem,
    s1_sem,
    r1_sem,
    s2_sem,
    r2_sem,
    edge_sem,
):
    me = lax.axis_index("tm")
    pair = me // 2
    side = me % 2

    barrier = pltpu.get_barrier_semaphore()

    for j in range(1, DEVICES):
        pl.semaphore_signal(
            barrier,
            inc=1,
            device_id={"tm": (me + j) % DEVICES},
            device_id_type=MESH,
        )

    rows = LOCAL * 16
    loads = [
        pltpu.make_async_copy(wave.at[g], wbuf.at[g, pl.ds(0, rows)], wave_sem.at[g])
        for g in range(2)
    ]
    held = [
        pltpu.make_async_copy(src, dst, table_sem.at[i])
        for i, (src, dst) in enumerate(
            (
                (h_forward, forward),
                (h_bands, bands),
                (h_window, window),
                (h_turn, turn),
                (h_bins, bins),
                (h_time, to_time),
                (h_bands_t, bands_t),
                (h_backward, backward),
            )
        )
    ]
    load_target = pltpu.make_async_copy(target, tbuf, target_sem)
    for copy in held[:3] + loads:
        copy.start()

    pl.semaphore_wait(barrier, DEVICES - 1)
    halo = pltpu.make_async_remote_copy(
        src_ref=wave.at[:, pl.ds(0, 16)],
        dst_ref=wbuf.at[:, pl.ds(rows, 16)],
        send_sem=halo_sem.at[0],
        recv_sem=halo_sem.at[1],
        device_id={"tm": (me + DEVICES - 1) % DEVICES},
        device_id_type=MESH,
    )

    @pl.when(me > 0)
    def _():
        halo.start()

    for copy in held[3:] + [load_target]:
        copy.start()
    for copy in held[:3] + loads:
        copy.wait()

    @pl.when(me > 0)
    def _():
        halo.wait_send()

    @pl.when(me < DEVICES - 1)
    def _():
        halo.wait_recv()


    @pl.when(me == DEVICES - 1)
    def _():
        wbuf[:, pl.ds(rows, 16), :] = jnp.zeros((2, 16, 128), F32)


    lane = lax.broadcasted_iota(jnp.int32, (1, LOCAL), 1)

    def hops(r, later):
        start = (r % 8) + later * 16
        return jnp.concatenate(
            [wbuf[r // 8, pl.ds(start + 8 * h, LOCAL, stride=16), :] for h in range(2)], axis=1
        )

    send1, recv1 = (send1a, send1b), (recv1a, recv1b)
    send2, recv2 = (send2a, send2b), (recv2a, recv2b)

    def message1(h, r, s):
        d = 2 * r + s
        return pltpu.make_async_remote_copy(
            src_ref=send1[h].at[r, s],
            dst_ref=recv1[h].at[me],
            send_sem=s1_sem.at[h],
            recv_sem=r1_sem.at[h],
            device_id={"tm": d},
            device_id_type=MESH,
        )

    def message2(h, i, d):
        return pltpu.make_async_remote_copy(
            src_ref=send2[h].at[d],
            dst_ref=recv2[h].at[me],
            send_sem=s2_sem.at[h],
            recv_sem=r2_sem.at[h, i // 2],
            device_id={"tm": d},
            device_id_type=MESH,
        )

    def apart(i):
        return (pair + i + RECORDS // 2) % RECORDS, (pair + RECORDS // 2 - 1 - i) % RECORDS

    def all_apart(send):
        @pl.loop(0, RECORDS // 2)
        def _(i):
            both = apart(i)
            for s in range(2):
                send(i, both[0], s)

            @pl.when(i < RECORDS // 2 - 1)
            def _():
                for s in range(2):
                    send(i, both[1], s)

        send(RECORDS // 2 - 1, pair, 1 - side)

    def await_all(ref, sem):
        pltpu.make_async_copy(ref, ref, sem).wait()

    win = window[0:1, :]

    @pl.loop(0, RECORDS // 2)
    def _(i):
        both = apart(i)
        now = jnp.concatenate([hops(r, 0) for r in both], axis=0)
        later = jnp.concatenate([hops(r, 1) for r in both], axis=0)
        added = later + win * (now - later)
        taken = win * (now + later) - later
        even = times(three(added), forward[:, 0:HALF])
        odd = times(three(taken), forward[:, HALF:FFT])
        power = [z[:, 0:LOCAL] * z[:, 0:LOCAL] + z[:, LOCAL:] * z[:, LOCAL:] for z in (even, odd)]
        power = three(jnp.concatenate(power, axis=1))
        energy = times(bands[...], power, (((1,), (1,)), ((), ())))
        for e, r in enumerate(both):
            stft[r, :, 0:HALF] = even[e * LOCAL : (e + 1) * LOCAL]
            stft[r, :, HALF:FFT] = odd[e * LOCAL : (e + 1) * LOCAL]
            lifted = energy[:, e * LOCAL : (e + 1) * LOCAL] + 0.05
            valid = (me * LOCAL + lane < lengths[r]).astype(F32)
            masked = jnp.exp(0.3 * jnp.log(lifted)) * valid
            slope[r] = 0.3 * masked / lifted
            total = jnp.sum(masked, axis=0, keepdims=True)
            for s in range(2):
                send1a[r, s, 0:PART, :] = masked[s * OWN : s * OWN + PART]
                send1a[r, s, PART:SLOT, :] = total
                send1b[r, s] = masked[s * OWN + PART : (s + 1) * OWN]

        for s in range(2):
            message1(0, both[0], s).start()

        @pl.when(i < RECORDS // 2 - 1)
        def _():
            for s in range(2):
                message1(0, both[1], s).start()

    message1(0, pair, 1 - side).start()
    for h in range(2):
        pltpu.make_async_copy(send1[h].at[pair, side], recv1[h].at[me], r1_sem.at[h]).start()
    all_apart(lambda i, r, s: message1(1, r, s).start())

    for copy in held[3:] + [load_target]:
        copy.wait()

    for i in range(8):
        ttall[pl.ds(i * 128, 128), 0:OWN] = tbuf[:, i * 128 : (i + 1) * 128].T

    @pl.loop(0, SIDE)
    def _(c):
        one = ttall[pl.ds(c, SIDE, stride=SIDE), :]
        wanted = jnp.concatenate([one] * 4, axis=0).T
        for h in range(2):
            tperm[h, c] = wanted[h * PART : (h + 1) * PART]

    count = lengths[pair].astype(F32) * BANDS
    chunk = 16
    wide = lax.broadcasted_iota(jnp.int32, (chunk * PART, LOCAL), 1)

    def over_devices(h):
        @pl.loop(0, PART // 8)
        def _(i):
            at = pl.ds(pl.multiple_of(i * 8, 8), 8)
            spectrum = real_forward([recv1[h][p, at, :] for p in range(DEVICES)])
            for c in range(SIDE):
                j = (c + 1) % SIDE
                re, im = spectrum[min(j, SIDE - j)]
                cos, sin = turn[c : c + 1, :], turn[SIDE + c : SIDE + c + 1, :]
                if im is None:
                    mid[h, c, at, 0:LOCAL] = re * cos
                    mid[h, c, at, LOCAL:] = -re * sin
                else:
                    if j > SIDE // 2:
                        im = -im
                    mid[h, c, at, 0:LOCAL] = re * cos + im * sin
                    mid[h, c, at, LOCAL:] = im * cos - re * sin

    def in_device(h, scale):
        loss = jnp.zeros((8, LOCAL), F32)
        inner = jnp.zeros((8, LOCAL), F32)
        for i in range(SIDE // chunk):
            part = mid[h, i * chunk : (i + 1) * chunk].reshape(chunk * PART, HALF)
            z = times(three(part), bins[...]) * scale
            here, other = z[:, 0:LOCAL], z[:, LOCAL:]
            power = here * here + other * other
            above = 1.0 + power
            wanted = tperm[h, i * chunk : (i + 1) * chunk].reshape(chunk * PART, LOCAL)
            mismatch = jnp.log(above) - wanted
            factor = 2.0 * mismatch / above
            loss += jnp.sum((mismatch * mismatch).reshape(-1, 8, LOCAL), axis=0)
            inner += jnp.sum((factor * power).reshape(-1, 8, LOCAL), axis=0)
            grad = here * (factor * scale)
            high = grad.astype(BF16)
            first = jnp.where(wide < 2 * SIDE, high.astype(F32), grad - high.astype(F32))
            back = times(jnp.concatenate([first.astype(BF16), high], axis=1), to_time[...])
            mid[h, i * chunk : (i + 1) * chunk] = back.reshape(chunk, PART, HALF)
        return loss, inner

    def to_devices(h):
        @pl.loop(0, PART // 8)
        def _(i):
            at = pl.ds(pl.multiple_of(i * 8, 8), 8)

            def bin_of(j):
                c = (j - 1) % SIDE
                re, im = mid[h, c, at, 0:LOCAL], mid[h, c, at, LOCAL:]
                cos, sin = turn[c : c + 1, :], turn[SIDE + c : SIDE + c + 1, :]
                return re * cos - im * sin, re * sin + im * cos

            paired = [(bin_of(0)[0], None)]
            for j in range(1, SIDE // 2):
                (xr, xi), (yr, yi) = bin_of(j), bin_of(SIDE - j)
                paired.append((0.5 * (xr + yr), 0.5 * (xi - yi)))
            paired.append((bin_of(SIDE // 2)[0], None))
            for p, g in enumerate(real_backward(paired, SIDE)):
                send2[h][p, at, :] = g

    def back(h):
        all_apart(lambda i, r, s: message2(h, i, 2 * r + s).start())
        pltpu.make_async_copy(send2[h].at[me], recv2[h].at[me], r2_sem.at[h, 3]).start()

    await_all(recv1a, r1_sem.at[0])
    over_devices(0)
    total = jnp.sum(recv1a[:, PART:SLOT, :], axis=0)
    loud = jnp.sum(total, axis=1, keepdims=True) / count + 1e-5
    scale = 1.0 / loud
    loss, inner = in_device(0, scale)
    to_devices(0)
    back(0)
    await_all(recv1b, r1_sem.at[1])
    over_devices(1)
    more_loss, more_inner = in_device(1, scale)
    loss, inner = loss + more_loss, inner + more_inner
    loss = 0.125 * jnp.sum(jnp.sum(loss, axis=0, keepdims=True), axis=1, keepdims=True)
    inner = 0.25 * jnp.sum(jnp.sum(inner, axis=0, keepdims=True), axis=1, keepdims=True)
    inner = inner / count * scale
    extra = jnp.where(lane == 0, loss, inner)
    send2b[:, PART:SLOT, :] = jnp.broadcast_to(extra[None], (DEVICES, 1, LOCAL))
    to_devices(1)
    back(1)

    row = lax.broadcasted_iota(jnp.int32, (LOCAL, HALF), 0)
    losses[...] = jnp.zeros((1, LOCAL), F32)
    over = pltpu.make_async_remote_copy(
        src_ref=leave,
        dst_ref=edge,
        send_sem=edge_sem.at[0],
        recv_sem=edge_sem.at[1],
        device_id={"tm": (me + 1) % DEVICES},
        device_id_type=MESH,
    )

    def await_back(quarter):
        for h in range(2):
            await_all(recv2[h].at[pl.ds(0, DEVICES // 4)], r2_sem.at[h, quarter])

    def grad_power(both):
        powers = []
        for r in both:
            extras = recv2b[2 * r, PART:SLOT, :] + recv2b[2 * r + 1, PART:SLOT, :]
            losses[...] = jnp.where(lane == r, extras[:, 0:1], losses[...])
            mean = extras[:, 1:2]
            grad = jnp.concatenate(
                [ref[2 * r + s, 0:PART, :] for s in range(2) for ref in recv2], axis=0
            )
            powers.append(three(slope[r] * (grad - mean), axis=0))
        grad = times(jnp.concatenate(powers, axis=1), bands_t[...], (((0,), (0,)), ((), ())))
        return grad + grad

    def to_frames(both, grad, first):
        pieces = []
        for h in range(2):
            z, g = [], []
            for e, r in enumerate(both):
                z.append(stft[r, first:, h * HALF : (h + 1) * HALF])
                g.append(grad[e * LOCAL + first : (e + 1) * LOCAL, h * LOCAL : (h + 1) * LOCAL])
            z, g = jnp.concatenate(z, axis=0), jnp.concatenate(g, axis=0)
            z = z * jnp.concatenate([g, g], axis=1)
            pieces.append(times(three(z), backward[:, h * HALF : (h + 1) * HALF]))
        return pieces

    def store_edge(r, trail):
        for h in range(2):
            leave[r // 8, pl.ds(8 * h + r % 8, 1), :] = trail[:, h * LOCAL : (h + 1) * LOCAL]

    def back_to_wave(both, grad, edges):
        plus, minus = to_frames(both, grad, 0)
        leading = win * (plus + minus)
        trailing = (1.0 - win) * (plus - minus)
        for e, r in enumerate(both):
            trail = trailing[e * LOCAL : (e + 1) * LOCAL]
            moved = jnp.where(row == 0, 0.0, pltpu.roll(trail, 1, 0))
            full = leading[e * LOCAL : (e + 1) * LOCAL] + moved
            for h in range(2):
                at = pl.ds((r % 8) + 8 * h, LOCAL, stride=16)
                out[r // 8, at, :] = full[:, h * LOCAL : (h + 1) * LOCAL]
            if edges:
                store_edge(r, trail[LOCAL - 1 :])

    def group(first, count):
        return [
            [
                r
                for n in (first + m, first + m + 1)
                for r in (
                    (pair + RECORDS // 2 - n) % RECORDS,
                    (pair + RECORDS // 2 + 1 + n) % RECORDS,
                )
            ]
            for m in range(0, count, 2)
        ]

    @pl.loop(0, 2)
    def _(i):
        now = group(2 * i, 2)
        await_back(i)
        for both in now:
            back_to_wave(both, grad_power(both), True)

    final = group(4, 4)
    for quarter in (2, 3):
        await_back(quarter)
    grads = [grad_power(both) for both in final]
    for both, grad in zip(final, grads):
        plus, minus = to_frames(both, grad, LOCAL - 8)
        trailing = (1.0 - win) * (plus - minus)
        for e, r in enumerate(both):
            store_edge(r, trailing[8 * e + 7 : 8 * e + 8])

    @pl.when(me < DEVICES - 1)
    def _():
        over.start()

    for both, grad in zip(final, grads):
        back_to_wave(both, grad, False)

    others = pl.ds(0, DEVICES - 1)
    for h in range(2):
        await_all(recv1[h].at[others], s1_sem.at[h])
        await_all(recv2[h].at[others], s2_sem.at[h])

    @pl.when(me < DEVICES - 1)
    def _():
        over.wait_send()

    @pl.when(me > 0)
    def _():
        over.wait_recv()
        out[:, 0:16, :] = out[:, 0:16, :] + edge[...]


def hand_over(grad, losses, out, loss, came, kept, sem):
    step = LOCAL * 16 // 4
    arrive = pltpu.make_async_copy(losses, came, sem.at[8])
    arrive.start()
    copies = []
    for i in range(8):
        at = (i // 4, pl.ds((i % 4) * step, step))
        copies.append(pltpu.make_async_copy(grad.at[at], out.at[at], sem.at[i]))
        copies[-1].start()
    arrive.wait()
    for r in range(RECORDS):
        kept[r] = came[0, r]
    copies.append(pltpu.make_async_copy(kept, loss, sem.at[9]))
    copies[-1].start()
    for copy in copies:
        copy.wait()


def body(wave, target_mod, lengths):
    rows = LOCAL * 16
    wave = wave.reshape(2, 8, LOCAL * 2, 128).transpose(0, 2, 1, 3).reshape(2, rows, 128)
    held = [jnp.asarray(t) for t in tables()]
    space = pl.BlockSpec(memory_space=pl.ANY)
    in_hbm = functools.partial(pltpu.with_memory_space_constraint, memory_space=pltpu.HBM)
    scratch = [pltpu.VMEM(t.shape, t.dtype) for t in held]
    scratch += [
        pltpu.VMEM((2, rows + 16, 128), F32),
        pltpu.VMEM((OWN, SIDE * SIDE), F32),
        pltpu.VMEM((SIDE * SIDE, 128), F32),
        pltpu.VMEM((2, SIDE, PART, 128), F32),
        pltpu.VMEM((RECORDS, LOCAL, FFT), F32),
        pltpu.VMEM((RECORDS, BANDS, LOCAL), F32),
        pltpu.VMEM((RECORDS, 2, SLOT, LOCAL), F32),
        pltpu.VMEM((RECORDS, 2, PART, LOCAL), F32),
        pltpu.VMEM((DEVICES, SLOT, LOCAL), F32),
        pltpu.VMEM((DEVICES, PART, LOCAL), F32),
        pltpu.VMEM((2, SIDE, PART, HALF), F32),
        pltpu.VMEM((DEVICES, PART, LOCAL), F32),
        pltpu.VMEM((DEVICES, SLOT, LOCAL), F32),
        pltpu.VMEM((DEVICES, PART, LOCAL), F32),
        pltpu.VMEM((DEVICES, SLOT, LOCAL), F32),
        pltpu.VMEM((2, 16, 128), F32),
        pltpu.VMEM((2, 16, 128), F32),
        pltpu.SemaphoreType.DMA((2,)),
        pltpu.SemaphoreType.DMA((len(held),)),
        pltpu.SemaphoreType.DMA,
        pltpu.SemaphoreType.DMA((2,)),
        pltpu.SemaphoreType.DMA((2,)),
        pltpu.SemaphoreType.DMA((2,)),
        pltpu.SemaphoreType.DMA((2,)),
        pltpu.SemaphoreType.DMA((2, 4)),
        pltpu.SemaphoreType.DMA((2,)),
    ]
    grad, losses = pl.pallas_call(
        kernel,
        out_shape=(
            pltpu.VMEM((2, rows, 128), F32),
            jax.ShapeDtypeStruct((1, LOCAL), F32),
        ),
        in_specs=[space, space, pl.BlockSpec(memory_space=pltpu.SMEM)] + [space] * len(held),
        out_specs=(pl.BlockSpec(memory_space=pltpu.VMEM),) * 2,
        scratch_shapes=scratch,
        compiler_params=pltpu.CompilerParams(
            collective_id=0, has_side_effects=True, vmem_limit_bytes=54000 * 1024
        ),
    )(in_hbm(wave), in_hbm(target_mod), lengths, *(in_hbm(t) for t in held))
    grad, loss = pl.pallas_call(
        hand_over,
        out_shape=(
            jax.ShapeDtypeStruct((2, rows, 128), F32),
            jax.ShapeDtypeStruct((RECORDS,), F32),
        ),
        in_specs=[pl.BlockSpec(memory_space=pltpu.VMEM), space],
        out_specs=(space, space),
        scratch_shapes=[
            pltpu.SMEM((1, LOCAL), F32),
            pltpu.SMEM((RECORDS,), F32),
            pltpu.SemaphoreType.DMA((10,)),
        ],
    )(pltpu.with_memory_space_constraint(grad, pltpu.VMEM), losses)
    grad = grad.reshape(2, LOCAL * 2, 8, 128).transpose(0, 2, 1, 3).reshape(RECORDS, LOCAL * HALF)
    return grad, loss


def solution(mesh):
    in_specs = (P("rec", "tm"), P(("rec", "tm"), None), P("rec"))
    out_specs = (P("rec", "tm"), P("rec"))
    return jax.shard_map(body, mesh=mesh, in_specs=in_specs, out_specs=out_specs, check_vma=False)
```

```python
import functools
import math

import jax
import jax.numpy as jnp
import ml_dtypes
import numpy as np
from jax import lax
from jax.experimental import pallas as pl
from jax.experimental.pallas import tpu as pltpu
from jax.sharding import PartitionSpec as P

FFT = 512
HALF = FFT // 2
BANDS = 96
OWN = BANDS // 2
RECORDS = 16
DEVICES = 32
LOCAL = 128
FRAMES = LOCAL * DEVICES
SIDE = 32
PART = OWN // 2
SLOT = PART + 1
RATE = 16000.0
F32 = jnp.float32
BF16 = jnp.bfloat16
MESH = pl.DeviceIdType.MESH


def a_weight(freq):
    square = freq * freq
    upper = 12194.0**2 * square * square
    lower = (
        (square + 20.6**2)
        * np.sqrt((square + 107.7**2) * (square + 737.9**2))
        * (square + 12194.0**2)
    )
    return upper / lower


def bark_scale(freq):
    return 13.0 * np.arctan(0.00076 * freq) + 3.5 * np.arctan((freq / 7500.0) ** 2)


def band_table():
    freq = np.arange(HALF) * (RATE / FFT)
    top = bark_scale(np.float64(RATE / 2.0))
    centres = (np.arange(BANDS) + 0.5) * (top / BANDS)
    spread = max(0.5, 2.0 * top / BANDS)
    shape = np.maximum(0.0, 1.0 - np.abs(bark_scale(freq)[:, None] - centres[None, :]) / spread)
    weight = 0.1 + a_weight(freq) / a_weight(np.float64(1000.0))
    return shape * weight[:, None] / np.maximum(shape.sum(axis=0), 1.0)[None, :]


def two(table):
    high = table.astype(np.float32).astype(ml_dtypes.bfloat16)
    low = (table - high.astype(np.float64)).astype(np.float32).astype(ml_dtypes.bfloat16)
    return high, low


def against(table, axis):
    high, low = two(table)
    return np.concatenate([high, high, low], axis=axis)


def cycle(index, length):
    angle = (index % length) * (2.0 * math.pi / length)
    return np.cos(angle), np.sin(angle)


@functools.cache
def tables():
    n, m = np.arange(HALF)[:, None], np.arange(HALF // 2)[None, :]
    halves = []
    for odd in (0, 1):
        cos, sin = cycle(n * (2 * m + odd), FFT)
        halves.append(np.concatenate([cos, -sin], axis=1) / math.sqrt(FFT))
    forward = np.concatenate([against(h, 0) for h in halves], axis=1)
    backward = np.concatenate([against(h.T, 0) for h in halves], axis=1)
    bands = band_table()
    bands = np.concatenate([bands[0::2], bands[1::2]], axis=0).T
    tau, a = np.arange(LOCAL)[:, None], np.arange(SIDE)[None, :]
    cos, sin = cycle(tau * a, LOCAL)
    cos, sin = cos / math.sqrt(FRAMES), sin / math.sqrt(FRAMES)
    re = np.concatenate([cos, sin], axis=0)
    im = np.concatenate([-sin, cos], axis=0)
    to_bins = np.concatenate([re, im, re, im, im, re, im, re], axis=1)
    high, low = two(np.concatenate([re.T, im.T], axis=0))
    to_time = np.concatenate([high, high, low, np.zeros_like(low)], axis=0)
    cos, sin = cycle((np.arange(SIDE)[:, None] + 1) * np.arange(LOCAL)[None, :], FRAMES)
    turn = np.concatenate([cos, sin], axis=0).astype(np.float32)
    window = 0.5 - 0.5 * np.cos(np.arange(HALF) * (2.0 * math.pi / FFT))
    window = np.broadcast_to(window.astype(np.float32), (8, HALF))
    return (
        forward,
        against(bands, 1),
        against(bands, 0),
        backward,
        against(to_bins, 0),
        to_time,
        turn,
        np.ascontiguousarray(window),
    )


def three(x, axis=-1):
    high = x.astype(BF16)
    low = (x - high.astype(F32)).astype(BF16)
    return jnp.concatenate([high, low, high], axis=axis)


def times(a, b, dims=(((1,), (0,)), ((), ()))):
    return lax.dot_general(a, b, dims, preferred_element_type=F32)


def turned(z, k, n):
    re, im = z
    k = k % n
    if im is None:
        im = jnp.zeros_like(re)
    if k == 0:
        return re, im
    if 4 * k == n:
        return im, -re
    if 2 * k == n:
        return -re, -im
    if 4 * k == 3 * n:
        return -im, re
    c, s = math.cos(2 * math.pi * k / n), math.sin(2 * math.pi * k / n)
    if 8 * k == n:
        return c * (re + im), c * (im - re)
    return c * re + s * im, c * im - s * re


def real_forward(x):
    n = len(x)
    if n == 1:
        return [(x[0], None)]
    if n == 2:
        return [(x[0] + x[1], None), (x[0] - x[1], None)]
    even, odd = real_forward(x[0::2]), real_forward(x[1::2])
    out = [None] * (n // 2 + 1)
    out[0] = (even[0][0] + odd[0][0], None)
    out[n // 2] = (even[0][0] - odd[0][0], None)
    quarter = n // 4
    out[quarter] = (even[quarter][0], -odd[quarter][0])
    for k in range(1, quarter):
        tr, ti = turned(odd[k], k, n)
        er, ei = even[k]
        out[k] = (er + tr, ei + ti)
        out[n // 2 - k] = (er - tr, ti - ei)
    return out


def real_backward(q, n):
    if n == 1:
        return [q[0][0]]
    if n == 2:
        return [q[0][0] + q[1][0], q[0][0] - q[1][0]]
    half, quarter = n // 2, n // 4
    a, b = [], []
    for j in range(quarter + 1):
        (xr, xi), (yr, yi) = q[j], q[half - j]
        if j == 0:
            a.append((xr + yr, None))
            b.append((xr - yr, None))
        elif j == quarter:
            a.append((xr + xr, None))
            b.append((-(xi + xi), None))
        else:
            a.append((xr + yr, xi - yi))
            dr, di = xr - yr, xi + yi
            b.append(turned((dr, di), n - j, n))
    even, odd = real_backward(a, half), real_backward(b, half)
    out = [None] * n
    out[0::2], out[1::2] = even, odd
    return out


def kernel(
    wave,
    target,
    lengths,
    h_forward,
    h_bands,
    h_bands_t,
    h_backward,
    h_bins,
    h_time,
    h_turn,
    h_window,
    out,
    losses,
    forward,
    bands,
    bands_t,
    backward,
    bins,
    to_time,
    turn,
    window,
    wbuf,
    tbuf,
    ttall,
    tperm,
    stft,
    slope,
    send1a,
    send1b,
    recv1a,
    recv1b,
    mid,
    send2a,
    send2b,
    recv2a,
    recv2b,
    leave,
    edge,
    wave_sem,
    table_sem,
    target_sem,
    halo_sem,
    s1_sem,
    r1_sem,
    s2_sem,
    r2_sem,
    edge_sem,
):
    me = lax.axis_index("tm")
    pair = me // 2
    side = me % 2

    barrier = pltpu.get_barrier_semaphore()

    for j in range(1, DEVICES):
        pl.semaphore_signal(
            barrier,
            inc=1,
            device_id={"tm": (me + j) % DEVICES},
            device_id_type=MESH,
        )

    rows = LOCAL * 16
    loads = [
        pltpu.make_async_copy(wave.at[g], wbuf.at[g, pl.ds(0, rows)], wave_sem.at[g])
        for g in range(2)
    ]
    held = [
        pltpu.make_async_copy(src, dst, table_sem.at[i])
        for i, (src, dst) in enumerate(
            (
                (h_forward, forward),
                (h_bands, bands),
                (h_window, window),
                (h_turn, turn),
                (h_bins, bins),
                (h_time, to_time),
                (h_bands_t, bands_t),
                (h_backward, backward),
            )
        )
    ]
    load_target = pltpu.make_async_copy(target, tbuf, target_sem)
    for copy in held[:3] + loads:
        copy.start()

    pl.semaphore_wait(barrier, DEVICES - 1)
    halo = pltpu.make_async_remote_copy(
        src_ref=wave.at[:, pl.ds(0, 16)],
        dst_ref=wbuf.at[:, pl.ds(rows, 16)],
        send_sem=halo_sem.at[0],
        recv_sem=halo_sem.at[1],
        device_id={"tm": (me + DEVICES - 1) % DEVICES},
        device_id_type=MESH,
    )

    @pl.when(me > 0)
    def _():
        halo.start()

    for copy in held[3:] + [load_target]:
        copy.start()
    for copy in held[:3] + loads:
        copy.wait()

    @pl.when(me > 0)
    def _():
        halo.wait_send()

    @pl.when(me < DEVICES - 1)
    def _():
        halo.wait_recv()


    @pl.when(me == DEVICES - 1)
    def _():
        wbuf[:, pl.ds(rows, 16), :] = jnp.zeros((2, 16, 128), F32)


    lane = lax.broadcasted_iota(jnp.int32, (1, LOCAL), 1)

    def hops(r, later):
        start = (r % 8) + later * 16
        return jnp.concatenate(
            [wbuf[r // 8, pl.ds(start + 8 * h, LOCAL, stride=16), :] for h in range(2)], axis=1
        )

    send1, recv1 = (send1a, send1b), (recv1a, recv1b)
    send2, recv2 = (send2a, send2b), (recv2a, recv2b)

    def message1(h, r, s):
        d = 2 * r + s
        return pltpu.make_async_remote_copy(
            src_ref=send1[h].at[r, s],
            dst_ref=recv1[h].at[me],
            send_sem=s1_sem.at[h],
            recv_sem=r1_sem.at[h],
            device_id={"tm": d},
            device_id_type=MESH,
        )

    def message2(h, i, d):
        return pltpu.make_async_remote_copy(
            src_ref=send2[h].at[d],
            dst_ref=recv2[h].at[me],
            send_sem=s2_sem.at[h],
            recv_sem=r2_sem.at[h, i // 2],
            device_id={"tm": d},
            device_id_type=MESH,
        )

    def apart(i):
        return (pair + i + RECORDS // 2) % RECORDS, (pair + RECORDS // 2 - 1 - i) % RECORDS

    def all_apart(send):
        @pl.loop(0, RECORDS // 2)
        def _(i):
            both = apart(i)
            for s in range(2):
                send(i, both[0], s)

            @pl.when(i < RECORDS // 2 - 1)
            def _():
                for s in range(2):
                    send(i, both[1], s)

        send(RECORDS // 2 - 1, pair, 1 - side)

    def await_all(ref, sem):
        pltpu.make_async_copy(ref, ref, sem).wait()

    win = window[0:1, :]

    @pl.loop(0, RECORDS // 2)
    def _(i):
        both = apart(i)
        now = jnp.concatenate([hops(r, 0) for r in both], axis=0)
        later = jnp.concatenate([hops(r, 1) for r in both], axis=0)
        added = later + win * (now - later)
        taken = win * (now + later) - later
        even = times(three(added), forward[:, 0:HALF])
        odd = times(three(taken), forward[:, HALF:FFT])
        power = [z[:, 0:LOCAL] * z[:, 0:LOCAL] + z[:, LOCAL:] * z[:, LOCAL:] for z in (even, odd)]
        power = three(jnp.concatenate(power, axis=1))
        energy = times(bands[...], power, (((1,), (1,)), ((), ())))
        for e, r in enumerate(both):
            stft[r, :, 0:HALF] = even[e * LOCAL : (e + 1) * LOCAL]
            stft[r, :, HALF:FFT] = odd[e * LOCAL : (e + 1) * LOCAL]
            lifted = energy[:, e * LOCAL : (e + 1) * LOCAL] + 0.05
            valid = (me * LOCAL + lane < lengths[r]).astype(F32)
            masked = jnp.exp(0.3 * jnp.log(lifted)) * valid
            slope[r] = 0.3 * masked / lifted
            total = jnp.sum(masked, axis=0, keepdims=True)
            for s in range(2):
                send1a[r, s, 0:PART, :] = masked[s * OWN : s * OWN + PART]
                send1a[r, s, PART:SLOT, :] = total
                send1b[r, s] = masked[s * OWN + PART : (s + 1) * OWN]

        for s in range(2):
            message1(0, both[0], s).start()

        @pl.when(i < RECORDS // 2 - 1)
        def _():
            for s in range(2):
                message1(0, both[1], s).start()

    message1(0, pair, 1 - side).start()
    for h in range(2):
        pltpu.make_async_copy(send1[h].at[pair, side], recv1[h].at[me], r1_sem.at[h]).start()
    all_apart(lambda i, r, s: message1(1, r, s).start())

    for copy in held[3:] + [load_target]:
        copy.wait()

    for i in range(8):
        ttall[pl.ds(i * 128, 128), 0:OWN] = tbuf[:, i * 128 : (i + 1) * 128].T

    @pl.loop(0, SIDE)
    def _(c):
        one = ttall[pl.ds(c, SIDE, stride=SIDE), :]
        wanted = jnp.concatenate([one] * 4, axis=0).T
        for h in range(2):
            tperm[h, c] = wanted[h * PART : (h + 1) * PART]

    count = lengths[pair].astype(F32) * BANDS
    chunk = 16
    wide = lax.broadcasted_iota(jnp.int32, (chunk * PART, LOCAL), 1)

    def over_devices(h):
        @pl.loop(0, PART // 8)
        def _(i):
            at = pl.ds(pl.multiple_of(i * 8, 8), 8)
            spectrum = real_forward([recv1[h][p, at, :] for p in range(DEVICES)])
            for c in range(SIDE):
                j = (c + 1) % SIDE
                re, im = spectrum[min(j, SIDE - j)]
                cos, sin = turn[c : c + 1, :], turn[SIDE + c : SIDE + c + 1, :]
                if im is None:
                    mid[h, c, at, 0:LOCAL] = re * cos
                    mid[h, c, at, LOCAL:] = -re * sin
                else:
                    if j > SIDE // 2:
                        im = -im
                    mid[h, c, at, 0:LOCAL] = re * cos + im * sin
                    mid[h, c, at, LOCAL:] = im * cos - re * sin

    def in_device(h, scale):
        loss = jnp.zeros((8, LOCAL), F32)
        inner = jnp.zeros((8, LOCAL), F32)
        for i in range(SIDE // chunk):
            part = mid[h, i * chunk : (i + 1) * chunk].reshape(chunk * PART, HALF)
            z = times(three(part), bins[...]) * scale
            here, other = z[:, 0:LOCAL], z[:, LOCAL:]
            power = here * here + other * other
            above = 1.0 + power
            wanted = tperm[h, i * chunk : (i + 1) * chunk].reshape(chunk * PART, LOCAL)
            mismatch = jnp.log(above) - wanted
            factor = 2.0 * mismatch / above
            loss += jnp.sum((mismatch * mismatch).reshape(-1, 8, LOCAL), axis=0)
            inner += jnp.sum((factor * power).reshape(-1, 8, LOCAL), axis=0)
            grad = here * (factor * scale)
            high = grad.astype(BF16)
            first = jnp.where(wide < 2 * SIDE, high.astype(F32), grad - high.astype(F32))
            back = times(jnp.concatenate([first.astype(BF16), high], axis=1), to_time[...])
            mid[h, i * chunk : (i + 1) * chunk] = back.reshape(chunk, PART, HALF)
        return loss, inner

    def to_devices(h):
        @pl.loop(0, PART // 8)
        def _(i):
            at = pl.ds(pl.multiple_of(i * 8, 8), 8)

            def bin_of(j):
                c = (j - 1) % SIDE
                re, im = mid[h, c, at, 0:LOCAL], mid[h, c, at, LOCAL:]
                cos, sin = turn[c : c + 1, :], turn[SIDE + c : SIDE + c + 1, :]
                return re * cos - im * sin, re * sin + im * cos

            paired = [(bin_of(0)[0], None)]
            for j in range(1, SIDE // 2):
                (xr, xi), (yr, yi) = bin_of(j), bin_of(SIDE - j)
                paired.append((0.5 * (xr + yr), 0.5 * (xi - yi)))
            paired.append((bin_of(SIDE // 2)[0], None))
            for p, g in enumerate(real_backward(paired, SIDE)):
                send2[h][p, at, :] = g

    def back(h):
        all_apart(lambda i, r, s: message2(h, i, 2 * r + s).start())
        pltpu.make_async_copy(send2[h].at[me], recv2[h].at[me], r2_sem.at[h, 3]).start()

    await_all(recv1a, r1_sem.at[0])
    over_devices(0)
    total = jnp.sum(recv1a[:, PART:SLOT, :], axis=0)
    loud = jnp.sum(total, axis=1, keepdims=True) / count + 1e-5
    scale = 1.0 / loud
    loss, inner = in_device(0, scale)
    to_devices(0)
    back(0)
    await_all(recv1b, r1_sem.at[1])
    over_devices(1)
    more_loss, more_inner = in_device(1, scale)
    loss, inner = loss + more_loss, inner + more_inner
    loss = 0.125 * jnp.sum(jnp.sum(loss, axis=0, keepdims=True), axis=1, keepdims=True)
    inner = 0.25 * jnp.sum(jnp.sum(inner, axis=0, keepdims=True), axis=1, keepdims=True)
    inner = inner / count * scale
    extra = jnp.where(lane == 0, loss, inner)
    send2b[:, PART:SLOT, :] = jnp.broadcast_to(extra[None], (DEVICES, 1, LOCAL))
    to_devices(1)
    back(1)

    row = lax.broadcasted_iota(jnp.int32, (LOCAL, HALF), 0)
    losses[...] = jnp.zeros((1, LOCAL), F32)
    over = pltpu.make_async_remote_copy(
        src_ref=leave,
        dst_ref=edge,
        send_sem=edge_sem.at[0],
        recv_sem=edge_sem.at[1],
        device_id={"tm": (me + 1) % DEVICES},
        device_id_type=MESH,
    )

    def await_back(quarter):
        for h in range(2):
            await_all(recv2[h].at[pl.ds(0, DEVICES // 4)], r2_sem.at[h, quarter])

    def grad_power(both):
        powers = []
        for r in both:
            extras = recv2b[2 * r, PART:SLOT, :] + recv2b[2 * r + 1, PART:SLOT, :]
            losses[...] = jnp.where(lane == r, extras[:, 0:1], losses[...])
            mean = extras[:, 1:2]
            grad = jnp.concatenate(
                [ref[2 * r + s, 0:PART, :] for s in range(2) for ref in recv2], axis=0
            )
            powers.append(three(slope[r] * (grad - mean), axis=0))
        grad = times(jnp.concatenate(powers, axis=1), bands_t[...], (((0,), (0,)), ((), ())))
        return grad + grad

    def to_frames(both, grad, first):
        pieces = []
        for h in range(2):
            z, g = [], []
            for e, r in enumerate(both):
                z.append(stft[r, first:, h * HALF : (h + 1) * HALF])
                g.append(grad[e * LOCAL + first : (e + 1) * LOCAL, h * LOCAL : (h + 1) * LOCAL])
            z, g = jnp.concatenate(z, axis=0), jnp.concatenate(g, axis=0)
            z = z * jnp.concatenate([g, g], axis=1)
            pieces.append(times(three(z), backward[:, h * HALF : (h + 1) * HALF]))
        return pieces

    def store_edge(r, trail):
        for h in range(2):
            leave[r // 8, pl.ds(8 * h + r % 8, 1), :] = trail[:, h * LOCAL : (h + 1) * LOCAL]

    def back_to_wave(both, grad, edges):
        plus, minus = to_frames(both, grad, 0)
        leading = win * (plus + minus)
        trailing = (1.0 - win) * (plus - minus)
        for e, r in enumerate(both):
            trail = trailing[e * LOCAL : (e + 1) * LOCAL]
            moved = jnp.where(row == 0, 0.0, pltpu.roll(trail, 1, 0))
            full = leading[e * LOCAL : (e + 1) * LOCAL] + moved
            for h in range(2):
                at = pl.ds((r % 8) + 8 * h, LOCAL, stride=16)
                out[r // 8, at, :] = full[:, h * LOCAL : (h + 1) * LOCAL]
            if edges:
                store_edge(r, trail[LOCAL - 1 :])

    def group(first, count):
        return [
            [
                r
                for n in (first + m, first + m + 1)
                for r in (
                    (pair + RECORDS // 2 - n) % RECORDS,
                    (pair + RECORDS // 2 + 1 + n) % RECORDS,
                )
            ]
            for m in range(0, count, 2)
        ]

    @pl.loop(0, 2)
    def _(i):
        now = group(2 * i, 2)
        await_back(i)
        for both in now:
            back_to_wave(both, grad_power(both), True)

    final = [sum(group(4, 4), [])]
    for quarter in (2, 3):
        await_back(quarter)
    grads = [grad_power(both) for both in final]
    for both, grad in zip(final, grads):
        plus, minus = to_frames(both, grad, LOCAL - 8)
        trailing = (1.0 - win) * (plus - minus)
        for e, r in enumerate(both):
            store_edge(r, trailing[8 * e + 7 : 8 * e + 8])

    @pl.when(me < DEVICES - 1)
    def _():
        over.start()

    for both, grad in zip(final, grads):
        back_to_wave(both, grad, False)

    others = pl.ds(0, DEVICES - 1)
    for h in range(2):
        await_all(recv1[h].at[others], s1_sem.at[h])
        await_all(recv2[h].at[others], s2_sem.at[h])

    @pl.when(me < DEVICES - 1)
    def _():
        over.wait_send()

    @pl.when(me > 0)
    def _():
        over.wait_recv()
        out[:, 0:16, :] = out[:, 0:16, :] + edge[...]


def hand_over(grad, losses, out, loss, came, kept, sem):
    step = LOCAL * 16 // 4
    arrive = pltpu.make_async_copy(losses, came, sem.at[8])
    arrive.start()
    copies = []
    for i in range(8):
        at = (i // 4, pl.ds((i % 4) * step, step))
        copies.append(pltpu.make_async_copy(grad.at[at], out.at[at], sem.at[i]))
        copies[-1].start()
    arrive.wait()
    for r in range(RECORDS):
        kept[r] = came[0, r]
    copies.append(pltpu.make_async_copy(kept, loss, sem.at[9]))
    copies[-1].start()
    for copy in copies:
        copy.wait()


def body(wave, target_mod, lengths):
    rows = LOCAL * 16
    wave = wave.reshape(2, 8, LOCAL * 2, 128).transpose(0, 2, 1, 3).reshape(2, rows, 128)
    held = [jnp.asarray(t) for t in tables()]
    space = pl.BlockSpec(memory_space=pl.ANY)
    in_hbm = functools.partial(pltpu.with_memory_space_constraint, memory_space=pltpu.HBM)
    scratch = [pltpu.VMEM(t.shape, t.dtype) for t in held]
    scratch += [
        pltpu.VMEM((2, rows + 16, 128), F32),
        pltpu.VMEM((OWN, SIDE * SIDE), F32),
        pltpu.VMEM((SIDE * SIDE, 128), F32),
        pltpu.VMEM((2, SIDE, PART, 128), F32),
        pltpu.VMEM((RECORDS, LOCAL, FFT), F32),
        pltpu.VMEM((RECORDS, BANDS, LOCAL), F32),
        pltpu.VMEM((RECORDS, 2, SLOT, LOCAL), F32),
        pltpu.VMEM((RECORDS, 2, PART, LOCAL), F32),
        pltpu.VMEM((DEVICES, SLOT, LOCAL), F32),
        pltpu.VMEM((DEVICES, PART, LOCAL), F32),
        pltpu.VMEM((2, SIDE, PART, HALF), F32),
        pltpu.VMEM((DEVICES, PART, LOCAL), F32),
        pltpu.VMEM((DEVICES, SLOT, LOCAL), F32),
        pltpu.VMEM((DEVICES, PART, LOCAL), F32),
        pltpu.VMEM((DEVICES, SLOT, LOCAL), F32),
        pltpu.VMEM((2, 16, 128), F32),
        pltpu.VMEM((2, 16, 128), F32),
        pltpu.SemaphoreType.DMA((2,)),
        pltpu.SemaphoreType.DMA((len(held),)),
        pltpu.SemaphoreType.DMA,
        pltpu.SemaphoreType.DMA((2,)),
        pltpu.SemaphoreType.DMA((2,)),
        pltpu.SemaphoreType.DMA((2,)),
        pltpu.SemaphoreType.DMA((2,)),
        pltpu.SemaphoreType.DMA((2, 4)),
        pltpu.SemaphoreType.DMA((2,)),
    ]
    grad, losses = pl.pallas_call(
        kernel,
        out_shape=(
            pltpu.VMEM((2, rows, 128), F32),
            jax.ShapeDtypeStruct((1, LOCAL), F32),
        ),
        in_specs=[space, space, pl.BlockSpec(memory_space=pltpu.SMEM)] + [space] * len(held),
        out_specs=(pl.BlockSpec(memory_space=pltpu.VMEM),) * 2,
        scratch_shapes=scratch,
        compiler_params=pltpu.CompilerParams(
            collective_id=0, has_side_effects=True, vmem_limit_bytes=54000 * 1024
        ),
    )(in_hbm(wave), in_hbm(target_mod), lengths, *(in_hbm(t) for t in held))
    grad, loss = pl.pallas_call(
        hand_over,
        out_shape=(
            jax.ShapeDtypeStruct((2, rows, 128), F32),
            jax.ShapeDtypeStruct((RECORDS,), F32),
        ),
        in_specs=[pl.BlockSpec(memory_space=pltpu.VMEM), space],
        out_specs=(space, space),
        scratch_shapes=[
            pltpu.SMEM((1, LOCAL), F32),
            pltpu.SMEM((RECORDS,), F32),
            pltpu.SemaphoreType.DMA((10,)),
        ],
    )(pltpu.with_memory_space_constraint(grad, pltpu.VMEM), losses)
    grad = grad.reshape(2, LOCAL * 2, 8, 128).transpose(0, 2, 1, 3).reshape(RECORDS, LOCAL * HALF)
    return grad, loss


def solution(mesh):
    in_specs = (P("rec", "tm"), P(("rec", "tm"), None), P("rec"))
    out_specs = (P("rec", "tm"), P("rec"))
    return jax.shard_map(body, mesh=mesh, in_specs=in_specs, out_specs=out_specs, check_vma=False)
```
